256 devices in a mesh: seq: 8 (over y, x_hi), dp: 32 (over z, x_lo, core).
Axes of the slice: x: 4 (x_hi: 2, x_lo: 2; x = x_hi * 2 + x_lo), y: 4, z: 8, core: 2. Of those that a mesh axis runs over, the one named last changes fastest.
Arguments:
- input_tokens: bfloat16 [32, 1024, 5120], P('dp', 'seq'), may hold values from -6 to 6
- query_unnormed: bfloat16 [32, 1024, 3072], P('dp', 'seq'), may hold values from -6 to 6
- key_unnormed: bfloat16 [32, 1024, 3072], P('dp', 'seq'), may hold values from -6 to 6
- value_projected: bfloat16 [32, 1024, 3072], P('dp', 'seq'), may hold values from -6 to 6
- cotangent: bfloat16 [32, 1024, 3072], P('dp', 'seq'), may hold values from -0.625 to 0.625
- query_norm_gain: float32 [3072], replicated, may hold values from 0.5 to 1.5
- key_norm_gain: float32 [3072], replicated, may hold values from 0.5 to 1.5
- adapter_down_maps: bfloat16 [3, 32, 5120], replicated, may hold values from -0.078125 to 0.078125
- adapter_up_maps: bfloat16 [3, 32, 3072], replicated, may hold values from -0.109375 to 0.109375
- generated_mask: int32 [32, 8, 128], P('dp', 'seq'), may hold values 0 or 1
- block_begin_flags: int32 [32, 8], P('dp'), may hold values from 0 to 1, as said below
Outputs:
- grad_down: bfloat16 [3, 32, 5120], replicated
- grad_up: bfloat16 [3, 32, 3072], replicated
The draws below stay inside these ranges and needn't reach their ends.
Inputs may be any that keep to these rules, and one draw needn't show every extreme that they name: `block_begin_flags`: the first frame of every video begins a causal block.
All inputs are finite; a program needn't handle non-finite values. No bound on the sum of `generated_mask` on one device may be relied on, other than what follows from the above.
Results may differ from the reference program's by a relative error of at most 0.01025.
The reference program's roundings to bfloat16 on the way count: a program that leaves them out, or rounds other values in their place, can miss the bound.
Values may be sent and summed in bfloat16 or wider, within the bound.
No kernel may reach another device: no remote copies, remote signals or barrier semaphores. Data moves between devices by JAX's collectives and lax.ppermute only.
A program may use at most 128 MiB of HBM per device.

```python
import math
import jax
import jax.numpy as jnp
from jax import lax

MODEL_WIDTH = 5120
HEADS = 24
HEAD_DIM = 128
ADAPTER_RANK = 32
GRID_W = 16
HEAD_CHANNELS = 3072
FRAME_TOK = 128
FRAMES = 8
TOKENS = 1024
VIDEOS = 32


def draw_query_unnormed(key, part):
    key = jax.random.fold_in(key, 11)
    own_rows = jnp.clip(jax.random.normal(key, (VIDEOS, TOKENS, HEAD_CHANNELS), jnp.float32), -6.0, 6.0)
    return own_rows.astype(jnp.bfloat16)


def draw_key_unnormed(key, part):
    key = jax.random.fold_in(key, 17)
    own_rows = jnp.clip(jax.random.normal(key, (VIDEOS, TOKENS, HEAD_CHANNELS), jnp.float32), -6.0, 6.0)
    return own_rows.astype(jnp.bfloat16)


def draw_block_begin_flags(key, part):
    key = jax.random.fold_in(key, 23)
    flags = jax.random.randint(key, (VIDEOS, FRAMES), 0, 2, dtype=jnp.int32)
    first = jnp.arange(FRAMES)[None, :] == 0
    return jnp.where(first, 1, flags).astype(jnp.int32)


def with_ends(result, rng, low, high):
    index_at = [jax.random.randint(jax.random.fold_in(rng, axis), (), 0, length) for axis, length in enumerate(result.shape)]
    widest = result.shape.index(max(result.shape))
    beside = index_at[:widest] + [(index_at[widest] + 1) % result.shape[widest]] + index_at[widest + 1:]
    return result.at[tuple(index_at)].set(low).at[tuple(beside)].set(high)


def levels(rng, shape, shards, smallest, top_value):
    level = 1.0
    for axis_at, parts in shards:
        draws = jax.random.uniform(jax.random.fold_in(jax.random.fold_in(rng, 6), axis_at), (parts,), jnp.float32, smallest / len(shards), top_value / len(shards))
        level = level * jnp.repeat(jnp.exp(draws), shape[axis_at] // parts).reshape((-1,) + (1,) * (len(shape) - 1 - axis_at))
    return level


def normal_values(own_key, shape, spread, bound, split=(), kind=jnp.bfloat16):
    values = jax.random.normal(own_key, shape, jnp.float32) * spread
    if len(split) > 0:
        values = levels(own_key, shape, split, -0.22, 0.18) * values
    return jnp.clip(values, min=-bound, max=bound).astype(kind)


def setup_inputs(seed: int = 0) -> dict:
    key_of = jax.random.split(jax.random.key(seed), 12)
    return {
        "input_tokens": normal_values(key_of[0], (VIDEOS, TOKENS, MODEL_WIDTH), 1.0, 6.0, ((0, 32), (1, 8))),
        "query_unnormed": draw_query_unnormed(jax.random.fold_in(key_of[11], 71), 0),
        "key_unnormed": draw_key_unnormed(jax.random.fold_in(key_of[11], 71), 0),
        "value_projected": normal_values(key_of[3], (VIDEOS, TOKENS, HEAD_CHANNELS), 1.0, 6.0, ((0, 32), (1, 8))),
        "cotangent": normal_values(key_of[4], (VIDEOS, TOKENS, HEAD_CHANNELS), (18 / (VIDEOS * TOKENS) ** 0.5), 0.625, ((0, 32), (1, 8))),
        "query_norm_gain": jnp.clip(1.0 + 0.1 * jax.random.normal(key_of[5], (HEAD_CHANNELS,), jnp.float32), 0.5, 1.5),
        "key_norm_gain": jnp.clip(1.0 + 0.1 * jax.random.normal(key_of[6], (HEAD_CHANNELS,), jnp.float32), 0.5, 1.5),
        "adapter_down_maps": normal_values(key_of[7], (3, ADAPTER_RANK, MODEL_WIDTH), MODEL_WIDTH ** -0.5, 0.078125),
        "adapter_up_maps": normal_values(key_of[8], (3, ADAPTER_RANK, HEAD_CHANNELS), HEAD_CHANNELS ** -0.5, 0.109375),
        "generated_mask": with_ends((jax.random.randint(key_of[9], (VIDEOS, FRAMES, FRAME_TOK), 0, 4) < 3).astype(jnp.int32), jax.random.fold_in(key_of[9], 1), 0, 1),
        "block_begin_flags": draw_block_begin_flags(jax.random.fold_in(key_of[11], 71), 0),
    }


NORM_EPS = 1e-06

def rope_angles(token_ids):
    time_dims = HEAD_DIM - 4 * (HEAD_DIM // 6)
    space_dims = 2 * (HEAD_DIM // 6)
    time_pairs = time_dims // 2
    space_pairs = space_dims // 2
    frame_pos = (token_ids // FRAME_TOK).astype(jnp.float32)
    within = token_ids % FRAME_TOK
    row_pos = (within // GRID_W).astype(jnp.float32)
    column_pos = (within % GRID_W).astype(jnp.float32)
    pairs = jnp.arange(HEAD_DIM, dtype=jnp.int32) // 2
    in_time = pairs < time_pairs
    in_rows = jnp.logical_and(pairs >= time_pairs, pairs < time_pairs + space_pairs)
    offset = jnp.where(in_time, pairs, jnp.where(in_rows, pairs - time_pairs, pairs - time_pairs - space_pairs))
    extent = jnp.where(in_time, time_dims, space_dims)
    rates = jnp.exp(-math.log(10000.0) * (2 * offset).astype(jnp.float32) / extent.astype(jnp.float32))
    chosen_pos = jnp.where(in_time[None, :], frame_pos[:, None], jnp.where(in_rows[None, :], row_pos[:, None], column_pos[:, None]))
    return chosen_pos * rates[None, :]

def rotate(values, angle, sign):
    count = values.shape[0]
    heads_view = values.reshape(count, -1, HEAD_DIM)
    cosine = jnp.cos(angle)[:, None, :]
    sine = sign * jnp.sin(angle)[:, None, :]
    after = jnp.roll(heads_view, -1, axis=2)
    before = jnp.roll(heads_view, 1, axis=2)
    is_even = jnp.arange(HEAD_DIM) % 2 == 0
    partner = jnp.where(is_even, -after, before)
    return (heads_view * cosine + partner * sine).reshape(count, -1)

def normalize(raw_rows):
    widened = raw_rows.astype(jnp.float32)
    rho_rows = lax.rsqrt(lax.optimization_barrier(jnp.mean(widened * widened, axis=-1, keepdims=True)) + NORM_EPS)
    return (widened * rho_rows, rho_rows)

def norm_back(grad_rot, normed, rho_rows, gain, angle):
    widened = gain[None, :] * rotate(grad_rot.astype(jnp.float32), angle, -1.0)
    along = lax.optimization_barrier(jnp.mean(normed * widened, axis=-1, keepdims=True))
    return (rho_rows * (widened - normed * along)).astype(jnp.bfloat16)

def head_grads(operands, visible):
    queries, key_rows, value_rows, grad_rows = operands
    scaling = 1.0 / math.sqrt(HEAD_DIM)
    scores = jnp.dot(queries, key_rows.T, preferred_element_type=jnp.float32) * scaling
    scores = jnp.where(visible, scores, -jnp.inf)
    row_top = lax.optimization_barrier(jnp.max(scores, axis=-1, keepdims=True))
    weights = jnp.exp(scores - row_top)
    prob_rows = weights / lax.optimization_barrier(jnp.sum(weights, axis=-1, keepdims=True))
    prob_half = prob_rows.astype(jnp.bfloat16)
    grad_prob = jnp.dot(grad_rows, value_rows.T, preferred_element_type=jnp.float32)
    row_delta = lax.optimization_barrier(jnp.sum(prob_rows * grad_prob, axis=-1, keepdims=True))
    grad_score = (prob_rows * (grad_prob - row_delta)).astype(jnp.bfloat16)
    grad_query = (jnp.dot(grad_score, key_rows, preferred_element_type=jnp.float32) * scaling).astype(jnp.bfloat16)
    grad_key = (jnp.dot(grad_score.T, queries, preferred_element_type=jnp.float32) * scaling).astype(jnp.bfloat16)
    grad_value = jnp.dot(prob_half.T, grad_rows, preferred_element_type=jnp.float32).astype(jnp.bfloat16)
    return (grad_query, grad_key, grad_value)

def reference(input_tokens, query_unnormed, key_unnormed, value_projected, cotangent, query_norm_gain, key_norm_gain, adapter_down_maps, adapter_up_maps, generated_mask, block_begin_flags):
    angle = rope_angles(jnp.arange(TOKENS, dtype=jnp.int32))

    def per_video(members):
        layer_activations, raw_query, raw_key, value_rows, cot_rows, mask_rows, starts = members
        block_frame = (jnp.cumsum(starts) - 1).astype(jnp.int32)
        block_tok = jnp.repeat(block_frame, FRAME_TOK)
        visible = block_tok[None, :] <= block_tok[:, None]
        normed_q, rho_q = normalize(raw_query)
        normed_k, rho_k = normalize(raw_key)
        queries = rotate(normed_q * query_norm_gain[None, :], angle, 1.0).astype(jnp.bfloat16)
        key_rows = rotate(normed_k * key_norm_gain[None, :], angle, 1.0).astype(jnp.bfloat16)
        grad_rows = jnp.where(mask_rows.reshape(-1)[:, None] > 0, cot_rows, jnp.zeros_like(cot_rows))

        def by_head(array):
            return array.reshape(TOKENS, HEADS, HEAD_DIM).transpose(1, 0, 2)

        def by_token(array):
            return array.transpose(1, 0, 2).reshape(TOKENS, HEAD_CHANNELS)

        def per_head(operands):
            return head_grads(operands, visible)
        grad_query, grad_key, grad_value = lax.map(per_head, (by_head(queries), by_head(key_rows), by_head(value_rows), by_head(grad_rows)))
        gradient_bundle = (norm_back(by_token(grad_query), normed_q, rho_q, query_norm_gain, angle), norm_back(by_token(grad_key), normed_k, rho_k, key_norm_gain, angle), by_token(grad_value))
        down_projected = jnp.einsum('mv,xkv->xkm', layer_activations.astype(jnp.float32), adapter_down_maps.astype(jnp.float32)).astype(jnp.bfloat16)
        downs = []
        uppers = []
        for adapter_branch in range(3):
            mixed_output = jnp.dot(adapter_up_maps[adapter_branch], gradient_bundle[adapter_branch].T, preferred_element_type=jnp.float32).astype(jnp.bfloat16)
            downs.append(jnp.dot(mixed_output, layer_activations, preferred_element_type=jnp.float32))
            uppers.append(jnp.dot(down_projected[adapter_branch], gradient_bundle[adapter_branch], preferred_element_type=jnp.float32))
        return (jnp.stack(downs), jnp.stack(uppers))
    downs, uppers = lax.map(per_video, (input_tokens, query_unnormed, key_unnormed, value_projected, cotangent, generated_mask, block_begin_flags))
    return (lax.optimization_barrier(jnp.sum(downs, axis=0)).astype(jnp.bfloat16), lax.optimization_barrier(jnp.sum(uppers, axis=0)).astype(jnp.bfloat16))
```

```python
import functools
import math

import jax
import jax.numpy as jnp
import numpy as np
from jax import lax
from jax.experimental import pallas as pl
from jax.experimental.pallas import tpu as pltpu
from jax.sharding import PartitionSpec as P

HEADS = 24
HEAD_DIM = 128
GRID_W = 16
FRAME_TOK = 128
FRAMES = 8
RANK = 32
WIDTH = 5120
CHANNELS = 3072
GROUPS = 8
LOCAL_HEADS = 3
NORM_EPS = 1e-06
SCALING = 1.0 / math.sqrt(HEAD_DIM)
BF = jnp.bfloat16
F32 = jnp.float32
HIDDEN = -1e30
COLS = WIDTH // 8
GCOLS = CHANNELS // 8
BOTH = COLS + GCOLS

VMEM = pl.BlockSpec(memory_space=pltpu.VMEM)
SMEM = pl.BlockSpec(memory_space=pltpu.SMEM)


def params(mib):
    return pltpu.CompilerParams(vmem_limit_bytes=mib * 1024 * 1024)


def rope_tables():
    time_dims = HEAD_DIM - 4 * (HEAD_DIM // 6)
    space_dims = 2 * (HEAD_DIM // 6)
    tp, sp = time_dims // 2, space_dims // 2
    tok = np.arange(FRAMES * FRAME_TOK)
    frame, within = tok // FRAME_TOK, tok % FRAME_TOK
    row, col = within // GRID_W, within % GRID_W
    pairs = np.arange(HEAD_DIM) // 2
    in_time = pairs < tp
    in_rows = (pairs >= tp) & (pairs < tp + sp)
    offset = np.where(in_time, pairs, np.where(in_rows, pairs - tp, pairs - tp - sp))
    extent = np.where(in_time, time_dims, space_dims)
    rates = np.exp(-math.log(10000.0) * (2 * offset) / extent)
    pos = np.where(
        in_time[None], frame[:, None], np.where(in_rows[None], row[:, None], col[:, None])
    )
    angle = pos * rates[None]
    even = (np.arange(HEAD_DIM) % 2 == 0)[None]
    sine = np.sin(angle)
    table = np.stack([np.cos(angle), np.where(even, -sine, 0.0), np.where(even, 0.0, sine)], 0)
    table = table.reshape(3, FRAMES, FRAME_TOK, HEAD_DIM).transpose(1, 0, 2, 3)
    return table.astype(np.float32)


def turn(z, table, frame, sign):
    after = pltpu.roll(z, HEAD_DIM - 1, 1) * table[frame, 1]
    before = pltpu.roll(z, 1, 1) * table[frame, 2]
    mixed = after + before
    base = z * table[frame, 0]
    return base + mixed if sign > 0 else base - mixed


def nt(a, b, **kw):
    return lax.dot_general(
        a, b, (((1,), (1,)), ((), ())), preferred_element_type=F32, **kw
    )


def nn(a, b):
    return lax.dot_general(a, b, (((1,), (0,)), ((), ())), preferred_element_type=F32)


def pack_vc_kernel(meta, value, cot, mask, *outs):
    s = meta[0]
    keep = jnp.broadcast_to(mask[...].astype(F32), (FRAME_TOK, FRAME_TOK)).T > 0.0
    for k in range(GROUPS):
        for h in range(LOCAL_HEADS):
            at = pl.ds(pl.multiple_of((jnp.bitwise_xor(s, k) * LOCAL_HEADS + h) * HEAD_DIM, HEAD_DIM), HEAD_DIM)
            outs[k][h, 0] = value[:, at]
            outs[k][h, 1] = jnp.where(keep, cot[:, at].astype(F32), 0.0).astype(BF)


def rho_of(raw):
    total = jnp.zeros((FRAME_TOK, HEAD_DIM), F32)
    for n in range(HEADS):
        part = raw[:, n * HEAD_DIM : (n + 1) * HEAD_DIM].astype(F32)
        total = total + part * part
    mean = jnp.sum(total, axis=1, keepdims=True) * (1.0 / CHANNELS)
    return lax.rsqrt(mean + NORM_EPS)


def prepare_kernel(meta, query, key, gains, table, ups, downs, tokens, *outs):
    s = meta[0]
    sends, aux, local = outs[:24], outs[24], outs[25]
    rows = []
    for n, raw in ((0, query), (1, key)):
        rho = rho_of(raw)
        rows.append(jnp.broadcast_to(rho, (FRAME_TOK, FRAME_TOK)).T[0:8])
        carried = jnp.zeros((RANK, FRAME_TOK), F32)
        for h in range(LOCAL_HEADS):
            for k in range(GROUPS):
                head = jnp.bitwise_xor(s, k) * LOCAL_HEADS + h
                at = pl.ds(pl.multiple_of(head * HEAD_DIM, HEAD_DIM), HEAD_DIM)
                normed = raw[:, at].astype(F32) * rho
                carried = carried + nt(ups[n, :, at], normed.astype(BF))
                turned = turn(normed * gains[n, head], table, s, 1)
                sends[h * GROUPS + k][n] = turned.astype(BF)
        local[n * RANK : (n + 1) * RANK, :] = carried
        local[64 + 8 * n : 72 + 8 * n, :] = rows[n]
    aux[0:96, :] = nt(downs[...], tokens[...]).astype(BF)
    at_row = lax.broadcasted_iota(jnp.int32, (16, FRAME_TOK), 0)
    extra = jnp.zeros((16, FRAME_TOK), F32)
    for n in range(2):
        wide = jnp.concatenate([rows[n], rows[n]], 0)
        high = wide.astype(BF).astype(F32)
        extra = jnp.where(at_row == 2 * n, high, extra)
        extra = jnp.where(at_row == 2 * n + 1, wide - high, extra)
    aux[96:112, :] = extra.astype(BF)


def attend_kernel(h, last, *refs):
    meta, blocks = refs[0], refs[1]
    qk, vc = refs[2:10], refs[10:18]
    gains, table, ups = refs[18:21]
    pos = 21
    before = None
    if h > 0:
        before = refs[pos]
        pos += 1
    wide_out = refs[pos]
    pos += 1
    if last:
        mix = refs[pos : pos + GROUPS]
        pos += GROUPS
    else:
        summed = refs[pos]
        pos += 1
    q_s, k_s, kt_s, v_s, g_s, sc, dp, pb, db, dk_acc, dv_acc, dq_s = refs[pos:]
    s = meta[0]
    head = s * LOCAL_HEADS + h
    for k in range(GROUPS):
        at = slice(k * FRAME_TOK, (k + 1) * FRAME_TOK)
        q_s[at, :] = qk[k][0]
        key = qk[k][1]
        k_s[at, :] = key
        kt_s[:, at] = key.astype(F32).T.astype(BF)
        v_s[at, :] = vc[k][0, 0]
        g_s[at, :] = vc[k][0, 1]
    owner = [blocks[jnp.bitwise_xor(s, k)] for k in range(GROUPS)]
    factor = SCALING * math.log2(math.e)
    lane = lax.broadcasted_iota(jnp.int32, (1, 256), 1)
    for t in range(4):
        b = t % 2
        tile = slice(t * 256, (t + 1) * 256)
        q_t, g_t = q_s[tile, :], g_s[tile, :]
        limit = jnp.where(lane < FRAME_TOK, owner[2 * t], owner[2 * t + 1])
        top = jnp.full((8, 256), 2.0 * HIDDEN, F32)
        for j in range(GROUPS):
            at = slice(j * FRAME_TOK, (j + 1) * FRAME_TOK)
            bias = jnp.where(owner[j] <= limit, 0.0, HIDDEN)
            part = nt(k_s[at, :], q_t) + bias
            sc[b, at, :] = part
            dp[b, at, :] = nt(v_s[at, :], g_t)
            top = jnp.maximum(top, jnp.max(part.reshape(16, 8, 256), axis=0))
        top = jnp.max(top, axis=0, keepdims=True)
        total = jnp.zeros((8, 256), F32)
        cross = jnp.zeros((8, 256), F32)
        for j in range(GROUPS):
            at = slice(j * FRAME_TOK, (j + 1) * FRAME_TOK)
            weight = jnp.exp2((sc[b, at, :] - top) * factor)
            sc[b, at, :] = weight
            total = total + jnp.sum(weight.reshape(16, 8, 256), axis=0)
            cross = cross + jnp.sum((weight * dp[b, at, :]).reshape(16, 8, 256), axis=0)
        inverse = 1.0 / jnp.sum(total, axis=0, keepdims=True)
        delta = jnp.sum(cross, axis=0, keepdims=True) * inverse
        for j in range(GROUPS):
            at = slice(j * FRAME_TOK, (j + 1) * FRAME_TOK)
            prob = sc[b, at, :] * inverse
            pb[b, at, :] = prob.astype(BF)
            db[b, at, :] = (prob * (dp[b, at, :] - delta)).astype(BF)
        dv, dk = nn(pb[b], g_t), nn(db[b], q_t)
        if t == 0:
            dv_acc[...] = dv
            dk_acc[...] = dk
        else:
            dv_acc[...] += dv
            dk_acc[...] += dk
        dq_s[tile, :] = nn(kt_s[...], db[b]).T
    up_at = pl.ds(pl.multiple_of(head * HEAD_DIM, HEAD_DIM), HEAD_DIM)
    ones = jnp.ones((8, HEAD_DIM), F32)
    sums = []
    for k in range(GROUPS):
        frame = jnp.bitwise_xor(s, k)
        at = slice(k * FRAME_TOK, (k + 1) * FRAME_TOK)
        rows, means = [], []
        for n, (acc, rot) in enumerate(((dq_s, q_s), (dk_acc, k_s))):
            grad = (acc[at, :] * SCALING).astype(BF).astype(F32)
            wide = (gains[n, head] * turn(grad, table, frame, -1)).astype(BF)
            wide_out[n, at, :] = wide
            rows.append(nt(ups[n, :, up_at], wide))
            means.append(nt(ones, grad * rot[at, :].astype(F32), precision=lax.Precision.HIGHEST))
        value = dv_acc[at, :].astype(BF)
        wide_out[2, at, :] = value
        rows.append(nt(ups[2, :, up_at], value))
        part = jnp.concatenate(rows + means, 0)
        if before is not None:
            part = part + before[k]
        sums.append(part)
    if not last:
        for k in range(GROUPS):
            summed[k] = sums[k]
        return
    at_row = lax.broadcasted_iota(jnp.int32, (8, FRAME_TOK), 0)
    highs, lows = [], []
    for n in range(2):
        gathered = jnp.zeros((8, FRAME_TOK), F32)
        for k in range(GROUPS):
            gathered = jnp.where(at_row == k, sums[k][96 + 8 * n : 104 + 8 * n], gathered)
        high = gathered.astype(BF).astype(F32)
        highs.append(high)
        lows.append(gathered - high)
    tail = jnp.concatenate(highs + lows, 0)
    for k in range(GROUPS):
        mix[k][...] = jnp.concatenate([sums[k][0:96], tail], 0).astype(BF)


def owner_kernel(meta, *refs):
    mixes = refs[:GROUPS]
    local, tokens, keep, send, rows_s, mixed_s = refs[GROUPS:]
    y, x, c = meta[1], meta[2], meta[3]
    total = jnp.zeros((96, FRAME_TOK), F32)
    means = [jnp.zeros((1, FRAME_TOK), F32) for _ in range(2)]
    for k in range(GROUPS):
        part = mixes[k][...].astype(F32)
        total = total + part[0:96]
        for n in range(2):
            first = 96 + 8 * n + k
            means[n] = means[n] + part[first : first + 1] + part[first + 16 : first + 17]
    for n in range(2):
        at = slice(n * RANK, (n + 1) * RANK)
        rho = local[64 + 8 * n : 65 + 8 * n, :]
        mean = means[n] * (1.0 / CHANNELS)
        rows_s[at, :] = rho * (total[at] - mean * local[at, :])
    rows_s[64:96, :] = total[64:96]
    for k in range(4):
        first = pl.multiple_of(jnp.bitwise_xor(y, k) * 24, 8)
        mixed_s[k * 24 : (k + 1) * 24, :] = rows_s[pl.ds(first, 24), :]
    mixed = mixed_s[...].astype(BF)
    for a in range(2):
        for b in range(4):
            block = jnp.bitwise_xor(c, a) * 4 + jnp.bitwise_xor(x, b)
            at = pl.ds(pl.multiple_of(block * COLS, HEAD_DIM), COLS)
            out = nn(mixed, tokens[:, at])
            for k in range(4):
                part = out[k * 24 : (k + 1) * 24]
                if a == 0:
                    keep[b, k] = part
                else:
                    send[b, k] = part.astype(BF)


def up_kernel(meta, *refs):
    mixes, auxes = refs[:8], refs[8:16]
    qks, wides = refs[16:40], refs[40:43]
    gains, table, keep, send, turned_s, up_s = refs[43:]
    s, x, c = meta[0], meta[2], meta[3]
    xl = jnp.bitwise_and(x, 1)
    for h in range(LOCAL_HEADS):
        lanes = slice(h * HEAD_DIM, (h + 1) * HEAD_DIM)
        for k in range(GROUPS):
            at = slice(k * FRAME_TOK, (k + 1) * FRAME_TOK)
            frame = jnp.bitwise_xor(s, k)
            for n in range(2):
                rot = qks[h * GROUPS + k][n].astype(F32)
                turned_s[n, at, lanes] = turn(rot, table, frame, -1).astype(BF)
    tails = [mixes[k][96:128, :].astype(F32) for k in range(GROUPS)]
    for n in range(3):
        plain_hi, plain_lo, along = [], [], []
        for p in range(GROUPS):
            aux = auxes[p][...].astype(F32)
            down = aux[n * RANK : (n + 1) * RANK]
            if n == 2:
                plain_hi.append(down.astype(BF))
                continue
            rho = aux[96 + 2 * n : 97 + 2 * n] + aux[97 + 2 * n : 98 + 2 * n]
            mean = jnp.zeros((1, FRAME_TOK), F32)
            for k in range(GROUPS):
                row = 8 * n + (p ^ k)
                mean = mean + tails[k][row : row + 1] + tails[k][row + 16 : row + 17]
            scaled = down * rho
            high = scaled.astype(BF)
            plain_hi.append(high)
            plain_lo.append((scaled - high.astype(F32)).astype(BF))
            along.append((scaled * (mean * (1.0 / CHANNELS))).astype(BF))
        high = jnp.concatenate(plain_hi, 1)
        for h in range(LOCAL_HEADS):
            lanes = slice(h * HEAD_DIM, (h + 1) * HEAD_DIM)
            out = nn(high, wides[h][n])
            if n < 2:
                gain = gains[n, s * LOCAL_HEADS + h]
                out = out + nn(jnp.concatenate(plain_lo, 1), wides[h][n])
                out = out - nn(jnp.concatenate(along, 1), turned_s[n, :, lanes]) / gain
            up_s[n * RANK : (n + 1) * RANK, lanes] = out
    for a in range(2):
        for b in range(2):
            block = jnp.bitwise_xor(c, a) * 2 + jnp.bitwise_xor(xl, b)
            part = up_s[pl.ds(pl.multiple_of(block * 24, 8), 24), :]
            if a == 0:
                keep[b] = part
            else:
                send[b] = part.astype(BF)


def core_sum_kernel(keep, got, own, *sends):
    for b in range(4):
        value = keep[b] + got[b].astype(F32)
        if b == 0:
            own[...] = value
        else:
            sends[b - 1][...] = value.astype(BF)


def up_core_kernel(keep, got, own, send):
    own[...] = keep[0] + got[0].astype(F32)
    send[...] = (keep[1] + got[1].astype(F32)).astype(BF)


def x_sum_kernel(own, r1, r2, r3, keep, *sends):
    for b in range(4):
        value = (own[b] + r1[b].astype(F32)) + (r2[b].astype(F32) + r3[b].astype(F32))
        if b == 0:
            keep[...] = value
        else:
            sends[b - 1][...] = value.astype(BF)


def y_sum_kernel(own, r1, r2, r3, up_own, up_got, out):
    value = (own[...] + r1[...].astype(F32)) + (r2[...].astype(F32) + r3[...].astype(F32))
    out[:, :COLS] = value.astype(BF)
    out[:, COLS:] = (up_own[...] + up_got[...].astype(F32)).astype(BF)


def z_sum_kernel(*refs):
    parts = [ref[...].astype(F32) for ref in refs[:8]]
    while len(parts) > 1:
        parts = [parts[n] + parts[n + 1] for n in range(0, len(parts), 2)]
    refs[8][...] = parts[0].astype(BF)


def stack_kernel(*refs):
    out = refs[-1]
    for n, ref in enumerate(refs[:-1]):
        out[n] = ref[...]


def final_kernel(meta, own, got, down_out, up_out):
    y, x, c = meta[1], meta[2], meta[3]

    def piece(ca, xa, ya, lanes):
        xr, yr = jnp.bitwise_xor(x, xa), jnp.bitwise_xor(y, ya)
        mine = own[xr, yr, :, lanes].astype(F32)
        other = got[xr, yr, :, lanes].astype(F32)
        return jnp.where(c == ca, mine, other)

    for ca in range(2):
        for xa in range(4):
            block = [piece(ca, xa, ya, slice(0, COLS)) for ya in range(4)]
            first = (ca * 4 + xa) * COLS
            down_out[:, first : first + COLS] = jnp.concatenate(block, 0).astype(BF)
    for ya in range(4):
        for xh in range(2):
            block = [
                piece(ca, xh * 2 + xl, ya, slice(COLS, BOTH)) for ca in range(2) for xl in range(2)
            ]
            first = (ya * 2 + xh) * GCOLS
            up_out[:, first : first + GCOLS] = jnp.concatenate(block, 0).astype(BF)


def shape(dims, dtype=BF):
    return jax.ShapeDtypeStruct(dims, dtype)


def call(kernel, ins, outs, scratch=(), smem=0, mib=16):
    single = not isinstance(outs, (list, tuple))
    return pl.pallas_call(
        kernel,
        out_shape=outs,
        in_specs=[SMEM] * smem + [VMEM] * (len(ins) - smem),
        out_specs=VMEM if single else [VMEM] * len(outs),
        scratch_shapes=list(scratch),
        compiler_params=params(mib),
    )(*ins)


def place(x, y, z, c):
    return (y * 2 + x // 2) * 32 + z * 4 + (x % 2) * 2 + c


def swap(array, dx=0, dy=0, dz=0, dc=0):
    pairs = [
        (place(x, y, z, c), place(x ^ dx, y ^ dy, z ^ dz, c ^ dc))
        for x in range(4)
        for y in range(4)
        for z in range(8)
        for c in range(2)
    ]
    return lax.ppermute(array, ("seq", "dp"), pairs)


def seq_swap(array, k):
    return swap(array, dx=2 * (k & 1), dy=k >> 1)


def seq_all(arrays):
    return [arrays[0]] + [seq_swap(arrays[k], k) for k in range(1, GROUPS)]


def attend(h, meta, blocks, qk, vc, gains, table, ups, before):
    last = h == LOCAL_HEADS - 1
    seq_len = FRAMES * FRAME_TOK
    piece = pl.BlockSpec((1, 2, FRAME_TOK, HEAD_DIM), lambda i: (h, 0, 0, 0))
    ins = [meta, blocks, *qk, *vc, gains, table, ups]
    specs = [SMEM] * 2 + [VMEM] * 8 + [piece] * 8 + [VMEM] * 3
    if before is not None:
        ins.append(before)
        specs.append(VMEM)
    outs = [shape((3, seq_len, HEAD_DIM))]
    if last:
        outs += [shape((128, FRAME_TOK))] * GROUPS
    else:
        outs += [shape((GROUPS, 112, FRAME_TOK), F32)]
    rows = (seq_len, HEAD_DIM)
    return pl.pallas_call(
        functools.partial(attend_kernel, h, last),
        grid=(1,),
        out_shape=outs,
        in_specs=specs,
        out_specs=[VMEM] * len(outs),
        scratch_shapes=[
            pltpu.VMEM(rows, BF),
            pltpu.VMEM(rows, BF),
            pltpu.VMEM((HEAD_DIM, seq_len), BF),
            pltpu.VMEM(rows, BF),
            pltpu.VMEM(rows, BF),
            pltpu.VMEM((2, seq_len, 256), F32),
            pltpu.VMEM((2, seq_len, 256), F32),
            pltpu.VMEM((2, seq_len, 256), BF),
            pltpu.VMEM((2, seq_len, 256), BF),
            pltpu.VMEM(rows, F32),
            pltpu.VMEM(rows, F32),
            pltpu.VMEM(rows, F32),
        ],
        compiler_params=params(32),
        cost_estimate=pl.CostEstimate(
            flops=10 * seq_len * seq_len * HEAD_DIM, bytes_accessed=4 << 20, transcendentals=seq_len * seq_len
        ),
    )(*ins)


def shards(
    input_tokens,
    query_unnormed,
    key_unnormed,
    value_projected,
    cotangent,
    query_norm_gain,
    key_norm_gain,
    adapter_down_maps,
    adapter_up_maps,
    generated_mask,
    block_begin_flags,
):
    s, d = lax.axis_index("seq"), lax.axis_index("dp")
    y, x, c = s // 2, (s % 2) * 2 + (d // 2) % 2, d % 2
    meta = jnp.stack([s, y, x, c]).astype(jnp.int32)
    blocks = jnp.cumsum(block_begin_flags[0]).astype(jnp.int32)
    table = jnp.asarray(rope_tables())
    gains = jnp.stack([query_norm_gain, key_norm_gain]).reshape(2, HEADS, 1, HEAD_DIM)
    tokens = input_tokens[0]
    downs = adapter_down_maps.reshape(96, WIDTH)

    vc = call(
        pack_vc_kernel,
        [meta, value_projected[0], cotangent[0], generated_mask[0]],
        [shape((LOCAL_HEADS, 2, FRAME_TOK, HEAD_DIM))] * GROUPS,
        smem=1,
    )
    vc = seq_all(vc)
    *sends, aux, local = call(
        prepare_kernel,
        [meta, query_unnormed[0], key_unnormed[0], gains, table, adapter_up_maps, downs, tokens],
        [shape((2, FRAME_TOK, HEAD_DIM))] * 24
        + [shape((112, FRAME_TOK)), shape((80, FRAME_TOK), F32)],
        smem=1,
        mib=24,
    )
    qks, wides = [], []
    before = None
    for h in range(LOCAL_HEADS):
        qks.append(seq_all(sends[h * GROUPS : (h + 1) * GROUPS]))
    auxes = seq_all([aux] * GROUPS)
    for h in range(LOCAL_HEADS):
        wide, *rest = attend(
            h, meta, blocks, qks[h], vc, gains, table, adapter_up_maps, before
        )
        wides.append(wide)
        before = rest[0]
    mixes = seq_all(rest)

    keep, send = call(
        owner_kernel,
        [meta, *mixes, local, tokens],
        [shape((4, 4, 24, COLS), F32), shape((4, 4, 24, COLS))],
        [pltpu.VMEM((96, FRAME_TOK), F32), pltpu.VMEM((96, FRAME_TOK), F32)],
        smem=1,
    )
    up_keep, up_send = call(
        up_kernel,
        [meta, *mixes, *auxes, *[q for qk in qks for q in qk], *wides, gains, table],
        [shape((2, 24, GCOLS), F32), shape((2, 24, GCOLS))],
        [pltpu.VMEM((2, 1024, GCOLS), BF), pltpu.VMEM((96, GCOLS), F32)],
        smem=1,
        mib=24,
    )
    got = swap(send, dc=1)
    up_got = swap(up_send, dc=1)
    slab = (4, 24, COLS)
    own, *parts = call(
        core_sum_kernel, [keep, got], [shape(slab, F32)] + [shape(slab)] * 3
    )
    up_own, up_part = call(
        up_core_kernel, [up_keep, up_got], [shape((24, GCOLS), F32), shape((24, GCOLS))]
    )
    parts = [swap(parts[n], dx=n + 1) for n in range(3)]
    up_part = swap(up_part, dx=1)
    own, *parts = call(
        x_sum_kernel, [own, *parts], [shape(slab[1:], F32)] + [shape(slab[1:])] * 3
    )
    parts = [swap(parts[n], dy=n + 1) for n in range(3)]
    part = call(y_sum_kernel, [own, *parts, up_own, up_part], shape((24, BOTH)))
    part = call(
        z_sum_kernel, [part] + [swap(part, dz=k) for k in range(1, 8)], shape((24, BOTH))
    )
    over_y = call(
        stack_kernel, [part] + [swap(part, dy=k) for k in range(1, 4)], shape((4, 24, BOTH))
    )
    over_x = call(
        stack_kernel,
        [over_y] + [swap(over_y, dx=k) for k in range(1, 4)],
        shape((4, 4, 24, BOTH)),
    )
    other = swap(over_x, dc=1)
    grad_down, grad_up = call(
        final_kernel,
        [meta, over_x, other],
        [shape((96, WIDTH)), shape((96, CHANNELS))],
        smem=1,
    )
    return grad_down.reshape(3, RANK, WIDTH), grad_up.reshape(3, RANK, CHANNELS)


def solution(mesh):
    rows = P("dp", "seq", None)
    placed = (rows,) * 5 + (P(),) * 4 + (rows, P("dp", None))
    return jax.shard_map(shards, mesh=mesh, in_specs=placed, out_specs=(P(), P()), check_vma=False)
```

```python
import functools
import math

import jax
import jax.numpy as jnp
import numpy as np
from jax import lax
from jax.experimental import pallas as pl
from jax.experimental.pallas import tpu as pltpu
from jax.sharding import PartitionSpec as P

HEADS = 24
HEAD_DIM = 128
GRID_W = 16
FRAME_TOK = 128
FRAMES = 8
RANK = 32
WIDTH = 5120
CHANNELS = 3072
GROUPS = 8
LOCAL_HEADS = 3
NORM_EPS = 1e-06
SCALING = 1.0 / math.sqrt(HEAD_DIM)
BF = jnp.bfloat16
F32 = jnp.float32
HIDDEN = -1e30
COLS = WIDTH // 8
GCOLS = CHANNELS // 8
BOTH = COLS + GCOLS

VMEM = pl.BlockSpec(memory_space=pltpu.VMEM)
SMEM = pl.BlockSpec(memory_space=pltpu.SMEM)


def params(mib):
    return pltpu.CompilerParams(vmem_limit_bytes=mib * 1024 * 1024)


def rope_tables():
    time_dims = HEAD_DIM - 4 * (HEAD_DIM // 6)
    space_dims = 2 * (HEAD_DIM // 6)
    tp, sp = time_dims // 2, space_dims // 2
    tok = np.arange(FRAMES * FRAME_TOK)
    frame, within = tok // FRAME_TOK, tok % FRAME_TOK
    row, col = within // GRID_W, within % GRID_W
    pairs = np.arange(HEAD_DIM) // 2
    in_time = pairs < tp
    in_rows = (pairs >= tp) & (pairs < tp + sp)
    offset = np.where(in_time, pairs, np.where(in_rows, pairs - tp, pairs - tp - sp))
    extent = np.where(in_time, time_dims, space_dims)
    rates = np.exp(-math.log(10000.0) * (2 * offset) / extent)
    pos = np.where(
        in_time[None], frame[:, None], np.where(in_rows[None], row[:, None], col[:, None])
    )
    angle = pos * rates[None]
    even = (np.arange(HEAD_DIM) % 2 == 0)[None]
    sine = np.sin(angle)
    table = np.stack([np.cos(angle), np.where(even, -sine, 0.0), np.where(even, 0.0, sine)], 0)
    table = table.reshape(3, FRAMES, FRAME_TOK, HEAD_DIM).transpose(1, 0, 2, 3)
    return table.astype(np.float32)


def turn(z, table, frame, sign):
    after = pltpu.roll(z, HEAD_DIM - 1, 1) * table[frame, 1]
    before = pltpu.roll(z, 1, 1) * table[frame, 2]
    mixed = after + before
    base = z * table[frame, 0]
    return base + mixed if sign > 0 else base - mixed


def nt(a, b, **kw):
    return lax.dot_general(
        a, b, (((1,), (1,)), ((), ())), preferred_element_type=F32, **kw
    )


def nn(a, b):
    return lax.dot_general(a, b, (((1,), (0,)), ((), ())), preferred_element_type=F32)


def rho_of(raw):
    total = jnp.zeros((FRAME_TOK, HEAD_DIM), F32)
    for n in range(HEADS):
        part = raw[:, n * HEAD_DIM : (n + 1) * HEAD_DIM].astype(F32)
        total = total + part * part
    mean = jnp.sum(total, axis=1, keepdims=True) * (1.0 / CHANNELS)
    return lax.rsqrt(mean + NORM_EPS)


def pack_kernel(heads, meta, query, key, value, cot, mask, gains, table, *refs):
    s = meta[0]
    ups, downs, tokens = refs[:3] if len(refs) > GROUPS else (None,) * 3
    outs = refs[-GROUPS - 1 : -1] if len(refs) > GROUPS else refs
    keep = jnp.broadcast_to(mask[...].astype(F32), (FRAME_TOK, FRAME_TOK)).T > 0.0
    rhos = [rho_of(raw) for raw in (query, key)]
    for k in range(GROUPS):
        for i, h in enumerate(heads):
            head = jnp.bitwise_xor(s, k) * LOCAL_HEADS + h
            at = pl.ds(pl.multiple_of(head * HEAD_DIM, HEAD_DIM), HEAD_DIM)
            for n, raw in ((0, query), (1, key)):
                normed = raw[:, at].astype(F32) * rhos[n]
                outs[k][4 * i + n] = turn(normed * gains[n, head], table, s, 1).astype(BF)
            outs[k][4 * i + 2] = value[:, at]
            outs[k][4 * i + 3] = jnp.where(keep, cot[:, at].astype(F32), 0.0).astype(BF)
    if ups is None:
        return
    local = refs[-1]
    rows = []
    for n, raw in ((0, query), (1, key)):
        rows.append(jnp.broadcast_to(rhos[n], (FRAME_TOK, FRAME_TOK)).T[0:8])
        carried = jnp.zeros((RANK, FRAME_TOK), F32)
        for head in range(HEADS):
            at = slice(head * HEAD_DIM, (head + 1) * HEAD_DIM)
            normed = (raw[:, at].astype(F32) * rhos[n]).astype(BF)
            carried = carried + nt(ups[n, :, at], normed)
        local[n * RANK : (n + 1) * RANK, :] = carried
        local[64 + 8 * n : 72 + 8 * n, :] = rows[n]
    down = nt(downs[...], tokens[...])
    at_row = lax.broadcasted_iota(jnp.int32, (RANK, FRAME_TOK), 0)
    extra = jnp.zeros((RANK, FRAME_TOK), F32)
    for n in range(2):
        wide = jnp.concatenate([rows[n]] * 4, 0)
        high = wide.astype(BF).astype(F32)
        extra = jnp.where(at_row == 2 * n, high, extra)
        extra = jnp.where(at_row == 2 * n + 1, wide - high, extra)
    aux = jnp.concatenate([down, extra], 0).astype(BF)
    for k in range(GROUPS):
        outs[k][4] = aux


def attend_kernel(h, last, *refs):
    meta, blocks = refs[0], refs[1]
    packs = refs[2:10]
    gains, table, ups = refs[10:13]
    pos = 13
    slot = 4 * (h % 2)
    before = None
    if h > 0:
        before = refs[pos]
        pos += 1
    wide_out = refs[pos]
    pos += 1
    summed = refs[pos]
    pos += 1
    if last:
        mean_out, mix = refs[pos : pos + 2]
        pos += 2
    q_s, k_s, kt_s, v_s, g_s, sc, dp, pb, db, dk_acc, dv_acc, dq_s = refs[pos:]
    s = meta[0]
    head = s * LOCAL_HEADS + h
    for k in range(GROUPS):
        at = slice(k * FRAME_TOK, (k + 1) * FRAME_TOK)
        q_s[at, :] = packs[k][slot]
        key = packs[k][slot + 1]
        k_s[at, :] = key
        kt_s[:, at] = key.astype(F32).T.astype(BF)
        v_s[at, :] = packs[k][slot + 2]
        g_s[at, :] = packs[k][slot + 3]
    owner = [blocks[jnp.bitwise_xor(s, k)] for k in range(GROUPS)]
    factor = SCALING * math.log2(math.e)
    lane = lax.broadcasted_iota(jnp.int32, (1, 256), 1)
    for t in range(4):
        b = t % 2
        tile = slice(t * 256, (t + 1) * 256)
        q_t, g_t = q_s[tile, :], g_s[tile, :]
        limit = jnp.where(lane < FRAME_TOK, owner[2 * t], owner[2 * t + 1])
        top = jnp.full((8, 256), 2.0 * HIDDEN, F32)
        for j in range(GROUPS):
            at = slice(j * FRAME_TOK, (j + 1) * FRAME_TOK)
            bias = jnp.where(owner[j] <= limit, 0.0, HIDDEN)
            part = nt(k_s[at, :], q_t) + bias
            sc[b, at, :] = part
            dp[b, at, :] = nt(v_s[at, :], g_t)
            top = jnp.maximum(top, jnp.max(part.reshape(16, 8, 256), axis=0))
        top = jnp.max(top, axis=0, keepdims=True)
        total = jnp.zeros((8, 256), F32)
        cross = jnp.zeros((8, 256), F32)
        for j in range(GROUPS):
            at = slice(j * FRAME_TOK, (j + 1) * FRAME_TOK)
            weight = jnp.exp2((sc[b, at, :] - top) * factor)
            sc[b, at, :] = weight
            total = total + jnp.sum(weight.reshape(16, 8, 256), axis=0)
            cross = cross + jnp.sum((weight * dp[b, at, :]).reshape(16, 8, 256), axis=0)
        inverse = 1.0 / jnp.sum(total, axis=0, keepdims=True)
        delta = jnp.sum(cross, axis=0, keepdims=True) * inverse
        for j in range(GROUPS):
            at = slice(j * FRAME_TOK, (j + 1) * FRAME_TOK)
            prob = sc[b, at, :] * inverse
            pb[b, at, :] = prob.astype(BF)
            db[b, at, :] = (prob * (dp[b, at, :] - delta)).astype(BF)
        dv, dk = nn(pb[b], g_t), nn(db[b], q_t)
        if t == 0:
            dv_acc[...] = dv
            dk_acc[...] = dk
        else:
            dv_acc[...] += dv
            dk_acc[...] += dk
        dq_s[tile, :] = nn(kt_s[...], db[b]).T
    up_at = pl.ds(pl.multiple_of(head * HEAD_DIM, HEAD_DIM), HEAD_DIM)
    ones = jnp.ones((8, HEAD_DIM), F32)
    sums = []
    for k in range(GROUPS):
        frame = jnp.bitwise_xor(s, k)
        at = slice(k * FRAME_TOK, (k + 1) * FRAME_TOK)
        rows, means = [], []
        for n, (acc, rot) in enumerate(((dq_s, q_s), (dk_acc, k_s))):
            grad = (acc[at, :] * SCALING).astype(BF).astype(F32)
            wide = (gains[n, head] * turn(grad, table, frame, -1)).astype(BF)
            wide_out[n, at, :] = wide
            rows.append(nt(ups[n, :, up_at], wide))
            means.append(nt(ones, grad * rot[at, :].astype(F32), precision=lax.Precision.HIGHEST))
        value = dv_acc[at, :].astype(BF)
        wide_out[2, at, :] = value
        rows.append(nt(ups[2, :, up_at], value))
        part = jnp.concatenate(rows + means, 0)
        if before is not None:
            part = part + before[k]
        sums.append(part)
    if not last:
        for k in range(GROUPS):
            summed[k] = sums[k]
        return
    at_row = lax.broadcasted_iota(jnp.int32, (8, FRAME_TOK), 0)
    for n in range(2):
        gathered = jnp.zeros((8, FRAME_TOK), F32)
        for k in range(GROUPS):
            gathered = jnp.where(at_row == k, sums[k][96 + 8 * n : 104 + 8 * n], gathered)
        mean_out[8 * n : 8 * n + 8, :] = gathered
    for i, k in enumerate((0, 1, 4, 5)):
        summed[i] = sums[k][0:96]
        mix[i * 96 : (i + 1) * 96, :] = sums[k ^ 2][0:96].astype(BF)
    mix[384:416, :] = halves(mean_out[...])


def halves(means):
    high = means.astype(BF).astype(F32)
    return jnp.concatenate([high, means - high], 0).astype(BF)


def add_means(means, got, first, bit):
    tail = got[first : first + 32, :].astype(F32)
    tail = tail[0:16] + tail[16:32]
    moved = [tail[8 * n + (p ^ bit) : 8 * n + (p ^ bit) + 1] for n in range(2) for p in range(8)]
    return means[...] + jnp.concatenate(moved, 0)


def mix_kernel(count, bit, keep, means, got, keep_out, means_out, send):
    total = add_means(means, got, 96 * count, bit)
    means_out[...] = total
    half = count // 2
    for i in range(count):
        value = keep[i] + got[i * 96 : (i + 1) * 96, :].astype(F32)
        if i < half:
            keep_out[i] = value
        else:
            send[(i - half) * 96 : (i - half + 1) * 96, :] = value.astype(BF)
    send[half * 96 : half * 96 + 32, :] = halves(total)


def owner_kernel(meta, kept, means, got, local, tokens, keep, send, means_out, rows_s, mixed_s):
    y, x, c = meta[1], meta[2], meta[3]
    total = kept[0] + got[0:96, :].astype(F32)
    full = add_means(means, got, 96, 1)
    means_out[...] = full
    for n in range(2):
        at = slice(n * RANK, (n + 1) * RANK)
        rho = local[64 + 8 * n : 65 + 8 * n, :]
        mean = full[8 * n : 8 * n + 1] * (1.0 / CHANNELS)
        rows_s[at, :] = rho * (total[at] - mean * local[at, :])
    rows_s[64:96, :] = total[64:96]
    for k in range(4):
        first = pl.multiple_of(jnp.bitwise_xor(y, k) * 24, 8)
        mixed_s[k * 24 : (k + 1) * 24, :] = rows_s[pl.ds(first, 24), :]
    mixed = mixed_s[...].astype(BF)
    for a in range(2):
        for b in range(4):
            block = jnp.bitwise_xor(c, a) * 4 + jnp.bitwise_xor(x, b)
            at = pl.ds(pl.multiple_of(block * COLS, HEAD_DIM), COLS)
            out = nn(mixed, tokens[:, at])
            for k in range(4):
                part = out[k * 24 : (k + 1) * 24]
                if a == 0:
                    keep[b, k] = part
                else:
                    send[b, k] = part.astype(BF)


def up_kernel(meta, means, *refs):
    firsts, lasts, wides = refs[:8], refs[8:16], refs[16:19]
    gains, table, keep, send, turned_s, up_s = refs[19:]
    s, x, c = meta[0], meta[2], meta[3]
    xl = jnp.bitwise_and(x, 1)
    for h in range(LOCAL_HEADS):
        lanes = slice(h * HEAD_DIM, (h + 1) * HEAD_DIM)
        for k in range(GROUPS):
            at = slice(k * FRAME_TOK, (k + 1) * FRAME_TOK)
            frame = jnp.bitwise_xor(s, k)
            for n in range(2):
                rot = (lasts if h == 2 else firsts)[k][4 * (h % 2) + n].astype(F32)
                turned_s[n, at, lanes] = turn(rot, table, frame, -1).astype(BF)
    for n in range(3):
        plain_hi, plain_lo, along = [], [], []
        for p in range(GROUPS):
            aux = lasts[p][4].astype(F32)
            down = aux[n * RANK : (n + 1) * RANK]
            if n == 2:
                plain_hi.append(down.astype(BF))
                continue
            rho = aux[96 + 2 * n : 97 + 2 * n] + aux[97 + 2 * n : 98 + 2 * n]
            mean = means[8 * n + p : 8 * n + p + 1, :]
            scaled = down * rho
            high = scaled.astype(BF)
            plain_hi.append(high)
            plain_lo.append((scaled - high.astype(F32)).astype(BF))
            along.append((scaled * (mean * (1.0 / CHANNELS))).astype(BF))
        high = jnp.concatenate(plain_hi, 1)
        for h in range(LOCAL_HEADS):
            lanes = slice(h * HEAD_DIM, (h + 1) * HEAD_DIM)
            out = nn(high, wides[h][n])
            if n < 2:
                gain = gains[n, s * LOCAL_HEADS + h]
                out = out + nn(jnp.concatenate(plain_lo, 1), wides[h][n])
                out = out - nn(jnp.concatenate(along, 1), turned_s[n, :, lanes]) / gain
            up_s[n * RANK : (n + 1) * RANK, lanes] = out
    for a in range(2):
        for b in range(2):
            block = jnp.bitwise_xor(c, a) * 2 + jnp.bitwise_xor(xl, b)
            part = up_s[pl.ds(pl.multiple_of(block * 24, 8), 24), :]
            if a == 0:
                keep[b] = part
            else:
                send[b] = part.astype(BF)


def core_sum_kernel(keep, got, own, *sends):
    for b in range(4):
        value = keep[b] + got[b].astype(F32)
        if b == 0:
            own[...] = value
        else:
            sends[b - 1][...] = value.astype(BF)


def up_core_kernel(keep, got, own, send):
    own[...] = keep[0] + got[0].astype(F32)
    send[...] = (keep[1] + got[1].astype(F32)).astype(BF)


def x_sum_kernel(own, r1, r2, r3, keep, *sends):
    for b in range(4):
        value = (own[b] + r1[b].astype(F32)) + (r2[b].astype(F32) + r3[b].astype(F32))
        if b == 0:
            keep[...] = value
        else:
            sends[b - 1][...] = value.astype(BF)


def y_sum_kernel(own, r1, r2, r3, up_own, up_got, out):
    value = (own[...] + r1[...].astype(F32)) + (r2[...].astype(F32) + r3[...].astype(F32))
    out[:, :COLS] = value.astype(BF)
    out[:, COLS:] = (up_own[...] + up_got[...].astype(F32)).astype(BF)


def z_sum_kernel(own, got, out):
    out[...] = (own[...].astype(F32) + got[...].astype(F32)).astype(BF)


def stack_kernel(*refs):
    out = refs[-1]
    for n, ref in enumerate(refs[:-1]):
        out[n] = ref[...]


def final_kernel(meta, own, got, down_out, up_out):
    y, x, c = meta[1], meta[2], meta[3]

    def piece(ca, xa, ya, lanes):
        xr, yr = jnp.bitwise_xor(x, xa), jnp.bitwise_xor(y, ya)
        mine = own[xr, yr, :, lanes].astype(F32)
        other = got[xr, yr, :, lanes].astype(F32)
        return jnp.where(c == ca, mine, other)

    for ca in range(2):
        for xa in range(4):
            block = [piece(ca, xa, ya, slice(0, COLS)) for ya in range(4)]
            first = (ca * 4 + xa) * COLS
            down_out[:, first : first + COLS] = jnp.concatenate(block, 0).astype(BF)
    for ya in range(4):
        for xh in range(2):
            block = [
                piece(ca, xh * 2 + xl, ya, slice(COLS, BOTH)) for ca in range(2) for xl in range(2)
            ]
            first = (ya * 2 + xh) * GCOLS
            up_out[:, first : first + GCOLS] = jnp.concatenate(block, 0).astype(BF)


def shape(dims, dtype=BF):
    return jax.ShapeDtypeStruct(dims, dtype)


def call(kernel, ins, outs, scratch=(), smem=0, mib=16):
    single = not isinstance(outs, (list, tuple))
    return pl.pallas_call(
        kernel,
        out_shape=outs,
        in_specs=[SMEM] * smem + [VMEM] * (len(ins) - smem),
        out_specs=VMEM if single else [VMEM] * len(outs),
        scratch_shapes=list(scratch),
        compiler_params=params(mib),
    )(*ins)


def place(x, y, z, c):
    return (y * 2 + x // 2) * 32 + z * 4 + (x % 2) * 2 + c


def swap(array, dx=0, dy=0, dz=0, dc=0):
    pairs = [
        (place(x, y, z, c), place(x ^ dx, y ^ dy, z ^ dz, c ^ dc))
        for x in range(4)
        for y in range(4)
        for z in range(8)
        for c in range(2)
    ]
    return lax.ppermute(array, ("seq", "dp"), pairs)


def seq_swap(array, k):
    return swap(array, dx=2 * (k & 1), dy=k >> 1)


def seq_all(arrays):
    return [arrays[0]] + [seq_swap(arrays[k], k) for k in range(1, GROUPS)]


def whole(array):
    zeros = (0,) * array.ndim
    return pl.BlockSpec(array.shape, lambda i: zeros)


def pack(ins, heads, outs):
    return pl.pallas_call(
        functools.partial(pack_kernel, heads),
        grid=(1,),
        out_shape=outs,
        in_specs=[SMEM] + [whole(a) for a in ins[1:]],
        out_specs=[VMEM] * len(outs),
        compiler_params=params(32),
    )(*ins)


def attend(h, meta, blocks, packs, gains, table, ups, before):
    last = h == LOCAL_HEADS - 1
    seq_len = FRAMES * FRAME_TOK
    ins = [meta, blocks, *packs, gains, table, ups]
    specs = [SMEM] * 2 + [VMEM] * 11
    if before is not None:
        ins.append(before)
        specs.append(VMEM)
    outs = [shape((3, seq_len, HEAD_DIM))]
    if last:
        outs += [shape((4, 96, FRAME_TOK), F32), shape((16, FRAME_TOK), F32), shape((416, FRAME_TOK))]
    else:
        outs += [shape((GROUPS, 112, FRAME_TOK), F32)]
    rows = (seq_len, HEAD_DIM)
    return pl.pallas_call(
        functools.partial(attend_kernel, h, last),
        out_shape=outs,
        in_specs=specs,
        out_specs=[VMEM] * len(outs),
        scratch_shapes=[
            pltpu.VMEM(rows, BF),
            pltpu.VMEM(rows, BF),
            pltpu.VMEM((HEAD_DIM, seq_len), BF),
            pltpu.VMEM(rows, BF),
            pltpu.VMEM(rows, BF),
            pltpu.VMEM((2, seq_len, 256), F32),
            pltpu.VMEM((2, seq_len, 256), F32),
            pltpu.VMEM((2, seq_len, 256), BF),
            pltpu.VMEM((2, seq_len, 256), BF),
            pltpu.VMEM(rows, F32),
            pltpu.VMEM(rows, F32),
            pltpu.VMEM(rows, F32),
        ],
        compiler_params=params(32),
        cost_estimate=pl.CostEstimate(
            flops=10 * seq_len * seq_len * HEAD_DIM, bytes_accessed=4 << 20, transcendentals=seq_len * seq_len
        ),
    )(*ins)


def shards(
    input_tokens,
    query_unnormed,
    key_unnormed,
    value_projected,
    cotangent,
    query_norm_gain,
    key_norm_gain,
    adapter_down_maps,
    adapter_up_maps,
    generated_mask,
    block_begin_flags,
):
    s, d = lax.axis_index("seq"), lax.axis_index("dp")
    y, x, c = s // 2, (s % 2) * 2 + (d // 2) % 2, d % 2
    meta = jnp.stack([s, y, x, c]).astype(jnp.int32)
    blocks = jnp.cumsum(block_begin_flags[0]).astype(jnp.int32)
    table = jnp.asarray(rope_tables())
    gains = jnp.stack([query_norm_gain, key_norm_gain]).reshape(2, HEADS, 1, HEAD_DIM)
    tokens = input_tokens[0]
    downs = adapter_down_maps.reshape(96, WIDTH)

    raws = [query_unnormed[0], key_unnormed[0], value_projected[0], cotangent[0]]
    first = [meta, *raws, generated_mask[0], gains, table]
    firsts = pack(first, (0, 1), [shape((8, FRAME_TOK, HEAD_DIM))] * GROUPS)
    *lasts, local = pack(
        first + [adapter_up_maps, downs, tokens],
        (2,),
        [shape((5, FRAME_TOK, HEAD_DIM))] * GROUPS + [shape((80, FRAME_TOK), F32)],
    )
    firsts, lasts = seq_all(firsts), seq_all(lasts)
    wides = []
    before = None
    for h in range(LOCAL_HEADS):
        wide, before, *rest = attend(
            h, meta, blocks, lasts if h == 2 else firsts, gains, table, adapter_up_maps, before
        )
        wides.append(wide)
    means, mix = rest
    kept = before
    for count, bit in ((4, 2), (2, 4)):
        half = count // 2
        kept, means, mix = call(
            functools.partial(mix_kernel, count, bit),
            [kept, means, seq_swap(mix, bit)],
            [
                shape((half, 96, FRAME_TOK), F32),
                shape((16, FRAME_TOK), F32),
                shape((half * 96 + 32, FRAME_TOK)),
            ],
        )
    mix = seq_swap(mix, 1)

    keep, send, means = call(
        owner_kernel,
        [meta, kept, means, mix, local, tokens],
        [shape((4, 4, 24, COLS), F32), shape((4, 4, 24, COLS)), shape((16, FRAME_TOK), F32)],
        [pltpu.VMEM((96, FRAME_TOK), F32), pltpu.VMEM((96, FRAME_TOK), F32)],
        smem=1,
    )
    up_keep, up_send = call(
        up_kernel,
        [meta, means, *firsts, *lasts, *wides, gains, table],
        [shape((2, 24, GCOLS), F32), shape((2, 24, GCOLS))],
        [pltpu.VMEM((2, 1024, GCOLS), BF), pltpu.VMEM((96, GCOLS), F32)],
        smem=1,
        mib=24,
    )
    got = swap(send, dc=1)
    up_got = swap(up_send, dc=1)
    slab = (4, 24, COLS)
    own, *parts = call(
        core_sum_kernel, [keep, got], [shape(slab, F32)] + [shape(slab)] * 3
    )
    up_own, up_part = call(
        up_core_kernel, [up_keep, up_got], [shape((24, GCOLS), F32), shape((24, GCOLS))]
    )
    parts = [swap(parts[n], dx=n + 1) for n in range(3)]
    up_part = swap(up_part, dx=1)
    own, *parts = call(
        x_sum_kernel, [own, *parts], [shape(slab[1:], F32)] + [shape(slab[1:])] * 3
    )
    parts = [swap(parts[n], dy=n + 1) for n in range(3)]
    part = call(y_sum_kernel, [own, *parts, up_own, up_part], shape((24, BOTH)))
    for k in (1, 2, 4):
        part = call(z_sum_kernel, [part, swap(part, dz=k)], shape((24, BOTH)))
    over_y = call(
        stack_kernel, [part] + [swap(part, dy=k) for k in range(1, 4)], shape((4, 24, BOTH))
    )
    over_x = call(
        stack_kernel,
        [over_y] + [swap(over_y, dx=k) for k in range(1, 4)],
        shape((4, 4, 24, BOTH)),
    )
    other = swap(over_x, dc=1)
    grad_down, grad_up = call(
        final_kernel,
        [meta, over_x, other],
        [shape((96, WIDTH)), shape((96, CHANNELS))],
        smem=1,
    )
    return grad_down.reshape(3, RANK, WIDTH), grad_up.reshape(3, RANK, CHANNELS)


def solution(mesh):
    rows = P("dp", "seq", None)
    placed = (rows,) * 5 + (P(),) * 4 + (rows, P("dp", None))
    return jax.shard_map(shards, mesh=mesh, in_specs=placed, out_specs=(P(), P()), check_vma=False)
```

```python
import functools
import math

import jax
import jax.numpy as jnp
import numpy as np
from jax import lax
from jax.experimental import pallas as pl
from jax.experimental.pallas import tpu as pltpu
from jax.sharding import PartitionSpec as P

HEADS = 24
HEAD_DIM = 128
GRID_W = 16
FRAME_TOK = 128
FRAMES = 8
RANK = 32
WIDTH = 5120
CHANNELS = 3072
GROUPS = 8
LOCAL_HEADS = 3
NORM_EPS = 1e-06
SCALING = 1.0 / math.sqrt(HEAD_DIM)
BF = jnp.bfloat16
F32 = jnp.float32
HIDDEN = -1e30
BIG = 58
COLS = WIDTH // 8
GCOLS = CHANNELS // 8
BOTH = COLS + GCOLS

VMEM = pl.BlockSpec(memory_space=pltpu.VMEM)
SMEM = pl.BlockSpec(memory_space=pltpu.SMEM)


def params(mib):
    return pltpu.CompilerParams(vmem_limit_bytes=mib * 1024 * 1024)


def rope_tables():
    time_dims = HEAD_DIM - 4 * (HEAD_DIM // 6)
    space_dims = 2 * (HEAD_DIM // 6)
    tp, sp = time_dims // 2, space_dims // 2
    tok = np.arange(FRAMES * FRAME_TOK)
    frame, within = tok // FRAME_TOK, tok % FRAME_TOK
    row, col = within // GRID_W, within % GRID_W
    pairs = np.arange(HEAD_DIM) // 2
    in_time = pairs < tp
    in_rows = (pairs >= tp) & (pairs < tp + sp)
    offset = np.where(in_time, pairs, np.where(in_rows, pairs - tp, pairs - tp - sp))
    extent = np.where(in_time, time_dims, space_dims)
    rates = np.exp(-math.log(10000.0) * (2 * offset) / extent)
    pos = np.where(
        in_time[None], frame[:, None], np.where(in_rows[None], row[:, None], col[:, None])
    )
    angle = pos * rates[None]
    even = (np.arange(HEAD_DIM) % 2 == 0)[None]
    sine = np.sin(angle)
    table = np.stack([np.cos(angle), np.where(even, -sine, 0.0), np.where(even, 0.0, sine)], 0)
    table = table.reshape(3, FRAMES, FRAME_TOK, HEAD_DIM).transpose(1, 0, 2, 3)
    return table.astype(np.float32)


def turn(z, table, frame, sign):
    after = pltpu.roll(z, HEAD_DIM - 1, 1) * table[frame, 1]
    before = pltpu.roll(z, 1, 1) * table[frame, 2]
    mixed = after + before
    base = z * table[frame, 0]
    return base + mixed if sign > 0 else base - mixed


def nt(a, b, **kw):
    return lax.dot_general(
        a, b, (((1,), (1,)), ((), ())), preferred_element_type=F32, **kw
    )


def nn(a, b):
    return lax.dot_general(a, b, (((1,), (0,)), ((), ())), preferred_element_type=F32)


def rho_of(raw):
    total = jnp.zeros((FRAME_TOK, HEAD_DIM), F32)
    for n in range(HEADS):
        part = raw[:, n * HEAD_DIM : (n + 1) * HEAD_DIM].astype(F32)
        total = total + part * part
    mean = jnp.sum(total, axis=1, keepdims=True) * (1.0 / CHANNELS)
    return lax.rsqrt(mean + NORM_EPS)


def pack_kernel(heads, meta, query, key, value, cot, mask, gains, table, *refs):
    s = meta[0]
    ups, downs, tokens, outs, local = refs if len(refs) > 1 else (None, None, None, *refs, None)
    keep = jnp.broadcast_to(mask[...].astype(F32), (FRAME_TOK, FRAME_TOK)).T > 0.0
    rhos = [rho_of(raw) for raw in (query, key)]
    for k in range(GROUPS):
        for i, h in enumerate(heads):
            head = k * LOCAL_HEADS + h
            at = slice(head * HEAD_DIM, (head + 1) * HEAD_DIM)
            for n, raw in ((0, query), (1, key)):
                normed = raw[:, at].astype(F32) * rhos[n]
                outs[k, 4 * i + n] = turn(normed * gains[n, head], table, s, 1).astype(BF)
            outs[k, 4 * i + 2] = value[:, at]
            outs[k, 4 * i + 3] = jnp.where(keep, cot[:, at].astype(F32), 0.0).astype(BF)
    if ups is None:
        return
    rows = []
    for n, raw in ((0, query), (1, key)):
        rows.append(jnp.broadcast_to(rhos[n], (FRAME_TOK, FRAME_TOK)).T[0:8])
        carried = jnp.zeros((RANK, FRAME_TOK), F32)
        for head in range(HEADS):
            at = slice(head * HEAD_DIM, (head + 1) * HEAD_DIM)
            normed = (raw[:, at].astype(F32) * rhos[n]).astype(BF)
            carried = carried + nt(ups[n, :, at], normed)
        local[n * RANK : (n + 1) * RANK, :] = carried
        local[64 + 8 * n : 72 + 8 * n, :] = rows[n]
    down = nt(downs[...], tokens[...])
    at_row = lax.broadcasted_iota(jnp.int32, (RANK, FRAME_TOK), 0)
    extra = jnp.zeros((RANK, FRAME_TOK), F32)
    for n in range(2):
        wide = jnp.concatenate([rows[n]] * 4, 0)
        high = wide.astype(BF).astype(F32)
        extra = jnp.where(at_row == 2 * n, high, extra)
        extra = jnp.where(at_row == 2 * n + 1, wide - high, extra)
    aux = jnp.concatenate([down, extra], 0).astype(BF)
    for k in range(GROUPS):
        outs[k, 4] = aux


def attend_kernel(h, last, *refs):
    meta, blocks = refs[0], refs[1]
    packs, gains, table, ups = refs[2:6]
    pos = 6
    before = None
    if h > 0:
        before = refs[pos]
        pos += 1
    wide_out = refs[pos]
    pos += 1
    summed = refs[pos]
    pos += 1
    if last:
        mean_out, mix = refs[pos : pos + 2]
        pos += 2
    q_s, k_s, kt_s, v_s, g_s, sc, dp, pb, db, dk_acc, dv_acc, dq_s, sums = refs[pos:]
    s = meta[0]
    head = s * LOCAL_HEADS + h
    for k in range(GROUPS):
        at = slice(k * FRAME_TOK, (k + 1) * FRAME_TOK)
        q_s[at, :] = packs[k, 0]
        key = packs[k, 1]
        k_s[at, :] = key
        kt_s[:, at] = key.astype(F32).T.astype(BF)
        v_s[at, :] = packs[k, 2]
        g_s[at, :] = packs[k, 3]
    owner = [blocks[k] for k in range(GROUPS)]
    factor = SCALING * math.log2(math.e)
    lane = lax.broadcasted_iota(jnp.int32, (1, 256), 1)
    for t in range(4):
        b = t % 2
        tile = slice(t * 256, (t + 1) * 256)
        q_t, g_t = q_s[tile, :], g_s[tile, :]
        limit = jnp.where(lane < FRAME_TOK, owner[2 * t], owner[2 * t + 1])
        top = jnp.full((8, 256), 2.0 * HIDDEN, F32)
        for j in range(GROUPS):
            at = slice(j * FRAME_TOK, (j + 1) * FRAME_TOK)
            bias = jnp.where(owner[j] <= limit, 0.0, HIDDEN)
            part = nt(k_s[at, :], q_t) + bias
            sc[b, at, :] = part
            dp[b, at, :] = nt(v_s[at, :], g_t)
            top = jnp.maximum(top, jnp.max(part.reshape(16, 8, 256), axis=0))
        top = jnp.max(top, axis=0, keepdims=True)
        total = jnp.zeros((8, 256), F32)
        cross = jnp.zeros((8, 256), F32)
        for j in range(GROUPS):
            at = slice(j * FRAME_TOK, (j + 1) * FRAME_TOK)
            weight = jnp.exp2((sc[b, at, :] - top) * factor)
            sc[b, at, :] = weight
            total = total + jnp.sum(weight.reshape(16, 8, 256), axis=0)
            cross = cross + jnp.sum((weight * dp[b, at, :]).reshape(16, 8, 256), axis=0)
        inverse = 1.0 / jnp.sum(total, axis=0, keepdims=True)
        delta = jnp.sum(cross, axis=0, keepdims=True) * inverse
        for j in range(GROUPS):
            at = slice(j * FRAME_TOK, (j + 1) * FRAME_TOK)
            prob = sc[b, at, :] * inverse
            pb[b, at, :] = prob.astype(BF)
            db[b, at, :] = (prob * (dp[b, at, :] - delta)).astype(BF)
        dv, dk = nn(pb[b], g_t), nn(db[b], q_t)
        if t == 0:
            dv_acc[...] = dv
            dk_acc[...] = dk
        else:
            dv_acc[...] += dv
            dk_acc[...] += dk
        dq_s[tile, :] = nn(kt_s[...], db[b]).T
    up_at = pl.ds(pl.multiple_of(head * HEAD_DIM, HEAD_DIM), HEAD_DIM)
    ones = jnp.ones((8, HEAD_DIM), F32)
    for k in range(GROUPS):
        at = slice(k * FRAME_TOK, (k + 1) * FRAME_TOK)
        rows, means = [], []
        for n, (acc, rot) in enumerate(((dq_s, q_s), (dk_acc, k_s))):
            grad = (acc[at, :] * SCALING).astype(BF).astype(F32)
            wide = (gains[n, head] * turn(grad, table, k, -1)).astype(BF)
            wide_out[n, at, :] = wide
            rows.append(nt(ups[n, :, up_at], wide))
            means.append(nt(ones, grad * rot[at, :].astype(F32), precision=lax.Precision.HIGHEST))
        value = dv_acc[at, :].astype(BF)
        wide_out[2, at, :] = value
        rows.append(nt(ups[2, :, up_at], value))
        part = jnp.concatenate(rows + means, 0)
        if before is not None:
            part = part + before[k]
        if last:
            sums[k] = part
        else:
            summed[k] = part
    if not last:
        return
    at_row = lax.broadcasted_iota(jnp.int32, (8, FRAME_TOK), 0)
    for n in range(2):
        gathered = jnp.zeros((8, FRAME_TOK), F32)
        for k in range(GROUPS):
            gathered = jnp.where(at_row == k, sums[jnp.bitwise_xor(s, k), 96 + 8 * n : 104 + 8 * n], gathered)
        mean_out[8 * n : 8 * n + 8, :] = gathered
    for i, k in enumerate((0, 1, 6, 7)):
        summed[i] = sums[jnp.bitwise_xor(s, k), 0:96]
        away = jnp.bitwise_xor(s, k ^ 2)
        mix[i * 96 : (i + 1) * 96, :] = sums[away, 0:96].astype(BF)
    mix[384:416, :] = halves(mean_out[...])


def halves(means):
    high = means.astype(BF).astype(F32)
    return jnp.concatenate([high, means - high], 0).astype(BF)


def add_means(means, got, first, bit):
    tail = got[first : first + 32, :].astype(F32)
    tail = tail[0:16] + tail[16:32]
    moved = [tail[8 * n + (p ^ bit) : 8 * n + (p ^ bit) + 1] for n in range(2) for p in range(8)]
    return means[...] + jnp.concatenate(moved, 0)


def mix_kernel(count, bit, keep, means, got, keep_out, means_out, send):
    total = add_means(means, got, 96 * count, bit)
    means_out[...] = total
    half = count // 2
    for i in range(count):
        value = keep[i] + got[i * 96 : (i + 1) * 96, :].astype(F32)
        if i < half:
            keep_out[i] = value
        else:
            send[(i - half) * 96 : (i - half + 1) * 96, :] = value.astype(BF)
    send[half * 96 : half * 96 + 32, :] = halves(total)


def owner_kernel(meta, kept, means, got, local, tokens, keep, send, means_out, rows_s, mixed_s):
    y, x, c = meta[1], meta[2], meta[3]
    total = kept[0] + got[0:96, :].astype(F32)
    full = add_means(means, got, 96, 1)
    means_out[...] = full
    for n in range(2):
        at = slice(n * RANK, (n + 1) * RANK)
        rho = local[64 + 8 * n : 65 + 8 * n, :]
        mean = full[8 * n : 8 * n + 1] * (1.0 / CHANNELS)
        rows_s[at, :] = rho * (total[at] - mean * local[at, :])
    rows_s[64:96, :] = total[64:96]
    for k in range(4):
        first = pl.multiple_of(jnp.bitwise_xor(y, k) * 24, 8)
        mixed_s[k * 24 : (k + 1) * 24, :] = rows_s[pl.ds(first, 24), :]
    mixed = mixed_s[...].astype(BF)
    for a in range(2):
        for b in range(4):
            block = jnp.bitwise_xor(c, a) * 4 + jnp.bitwise_xor(x, b)
            at = pl.ds(pl.multiple_of(block * COLS, HEAD_DIM), COLS)
            out = nn(mixed, tokens[:, at])
            for k in range(4):
                part = out[k * 24 : (k + 1) * 24]
                if a == 0:
                    keep[b, k] = part
                else:
                    send[b, k] = part.astype(BF)


def up_kernel(meta, means, *refs):
    firsts, lasts, wides = refs[0], refs[1], refs[2:5]
    gains, table, keep, send, turned_s, up_s = refs[5:]
    s, x, c = meta[0], meta[2], meta[3]
    xl = jnp.bitwise_and(x, 1)
    for h in range(LOCAL_HEADS):
        lanes = slice(h * HEAD_DIM, (h + 1) * HEAD_DIM)
        for k in range(GROUPS):
            at = slice(k * FRAME_TOK, (k + 1) * FRAME_TOK)
            for n in range(2):
                rot = (lasts if h == 2 else firsts)[k, 4 * (h % 2) + n].astype(F32)
                turned_s[n, at, lanes] = turn(rot, table, k, -1).astype(BF)
    for n in range(3):
        plain_hi, plain_lo, along = [], [], []
        for p in range(GROUPS):
            aux = lasts[p, 4].astype(F32)
            down = aux[n * RANK : (n + 1) * RANK]
            if n == 2:
                plain_hi.append(down.astype(BF))
                continue
            rho = aux[96 + 2 * n : 97 + 2 * n] + aux[97 + 2 * n : 98 + 2 * n]
            mean = means[pl.ds(8 * n + jnp.bitwise_xor(s, p), 1), :]
            scaled = down * rho
            high = scaled.astype(BF)
            plain_hi.append(high)
            plain_lo.append((scaled - high.astype(F32)).astype(BF))
            along.append((scaled * (mean * (1.0 / CHANNELS))).astype(BF))
        high = jnp.concatenate(plain_hi, 1)
        for h in range(LOCAL_HEADS):
            lanes = slice(h * HEAD_DIM, (h + 1) * HEAD_DIM)
            out = nn(high, wides[h][n])
            if n < 2:
                gain = gains[n, s * LOCAL_HEADS + h]
                out = out + nn(jnp.concatenate(plain_lo, 1), wides[h][n])
                out = out - nn(jnp.concatenate(along, 1), turned_s[n, :, lanes]) / gain
            up_s[n * RANK : (n + 1) * RANK, lanes] = out
    for a in range(2):
        for b in range(2):
            block = jnp.bitwise_xor(c, a) * 2 + jnp.bitwise_xor(xl, b)
            part = up_s[pl.ds(pl.multiple_of(block * 24, 8), 24), :]
            if a == 0:
                keep[b] = part
            else:
                send[b] = part.astype(BF)


def core_sum_kernel(keep, got, own, *sends):
    for b in range(4):
        value = keep[b] + got[b].astype(F32)
        if b == 0:
            own[...] = value
        else:
            sends[b - 1][...] = value.astype(BF)


def up_core_kernel(keep, got, own, send):
    own[...] = keep[0] + got[0].astype(F32)
    send[...] = (keep[1] + got[1].astype(F32)).astype(BF)


def x_sum_kernel(own, r1, r2, r3, keep, *sends):
    for b in range(4):
        value = (own[b] + r1[b].astype(F32)) + (r2[b].astype(F32) + r3[b].astype(F32))
        if b == 0:
            keep[...] = value
        else:
            sends[b - 1][...] = value.astype(BF)


def y_sum_kernel(own, r1, r2, r3, up_own, up_got, out):
    value = (own[...] + r1[...].astype(F32)) + (r2[...].astype(F32) + r3[...].astype(F32))
    out[:, :COLS] = value.astype(BF)
    out[:, COLS:] = (up_own[...] + up_got[...].astype(F32)).astype(BF)


def z_sum_kernel(own, got, out):
    out[...] = (own[...].astype(F32) + got[...].astype(F32)).astype(BF)


def stack_kernel(*refs):
    out = refs[-1]
    for n, ref in enumerate(refs[:-1]):
        out[n] = ref[...]


def final_kernel(meta, own, got, down_out, up_out):
    y, x, c = meta[1], meta[2], meta[3]

    def piece(ca, xa, ya, lanes):
        xr, yr = jnp.bitwise_xor(x, xa), jnp.bitwise_xor(y, ya)
        mine = own[xr, yr, :, lanes].astype(F32)
        other = got[xr, yr, :, lanes].astype(F32)
        return jnp.where(c == ca, mine, other)

    for ca in range(2):
        for xa in range(4):
            block = [piece(ca, xa, ya, slice(0, COLS)) for ya in range(4)]
            first = (ca * 4 + xa) * COLS
            down_out[:, first : first + COLS] = jnp.concatenate(block, 0).astype(BF)
    for ya in range(4):
        for xh in range(2):
            block = [
                piece(ca, xh * 2 + xl, ya, slice(COLS, BOTH)) for ca in range(2) for xl in range(2)
            ]
            first = (ya * 2 + xh) * GCOLS
            up_out[:, first : first + GCOLS] = jnp.concatenate(block, 0).astype(BF)


def shape(dims, dtype=BF):
    return jax.ShapeDtypeStruct(dims, dtype)


def call(kernel, ins, outs, scratch=(), smem=0, mib=16):
    single = not isinstance(outs, (list, tuple))
    return pl.pallas_call(
        kernel,
        out_shape=outs,
        in_specs=[SMEM] * smem + [VMEM] * (len(ins) - smem),
        out_specs=VMEM if single else [VMEM] * len(outs),
        scratch_shapes=list(scratch),
        compiler_params=params(mib),
    )(*ins)


def place(x, y, z, c):
    return (y * 2 + x // 2) * 32 + z * 4 + (x % 2) * 2 + c


def swap(array, dx=0, dy=0, dz=0, dc=0):
    pairs = [
        (place(x, y, z, c), place(x ^ dx, y ^ dy, z ^ dz, c ^ dc))
        for x in range(4)
        for y in range(4)
        for z in range(8)
        for c in range(2)
    ]
    return lax.ppermute(array, ("seq", "dp"), pairs)


def seq_swap(array, k):
    return swap(array, dx=2 * (k & 1), dy=k >> 1)


def whole(array):
    zeros = (0,) * len(array.shape)
    return pl.BlockSpec(array.shape, lambda i: zeros)


def pack(ins, heads, outs):
    return pl.pallas_call(
        functools.partial(pack_kernel, heads),
        grid=(1,),
        out_shape=outs,
        in_specs=[SMEM] + [whole(a) for a in ins[1:]],
        out_specs=[whole(a) for a in outs],
        compiler_params=params(BIG),
    )(*ins)


def attend(h, meta, blocks, packs, gains, table, ups, before):
    last = h == LOCAL_HEADS - 1
    seq_len = FRAMES * FRAME_TOK
    ins = [meta, blocks, packs, gains, table, ups]
    piece = pl.BlockSpec((GROUPS, 4, FRAME_TOK, HEAD_DIM), lambda i: (0, h % 2, 0, 0))
    specs = [SMEM] * 2 + [piece] + [whole(a) for a in ins[3:]]
    if before is not None:
        ins.append(before)
        specs.append(whole(before))
    outs = [shape((3, seq_len, HEAD_DIM))]
    if last:
        outs += [shape((4, 96, FRAME_TOK), F32), shape((16, FRAME_TOK), F32), shape((416, FRAME_TOK))]
    else:
        outs += [shape((GROUPS, 112, FRAME_TOK), F32)]
    rows = (seq_len, HEAD_DIM)
    return pl.pallas_call(
        functools.partial(attend_kernel, h, last),
        grid=(1,),
        out_shape=outs,
        in_specs=specs,
        out_specs=[whole(a) for a in outs],
        scratch_shapes=[
            pltpu.VMEM(rows, BF),
            pltpu.VMEM(rows, BF),
            pltpu.VMEM((HEAD_DIM, seq_len), BF),
            pltpu.VMEM(rows, BF),
            pltpu.VMEM(rows, BF),
            pltpu.VMEM((2, seq_len, 256), F32),
            pltpu.VMEM((2, seq_len, 256), F32),
            pltpu.VMEM((2, seq_len, 256), BF),
            pltpu.VMEM((2, seq_len, 256), BF),
            pltpu.VMEM(rows, F32),
            pltpu.VMEM(rows, F32),
            pltpu.VMEM(rows, F32),
            pltpu.VMEM((GROUPS, 112, FRAME_TOK), F32),
        ],
        compiler_params=params(BIG),
        cost_estimate=pl.CostEstimate(
            flops=10 * seq_len * seq_len * HEAD_DIM, bytes_accessed=4 << 20, transcendentals=seq_len * seq_len
        ),
    )(*ins)


def shards(
    input_tokens,
    query_unnormed,
    key_unnormed,
    value_projected,
    cotangent,
    query_norm_gain,
    key_norm_gain,
    adapter_down_maps,
    adapter_up_maps,
    generated_mask,
    block_begin_flags,
):
    s, d = lax.axis_index("seq"), lax.axis_index("dp")
    y, x, c = s // 2, (s % 2) * 2 + (d // 2) % 2, d % 2
    meta = jnp.stack([s, y, x, c]).astype(jnp.int32)
    blocks = jnp.cumsum(block_begin_flags[0]).astype(jnp.int32)
    table = jnp.asarray(rope_tables())
    gains = jnp.stack([query_norm_gain, key_norm_gain]).reshape(2, HEADS, 1, HEAD_DIM)
    tokens = input_tokens[0]
    downs = adapter_down_maps.reshape(96, WIDTH)

    raws = [query_unnormed[0], key_unnormed[0], value_projected[0], cotangent[0]]
    first = [meta, *raws, generated_mask[0], gains, table]
    (firsts,) = pack(first, (0, 1), [shape((GROUPS, 8, FRAME_TOK, HEAD_DIM))])
    lasts, local = pack(
        first + [adapter_up_maps, downs, tokens],
        (2,),
        [shape((GROUPS, 5, FRAME_TOK, HEAD_DIM)), shape((80, FRAME_TOK), F32)],
    )
    firsts = lax.all_to_all(firsts, "seq", 0, 0, tiled=True)
    lasts = lax.all_to_all(lasts, "seq", 0, 0, tiled=True)
    wides = []
    before = None
    for h in range(LOCAL_HEADS):
        wide, before, *rest = attend(
            h, meta, blocks, lasts if h == 2 else firsts, gains, table, adapter_up_maps, before
        )
        wides.append(wide)
    means, mix = rest
    kept = before
    for count, bit in ((4, 2), (2, 6)):
        half = count // 2
        kept, means, mix = call(
            functools.partial(mix_kernel, count, bit),
            [kept, means, seq_swap(mix, bit)],
            [
                shape((half, 96, FRAME_TOK), F32),
                shape((16, FRAME_TOK), F32),
                shape((half * 96 + 32, FRAME_TOK)),
            ],
        )
    mix = seq_swap(mix, 1)

    keep, send, means = call(
        owner_kernel,
        [meta, kept, means, mix, local, tokens],
        [shape((4, 4, 24, COLS), F32), shape((4, 4, 24, COLS)), shape((16, FRAME_TOK), F32)],
        [pltpu.VMEM((96, FRAME_TOK), F32), pltpu.VMEM((96, FRAME_TOK), F32)],
        smem=1,
    )
    up_keep, up_send = call(
        up_kernel,
        [meta, means, firsts, lasts, *wides, gains, table],
        [shape((2, 24, GCOLS), F32), shape((2, 24, GCOLS))],
        [pltpu.VMEM((2, 1024, GCOLS), BF), pltpu.VMEM((96, GCOLS), F32)],
        smem=1,
        mib=24,
    )
    got = swap(send, dc=1)
    up_got = swap(up_send, dc=1)
    slab = (4, 24, COLS)
    own, *parts = call(
        core_sum_kernel, [keep, got], [shape(slab, F32)] + [shape(slab)] * 3
    )
    up_own, up_part = call(
        up_core_kernel, [up_keep, up_got], [shape((24, GCOLS), F32), shape((24, GCOLS))]
    )
    parts = [swap(parts[n], dx=n + 1) for n in range(3)]
    up_part = swap(up_part, dx=1)
    own, *parts = call(
        x_sum_kernel, [own, *parts], [shape(slab[1:], F32)] + [shape(slab[1:])] * 3
    )
    parts = [swap(parts[n], dy=n + 1) for n in range(3)]
    part = call(y_sum_kernel, [own, *parts, up_own, up_part], shape((24, BOTH)))
    for k in (1, 2, 6):
        part = call(z_sum_kernel, [part, swap(part, dz=k)], shape((24, BOTH)))
    over_y = call(
        stack_kernel, [part] + [swap(part, dy=k) for k in range(1, 4)], shape((4, 24, BOTH))
    )
    over_x = call(
        stack_kernel,
        [over_y] + [swap(over_y, dx=k) for k in range(1, 4)],
        shape((4, 4, 24, BOTH)),
    )
    other = swap(over_x, dc=1)
    grad_down, grad_up = call(
        final_kernel,
        [meta, over_x, other],
        [shape((96, WIDTH)), shape((96, CHANNELS))],
        smem=1,
    )
    return grad_down.reshape(3, RANK, WIDTH), grad_up.reshape(3, RANK, CHANNELS)


def solution(mesh):
    rows = P("dp", "seq", None)
    placed = (rows,) * 5 + (P(),) * 4 + (rows, P("dp", None))
    return jax.shard_map(shards, mesh=mesh, in_specs=placed, out_specs=(P(), P()), check_vma=False)
```

```python
import functools
import math

import jax
import jax.numpy as jnp
import numpy as np
from jax import lax
from jax.experimental import pallas as pl
from jax.experimental.pallas import tpu as pltpu
from jax.sharding import PartitionSpec as P

HEADS = 24
HEAD_DIM = 128
GRID_W = 16
FRAME_TOK = 128
FRAMES = 8
RANK = 32
WIDTH = 5120
CHANNELS = 3072
GROUPS = 8
LOCAL_HEADS = 3
NORM_EPS = 1e-06
SCALING = 1.0 / math.sqrt(HEAD_DIM)
BF = jnp.bfloat16
F32 = jnp.float32
HIDDEN = -1e30
BIG = 58
COLS = WIDTH // 8
GCOLS = CHANNELS // 8
BOTH = COLS + GCOLS

VMEM = pl.BlockSpec(memory_space=pltpu.VMEM)
SMEM = pl.BlockSpec(memory_space=pltpu.SMEM)


def params(mib):
    return pltpu.CompilerParams(vmem_limit_bytes=mib * 1024 * 1024)


def rope_tables():
    time_dims = HEAD_DIM - 4 * (HEAD_DIM // 6)
    space_dims = 2 * (HEAD_DIM // 6)
    tp, sp = time_dims // 2, space_dims // 2
    tok = np.arange(FRAMES * FRAME_TOK)
    frame, within = tok // FRAME_TOK, tok % FRAME_TOK
    row, col = within // GRID_W, within % GRID_W
    pairs = np.arange(HEAD_DIM) // 2
    in_time = pairs < tp
    in_rows = (pairs >= tp) & (pairs < tp + sp)
    offset = np.where(in_time, pairs, np.where(in_rows, pairs - tp, pairs - tp - sp))
    extent = np.where(in_time, time_dims, space_dims)
    rates = np.exp(-math.log(10000.0) * (2 * offset) / extent)
    pos = np.where(
        in_time[None], frame[:, None], np.where(in_rows[None], row[:, None], col[:, None])
    )
    angle = pos * rates[None]
    even = (np.arange(HEAD_DIM) % 2 == 0)[None]
    sine = np.sin(angle)
    table = np.stack([np.cos(angle), np.where(even, -sine, 0.0), np.where(even, 0.0, sine)], 0)
    table = table.reshape(3, FRAMES, FRAME_TOK, HEAD_DIM)
    by_frame = np.where(in_time[None, None], table[:, :, 0], 0.0).transpose(1, 0, 2)
    within = np.where(in_time[None, None], 0.0, table[:, 0])
    return by_frame.reshape(3 * FRAMES, HEAD_DIM).astype(np.float32), within.astype(np.float32)


def turn(z, by_frame, within, frame, sign):
    cosine, left, right = (
        within[n] + by_frame[pl.ds(3 * frame + n, 1), :] for n in range(3)
    )
    mixed = pltpu.roll(z, HEAD_DIM - 1, 1) * left + pltpu.roll(z, 1, 1) * right
    base = z * cosine
    return base + mixed if sign > 0 else base - mixed


def position():
    s, d = lax.axis_index("seq"), lax.axis_index("dp")
    x = lax.rem(s, 2) * 2 + lax.rem(lax.div(d, 2), 2)
    return s, lax.div(s, 2), x, lax.rem(d, 2)


def nt(a, b, **kw):
    return lax.dot_general(
        a, b, (((1,), (1,)), ((), ())), preferred_element_type=F32, **kw
    )


def nn(a, b):
    return lax.dot_general(a, b, (((1,), (0,)), ((), ())), preferred_element_type=F32)


def rho_of(raw):
    total = jnp.zeros((raw.shape[0], HEAD_DIM), F32)
    for n in range(HEADS):
        part = raw[:, n * HEAD_DIM : (n + 1) * HEAD_DIM].astype(F32)
        total = total + part * part
    mean = jnp.sum(total, axis=1, keepdims=True) * (1.0 / CHANNELS)
    return lax.rsqrt(mean + NORM_EPS)


def pack_kernel(heads, query, key, value, cot, mask, gain_q, gain_k, by_frame, within, *refs):
    s = lax.axis_index("seq")
    ups, downs, tokens, outs, local, keep_s = refs if len(refs) > 2 else (None,) * 3 + (refs[0], None, refs[1])
    count = query.shape[0]
    keep_s[...] = jnp.broadcast_to(mask[...].astype(F32), (FRAME_TOK, FRAME_TOK)).T
    keep = keep_s[pl.ds(pl.multiple_of(pl.program_id(0) * count, count), count), :] > 0.0
    rhos = [rho_of(raw) for raw in (query, key)]
    for k in range(GROUPS):
        for i, h in enumerate(heads):
            head = k * LOCAL_HEADS + h
            at = slice(head * HEAD_DIM, (head + 1) * HEAD_DIM)
            for n, (raw, gain) in enumerate(((query, gain_q), (key, gain_k))):
                normed = raw[:, at].astype(F32) * rhos[n] * gain[head : head + 1, :]
                outs[k, 4 * i + n] = turn(normed, by_frame, within, s, 1).astype(BF)
            outs[k, 4 * i + 2] = value[:, at]
            outs[k, 4 * i + 3] = jnp.where(keep, cot[:, at].astype(F32), 0.0).astype(BF)
    if ups is None:
        return
    rows = []
    for n, raw in ((0, query), (1, key)):
        rows.append(jnp.broadcast_to(rhos[n], (FRAME_TOK, FRAME_TOK)).T[0:8])
        carried = jnp.zeros((RANK, FRAME_TOK), F32)
        for head in range(HEADS):
            at = slice(head * HEAD_DIM, (head + 1) * HEAD_DIM)
            normed = (raw[:, at].astype(F32) * rhos[n]).astype(BF)
            carried = carried + nt(ups[n, :, at], normed)
        local[n * RANK : (n + 1) * RANK, :] = carried
        local[64 + 8 * n : 72 + 8 * n, :] = rows[n]
    down = nt(downs[...], tokens[...])
    at_row = lax.broadcasted_iota(jnp.int32, (RANK, FRAME_TOK), 0)
    extra = jnp.zeros((RANK, FRAME_TOK), F32)
    for n in range(2):
        wide = jnp.concatenate([rows[n]] * 4, 0)
        high = wide.astype(BF).astype(F32)
        extra = jnp.where(at_row == 2 * n, high, extra)
        extra = jnp.where(at_row == 2 * n + 1, wide - high, extra)
    aux = jnp.concatenate([down, extra], 0).astype(BF)
    for k in range(GROUPS):
        outs[k, 4] = aux


def attend_kernel(base, last, flags, packs, gain_q, gain_k, by_frame, within, ups, *refs):
    before = None
    if last:
        before, refs = refs[0], refs[1:]
    wide_out, summed = refs[:2]
    refs = refs[2:]
    if last:
        mean_out, *mix = refs[:4]
        refs = refs[4:]
    q_s, k_s, kt_s, v_s, g_s, sc, dp, pb, db, dk_acc, dv_acc, dq_s, prod_s, sums = refs
    s = lax.axis_index("seq")
    step = pl.program_id(0)
    head = s * LOCAL_HEADS + base + step
    owner = []
    for k in range(GROUPS):
        owner.append(flags[0, k] + (owner[-1] if k else 0))
        at = slice(k * FRAME_TOK, (k + 1) * FRAME_TOK)
        q_s[at, :] = packs[k, 0]
        key = packs[k, 1]
        k_s[at, :] = key
        kt_s[:, at] = key.astype(F32).T.astype(BF)
        v_s[at, :] = packs[k, 2]
        g_s[at, :] = packs[k, 3]
    factor = SCALING * math.log2(math.e)
    lane = lax.broadcasted_iota(jnp.int32, (1, 256), 1)
    for t in range(4):
        b = t % 2
        tile = slice(t * 256, (t + 1) * 256)
        q_t, g_t = q_s[tile, :], g_s[tile, :]
        limit = jnp.where(lane < FRAME_TOK, owner[2 * t], owner[2 * t + 1])
        bias = [jnp.where(owner[j] <= limit, 0.0, HIDDEN) for j in range(GROUPS)]
        sc[b] = nt(k_s[...], q_t)
        dp[b] = nt(v_s[...], g_t)
        top = jnp.full((8, 256), 2.0 * HIDDEN, F32)
        for j in range(GROUPS):
            part = sc[b, j * FRAME_TOK : (j + 1) * FRAME_TOK, :]
            top = jnp.maximum(top, jnp.max(part.reshape(16, 8, 256), axis=0) + bias[j])
        top = jnp.max(top, axis=0, keepdims=True)
        total = jnp.zeros((8, 256), F32)
        cross = jnp.zeros((8, 256), F32)
        for j in range(GROUPS):
            at = slice(j * FRAME_TOK, (j + 1) * FRAME_TOK)
            weight = jnp.exp2((sc[b, at, :] - (top - bias[j])) * factor)
            sc[b, at, :] = weight
            total = total + jnp.sum(weight.reshape(16, 8, 256), axis=0)
            cross = cross + jnp.sum((weight * dp[b, at, :]).reshape(16, 8, 256), axis=0)
        inverse = 1.0 / jnp.sum(total, axis=0, keepdims=True)
        delta = jnp.sum(cross, axis=0, keepdims=True) * inverse
        for j in range(GROUPS):
            at = slice(j * FRAME_TOK, (j + 1) * FRAME_TOK)
            prob = sc[b, at, :] * inverse
            pb[b, at, :] = prob.astype(BF)
            db[b, at, :] = (prob * (dp[b, at, :] - delta)).astype(BF)
        dv, dk = nn(pb[b], g_t), nn(db[b], q_t)
        if t == 0:
            dv_acc[...] = dv
            dk_acc[...] = dk
        else:
            dv_acc[...] += dv
            dk_acc[...] += dk
        dq_s[tile, :] = nn(kt_s[...], db[b]).T
    up_at = pl.ds(pl.multiple_of(head * HEAD_DIM, HEAD_DIM), HEAD_DIM)
    gains = [gain[pl.ds(head, 1), :] for gain in (gain_q, gain_k)]
    for k in range(GROUPS):
        at = slice(k * FRAME_TOK, (k + 1) * FRAME_TOK)
        for n, (acc, rot) in enumerate(((dq_s, q_s), (dk_acc, k_s))):
            grad = (acc[at, :] * SCALING).astype(BF).astype(F32)
            wide = gains[n] * turn(grad, by_frame, within, k, -1)
            wide_out[0, n, at, :] = wide.astype(BF)
            prod_s[n, at, :] = (grad * rot[at, :].astype(F32)).astype(BF)
        wide_out[0, 2, at, :] = dv_acc[at, :].astype(BF)
    ones = jnp.ones((16, HEAD_DIM), BF)
    parts = [nt(ups[n, :, up_at], wide_out[0, n]) for n in range(3)]
    parts += [nt(ones, prod_s[n])[0:8] for n in range(2)]
    full = jnp.concatenate(parts, 0)
    for k in range(GROUPS):
        part = full[:, k * FRAME_TOK : (k + 1) * FRAME_TOK]
        if last:
            sums[k] = part + before[k]
        else:
            summed[k] = part + jnp.where(step > 0, summed[k], 0.0)
    if not last:
        return
    at_row = lax.broadcasted_iota(jnp.int32, (8, FRAME_TOK), 0)
    for n in range(2):
        gathered = jnp.zeros((8, FRAME_TOK), F32)
        for k in range(GROUPS):
            row = sums[jnp.bitwise_xor(s, k), 96 + 8 * n : 104 + 8 * n]
            gathered = jnp.where(at_row == k, row, gathered)
        mean_out[8 * n : 8 * n + 8, :] = gathered
    tail = halves(mean_out[...])
    for b in range(2):
        summed[b] = sums[jnp.bitwise_xor(s, b), 0:96]
        for a in range(1, 4):
            away = jnp.bitwise_xor(s, 2 * a + b)
            mix[a - 1][b * 96 : (b + 1) * 96, :] = sums[away, 0:96].astype(BF)
    for a in range(1, 4):
        mix[a - 1][192:224, :] = tail


def halves(means):
    high = means.astype(BF).astype(F32)
    return jnp.concatenate([high, means - high], 0).astype(BF)


def add_means(got, first, bit):
    tail = got[first : first + 32, :].astype(F32)
    tail = tail[0:16] + tail[16:32]
    moved = [tail[8 * n + (p ^ bit) : 8 * n + (p ^ bit) + 1] for n in range(2) for p in range(8)]
    return jnp.concatenate(moved, 0)


def mix_kernel(keep, means, r1, r2, r3, keep_out, means_out, send):
    total = (means[...] + add_means(r1, 192, 2)) + (add_means(r2, 192, 4) + add_means(r3, 192, 6))
    means_out[...] = total
    for i in range(2):
        at = slice(i * 96, (i + 1) * 96)
        value = keep[i] + r1[at, :].astype(F32)
        value = value + (r2[at, :].astype(F32) + r3[at, :].astype(F32))
        if i == 0:
            keep_out[...] = value
        else:
            send[0:96, :] = value.astype(BF)
    send[96:128, :] = halves(total)


def owner_kernel(kept, means, got, local, tokens, keep, send, means_out, rows_s, mixed_s):
    _, y, x, c = position()
    total = kept[...] + got[0:96, :].astype(F32)
    full = means[...] + add_means(got, 96, 1)
    means_out[...] = full
    for n in range(2):
        at = slice(n * RANK, (n + 1) * RANK)
        rho = local[64 + 8 * n : 65 + 8 * n, :]
        mean = full[8 * n : 8 * n + 1] * (1.0 / CHANNELS)
        rows_s[at, :] = rho * (total[at] - mean * local[at, :])
    rows_s[64:96, :] = total[64:96]
    for k in range(4):
        first = pl.multiple_of(jnp.bitwise_xor(y, k) * 24, 8)
        mixed_s[k * 24 : (k + 1) * 24, :] = rows_s[pl.ds(first, 24), :]
    mixed = mixed_s[...].astype(BF)
    for a in range(2):
        for b in range(4):
            block = jnp.bitwise_xor(c, a) * 4 + jnp.bitwise_xor(x, b)
            at = pl.ds(pl.multiple_of(block * COLS, HEAD_DIM), COLS)
            out = nn(mixed, tokens[:, at])
            for k in range(4):
                part = out[k * 24 : (k + 1) * 24]
                if a == 0:
                    keep[b, k] = part
                else:
                    send[b, k] = part.astype(BF)


def up_kernel(means, firsts, lasts, wide01, wide2, *refs):
    gain_q, gain_k, by_frame, within, keep, send, turned_s, up_s = refs
    wides = [wide01.at[0], wide01.at[1], wide2.at[0]]
    s, _, x, c = position()
    xl = jnp.bitwise_and(x, 1)
    for h in range(LOCAL_HEADS):
        lanes = slice(h * HEAD_DIM, (h + 1) * HEAD_DIM)
        for k in range(GROUPS):
            at = slice(k * FRAME_TOK, (k + 1) * FRAME_TOK)
            for n in range(2):
                rot = (lasts if h == 2 else firsts)[k, 4 * (h % 2) + n].astype(F32)
                turned_s[n, at, lanes] = turn(rot, by_frame, within, k, -1).astype(BF)
    for n in range(3):
        plain_hi, plain_lo, along = [], [], []
        for p in range(GROUPS):
            aux = lasts[p, 4].astype(F32)
            down = aux[n * RANK : (n + 1) * RANK]
            if n == 2:
                plain_hi.append(down.astype(BF))
                continue
            rho = aux[96 + 2 * n : 97 + 2 * n] + aux[97 + 2 * n : 98 + 2 * n]
            mean = means[pl.ds(8 * n + jnp.bitwise_xor(s, p), 1), :]
            scaled = down * rho
            high = scaled.astype(BF)
            plain_hi.append(high)
            plain_lo.append((scaled - high.astype(F32)).astype(BF))
            along.append((scaled * (mean * (1.0 / CHANNELS))).astype(BF))
        high = jnp.concatenate(plain_hi, 1)
        for h in range(LOCAL_HEADS):
            lanes = slice(h * HEAD_DIM, (h + 1) * HEAD_DIM)
            out = nn(high, wides[h][n])
            if n < 2:
                gain = (gain_q, gain_k)[n][pl.ds(s * LOCAL_HEADS + h, 1), :]
                out = out + nn(jnp.concatenate(plain_lo, 1), wides[h][n])
                out = out - nn(jnp.concatenate(along, 1), turned_s[n, :, lanes]) / gain
            up_s[n * RANK : (n + 1) * RANK, lanes] = out
    for a in range(2):
        for b in range(2):
            block = jnp.bitwise_xor(c, a) * 2 + jnp.bitwise_xor(xl, b)
            part = up_s[pl.ds(pl.multiple_of(block * 24, 8), 24), :]
            if a == 0:
                keep[b] = part
            else:
                send[b] = part.astype(BF)


def core_sum_kernel(keep, got, own, *sends):
    for b in range(4):
        value = keep[b] + got[b].astype(F32)
        if b == 0:
            own[...] = value
        else:
            sends[b - 1][...] = value.astype(BF)


def up_core_kernel(keep, got, own, send):
    own[...] = keep[0] + got[0].astype(F32)
    send[...] = (keep[1] + got[1].astype(F32)).astype(BF)


def x_sum_kernel(own, r1, r2, r3, keep, *sends):
    for b in range(4):
        value = (own[b] + r1[b].astype(F32)) + (r2[b].astype(F32) + r3[b].astype(F32))
        if b == 0:
            keep[...] = value
        else:
            sends[b - 1][...] = value.astype(BF)


def y_sum_kernel(own, r1, r2, r3, up_own, up_got, out):
    value = (own[...] + r1[...].astype(F32)) + (r2[...].astype(F32) + r3[...].astype(F32))
    out[:, :COLS] = value.astype(BF)
    out[:, COLS:] = (up_own[...] + up_got[...].astype(F32)).astype(BF)


def z_four_kernel(own, r1, r2, r3, out):
    value = (own[...].astype(F32) + r1[...].astype(F32)) + (r2[...].astype(F32) + r3[...].astype(F32))
    out[...] = value.astype(BF)


def z_sum_kernel(own, got, out):
    out[...] = (own[...].astype(F32) + got[...].astype(F32)).astype(BF)


def stack_kernel(*refs):
    out = refs[-1]
    for n, ref in enumerate(refs[:-1]):
        out[n] = ref[...]


def final_kernel(own, got, down_out, up_out):
    _, y, x, c = position()

    def piece(ca, xa, ya, lanes):
        xr, yr = jnp.bitwise_xor(x, xa), jnp.bitwise_xor(y, ya)
        mine = own[xr, yr, :, lanes].astype(F32)
        other = got[xr, yr, :, lanes].astype(F32)
        return jnp.where(c == ca, mine, other)

    for ca in range(2):
        for xa in range(4):
            block = [piece(ca, xa, ya, slice(0, COLS)) for ya in range(4)]
            first = (ca * 4 + xa) * COLS
            down_out[:, first : first + COLS] = jnp.concatenate(block, 0).astype(BF)
    for ya in range(4):
        for xh in range(2):
            block = [
                piece(ca, xh * 2 + xl, ya, slice(COLS, BOTH)) for ca in range(2) for xl in range(2)
            ]
            first = (ya * 2 + xh) * GCOLS
            up_out[:, first : first + GCOLS] = jnp.concatenate(block, 0).astype(BF)


def shape(dims, dtype=BF):
    return jax.ShapeDtypeStruct(dims, dtype)


def call(kernel, ins, outs, scratch=(), smem=0, mib=16):
    single = not isinstance(outs, (list, tuple))
    return pl.pallas_call(
        kernel,
        out_shape=outs,
        in_specs=[SMEM] * smem + [VMEM] * (len(ins) - smem),
        out_specs=VMEM if single else [VMEM] * len(outs),
        scratch_shapes=list(scratch),
        compiler_params=params(mib),
    )(*ins)


def place(x, y, z, c):
    return (y * 2 + x // 2) * 32 + z * 4 + (x % 2) * 2 + c


def swap(array, dx=0, dy=0, dz=0, dc=0):
    pairs = [
        (place(x, y, z, c), place(x ^ dx, y ^ dy, z ^ dz, c ^ dc))
        for x in range(4)
        for y in range(4)
        for z in range(8)
        for c in range(2)
    ]
    return lax.ppermute(array, ("seq", "dp"), pairs)


def seq_swap(array, k):
    return swap(array, dx=2 * (k & 1), dy=k >> 1)


def whole(array):
    zeros = (0,) * len(array.shape)
    return pl.BlockSpec(array.shape, lambda i: zeros)


def pack(ins, heads, outs, steps):
    count = FRAME_TOK // steps
    specs = [pl.BlockSpec((count, CHANNELS), lambda i: (i, 0))] * 4 + [whole(a) for a in ins[4:]]
    specs[8] = pl.BlockSpec((3, count, HEAD_DIM), lambda i: (0, i, 0))
    slots = outs[0].shape[1]
    out_specs = [pl.BlockSpec((GROUPS, slots, count, HEAD_DIM), lambda i: (0, 0, i, 0))]
    return pl.pallas_call(
        functools.partial(pack_kernel, heads),
        grid=(steps,),
        out_shape=outs,
        in_specs=specs,
        out_specs=out_specs + [whole(a) for a in outs[1:]],
        scratch_shapes=[pltpu.VMEM((FRAME_TOK, FRAME_TOK), F32)],
        compiler_params=params(BIG),
    )(*ins)


def attend(base, heads, ins, before):
    last = before is not None
    seq_len = FRAMES * FRAME_TOK
    rows = (seq_len, HEAD_DIM)
    piece = pl.BlockSpec((GROUPS, 4, FRAME_TOK, HEAD_DIM), lambda i: (0, i, 0, 0))
    specs = [SMEM, piece] + [whole(a) for a in ins[2:]]
    outs = [shape((heads, 3, *rows))]
    out_specs = [pl.BlockSpec((1, 3, *rows), lambda i: (i, 0, 0, 0))]
    if last:
        ins = [*ins, before]
        specs.append(whole(before))
        extra = [shape((2, 96, FRAME_TOK), F32), shape((16, FRAME_TOK), F32)]
        extra += [shape((224, FRAME_TOK))] * 3
        out_specs += [VMEM] * 5
    else:
        extra = [shape((GROUPS, 112, FRAME_TOK), F32)]
        out_specs += [whole(a) for a in extra]
    return pl.pallas_call(
        functools.partial(attend_kernel, base, last),
        grid=(heads,),
        out_shape=outs + extra,
        in_specs=specs,
        out_specs=out_specs,
        scratch_shapes=[
            pltpu.VMEM(rows, BF),
            pltpu.VMEM(rows, BF),
            pltpu.VMEM((HEAD_DIM, seq_len), BF),
            pltpu.VMEM(rows, BF),
            pltpu.VMEM(rows, BF),
            pltpu.VMEM((2, seq_len, 256), F32),
            pltpu.VMEM((2, seq_len, 256), F32),
            pltpu.VMEM((2, seq_len, 256), BF),
            pltpu.VMEM((2, seq_len, 256), BF),
            pltpu.VMEM(rows, F32),
            pltpu.VMEM(rows, F32),
            pltpu.VMEM(rows, F32),
            pltpu.VMEM((2, *rows), BF),
            pltpu.VMEM((GROUPS, 112, FRAME_TOK), F32),
        ],
        compiler_params=params(BIG),
        cost_estimate=pl.CostEstimate(
            flops=10 * heads * seq_len * seq_len * HEAD_DIM,
            bytes_accessed=heads * (4 << 20),
            transcendentals=heads * seq_len * seq_len,
        ),
    )(*ins)


def shards(
    input_tokens,
    query_unnormed,
    key_unnormed,
    value_projected,
    cotangent,
    query_norm_gain,
    key_norm_gain,
    adapter_down_maps,
    adapter_up_maps,
    generated_mask,
    block_begin_flags,
):
    by_frame, within = (jnp.asarray(t) for t in rope_tables())
    gain_q = query_norm_gain.reshape(HEADS, HEAD_DIM)
    gain_k = key_norm_gain.reshape(HEADS, HEAD_DIM)
    norms = [gain_q, gain_k, by_frame, within]
    tokens = input_tokens[0]
    downs = adapter_down_maps.reshape(96, WIDTH)

    raws = [query_unnormed[0], key_unnormed[0], value_projected[0], cotangent[0]]
    first = [*raws, generated_mask[0], *norms]
    (firsts,) = pack(first, (0, 1), [shape((GROUPS, 8, FRAME_TOK, HEAD_DIM))], 4)
    lasts, local = pack(
        first + [adapter_up_maps, downs, tokens],
        (2,),
        [shape((GROUPS, 5, FRAME_TOK, HEAD_DIM)), shape((80, FRAME_TOK), F32)],
        1,
    )
    firsts = lax.all_to_all(firsts, "seq", 0, 0, tiled=True)
    lasts = lax.all_to_all(lasts, "seq", 0, 0, tiled=True)
    shared = [*norms, adapter_up_maps]
    wide01, before = attend(0, 2, [block_begin_flags, firsts, *shared], None)
    wide2, kept, means, *mix = attend(2, 1, [block_begin_flags, lasts, *shared], before)
    mix = [swap(mix[a - 1], dy=a) for a in range(1, 4)]
    kept, means, mix = call(
        mix_kernel,
        [kept, means, *mix],
        [shape((96, FRAME_TOK), F32), shape((16, FRAME_TOK), F32), shape((128, FRAME_TOK))],
    )
    mix = seq_swap(mix, 1)

    keep, send, means = call(
        owner_kernel,
        [kept, means, mix, local, tokens],
        [shape((4, 4, 24, COLS), F32), shape((4, 4, 24, COLS)), shape((16, FRAME_TOK), F32)],
        [pltpu.VMEM((96, FRAME_TOK), F32), pltpu.VMEM((96, FRAME_TOK), F32)],
    )
    up_keep, up_send = call(
        up_kernel,
        [means, firsts, lasts, wide01, wide2, *norms],
        [shape((2, 24, GCOLS), F32), shape((2, 24, GCOLS))],
        [pltpu.VMEM((2, 1024, GCOLS), BF), pltpu.VMEM((96, GCOLS), F32)],
        mib=24,
    )
    got = swap(send, dc=1)
    up_got = swap(up_send, dc=1)
    slab = (4, 24, COLS)
    own, *parts = call(
        core_sum_kernel, [keep, got], [shape(slab, F32)] + [shape(slab)] * 3
    )
    up_own, up_part = call(
        up_core_kernel, [up_keep, up_got], [shape((24, GCOLS), F32), shape((24, GCOLS))]
    )
    parts = [swap(parts[n], dx=n + 1) for n in range(3)]
    up_part = swap(up_part, dx=1)
    own, *parts = call(
        x_sum_kernel, [own, *parts], [shape(slab[1:], F32)] + [shape(slab[1:])] * 3
    )
    parts = [swap(parts[n], dy=n + 1) for n in range(3)]
    part = call(y_sum_kernel, [own, *parts, up_own, up_part], shape((24, BOTH)))
    four = [swap(part, dz=k) for k in range(1, 4)]
    part = call(z_four_kernel, [part, *four], shape((24, BOTH)))
    part = call(z_sum_kernel, [part, swap(part, dz=7)], shape((24, BOTH)))
    over_y = call(
        stack_kernel, [part] + [swap(part, dy=k) for k in range(1, 4)], shape((4, 24, BOTH))
    )
    over_x = call(
        stack_kernel,
        [over_y] + [swap(over_y, dx=k) for k in range(1, 4)],
        shape((4, 4, 24, BOTH)),
    )
    other = swap(over_x, dc=1)
    grad_down, grad_up = call(
        final_kernel,
        [over_x, other],
        [shape((96, WIDTH)), shape((96, CHANNELS))],
    )
    return grad_down.reshape(3, RANK, WIDTH), grad_up.reshape(3, RANK, CHANNELS)


def solution(mesh):
    rows = P("dp", "seq", None)
    placed = (rows,) * 5 + (P(),) * 4 + (rows, P("dp", None))
    return jax.shard_map(shards, mesh=mesh, in_specs=placed, out_specs=(P(), P()), check_vma=False)
```

```python
import functools
import math

import jax
import jax.numpy as jnp
import numpy as np
from jax import lax
from jax.experimental import pallas as pl
from jax.experimental.pallas import tpu as pltpu
from jax.sharding import PartitionSpec as P

HEADS = 24
HEAD_DIM = 128
GRID_W = 16
FRAME_TOK = 128
FRAMES = 8
RANK = 32
WIDTH = 5120
CHANNELS = 3072
GROUPS = 8
LOCAL_HEADS = 3
NORM_EPS = 1e-06
SCALING = 1.0 / math.sqrt(HEAD_DIM)
BF = jnp.bfloat16
F32 = jnp.float32
HIDDEN = -1e30
BIG = 58
HELD = FRAMES * 112
COLS = WIDTH // 8
GCOLS = CHANNELS // 8
BOTH = COLS + GCOLS

VMEM = pl.BlockSpec(memory_space=pltpu.VMEM)
SMEM = pl.BlockSpec(memory_space=pltpu.SMEM)


def params(mib):
    return pltpu.CompilerParams(vmem_limit_bytes=mib * 1024 * 1024)


def rope_tables():
    time_dims = HEAD_DIM - 4 * (HEAD_DIM // 6)
    space_dims = 2 * (HEAD_DIM // 6)
    tp, sp = time_dims // 2, space_dims // 2
    tok = np.arange(FRAMES * FRAME_TOK)
    frame, within = tok // FRAME_TOK, tok % FRAME_TOK
    row, col = within // GRID_W, within % GRID_W
    pairs = np.arange(HEAD_DIM) // 2
    in_time = pairs < tp
    in_rows = (pairs >= tp) & (pairs < tp + sp)
    offset = np.where(in_time, pairs, np.where(in_rows, pairs - tp, pairs - tp - sp))
    extent = np.where(in_time, time_dims, space_dims)
    rates = np.exp(-math.log(10000.0) * (2 * offset) / extent)
    pos = np.where(
        in_time[None], frame[:, None], np.where(in_rows[None], row[:, None], col[:, None])
    )
    angle = pos * rates[None]
    even = (np.arange(HEAD_DIM) % 2 == 0)[None]
    sine = np.sin(angle)
    table = np.stack([np.cos(angle), np.where(even, -sine, 0.0), np.where(even, 0.0, sine)], 0)
    table = table.reshape(3, FRAMES, FRAME_TOK, HEAD_DIM)
    by_frame = np.where(in_time[None, None], table[:, :, 0], 0.0).transpose(1, 0, 2)
    within = np.where(in_time[None, None], 0.0, table[:, 0])
    return by_frame.reshape(3 * FRAMES, HEAD_DIM).astype(np.float32), within.astype(np.float32)


def angles(by_frame, within, frame):
    return [within[n] + by_frame[pl.ds(3 * frame + n, 1), :] for n in range(3)]


def turn(z, angle, sign):
    cosine, left, right = angle
    mixed = pltpu.roll(z, HEAD_DIM - 1, 1) * left + pltpu.roll(z, 1, 1) * right
    base = z * cosine
    return base + mixed if sign > 0 else base - mixed


def position():
    s, d = lax.axis_index("seq"), lax.axis_index("dp")
    x = lax.rem(s, 2) * 2 + lax.rem(lax.div(d, 2), 2)
    return s, lax.div(s, 2), x, lax.rem(d, 2)


def nt(a, b, **kw):
    return lax.dot_general(
        a, b, (((1,), (1,)), ((), ())), preferred_element_type=F32, **kw
    )


def nn(a, b):
    return lax.dot_general(a, b, (((1,), (0,)), ((), ())), preferred_element_type=F32)


def rho_of(raw):
    total = jnp.zeros((raw.shape[0], HEAD_DIM), F32)
    for n in range(HEADS):
        part = raw[:, n * HEAD_DIM : (n + 1) * HEAD_DIM].astype(F32)
        total = total + part * part
    mean = jnp.sum(total, axis=1, keepdims=True) * (1.0 / CHANNELS)
    return lax.rsqrt(mean + NORM_EPS)


def pack_kernel(heads, query, key, value, cot, mask, gain_q, gain_k, by_frame, within, *refs):
    s = lax.axis_index("seq")
    ups, downs, tokens, outs, local, keep_s = refs if len(refs) > 2 else (None,) * 3 + (refs[0], None, refs[1])
    count = query.shape[0]
    keep_s[...] = jnp.broadcast_to(mask[...].astype(F32), (FRAME_TOK, FRAME_TOK)).T
    keep = keep_s[pl.ds(pl.multiple_of(pl.program_id(0) * count, count), count), :] > 0.0
    rhos = [rho_of(raw) for raw in (query, key)]
    angle = angles(by_frame, within, s)
    for k in range(GROUPS):
        for i, h in enumerate(heads):
            head = k * LOCAL_HEADS + h
            at = slice(head * HEAD_DIM, (head + 1) * HEAD_DIM)
            for n, (raw, gain) in enumerate(((query, gain_q), (key, gain_k))):
                normed = raw[:, at].astype(F32) * rhos[n] * gain[head : head + 1, :]
                outs[k, 4 * i + n] = turn(normed, angle, 1).astype(BF)
            outs[k, 4 * i + 2] = value[:, at]
            outs[k, 4 * i + 3] = jnp.where(keep, cot[:, at].astype(F32), 0.0).astype(BF)
    if ups is None:
        return
    rows = []
    for n, raw in ((0, query), (1, key)):
        rows.append(jnp.broadcast_to(rhos[n], (FRAME_TOK, FRAME_TOK)).T[0:8])
        carried = jnp.zeros((RANK, FRAME_TOK), F32)
        for head in range(HEADS):
            at = slice(head * HEAD_DIM, (head + 1) * HEAD_DIM)
            normed = (raw[:, at].astype(F32) * rhos[n]).astype(BF)
            carried = carried + nt(ups[n, :, at], normed)
        local[n * RANK : (n + 1) * RANK, :] = carried
        local[64 + 8 * n : 72 + 8 * n, :] = rows[n]
    down = nt(downs[...], tokens[...])
    at_row = lax.broadcasted_iota(jnp.int32, (RANK, FRAME_TOK), 0)
    extra = jnp.zeros((RANK, FRAME_TOK), F32)
    for n in range(2):
        wide = jnp.concatenate([rows[n]] * 4, 0)
        high = wide.astype(BF).astype(F32)
        extra = jnp.where(at_row == 2 * n, high, extra)
        extra = jnp.where(at_row == 2 * n + 1, wide - high, extra)
    aux = jnp.concatenate([down, extra], 0).astype(BF)
    for k in range(GROUPS):
        outs[k, 4] = aux


def attend_kernel(base, last, flags, packs, gain_q, gain_k, by_frame, *refs):
    if last:
        state, refs = refs[0], refs[1:]
        before = state
        within = [state[HELD + n * FRAME_TOK : HELD + (n + 1) * FRAME_TOK, :] for n in range(3)]
        first = HELD + 3 * FRAME_TOK
        ups = [state[first + n * RANK : first + (n + 1) * RANK, :].astype(BF) for n in range(3)]
    else:
        within, ups_all, *refs = refs
    wide_out, summed = refs[:2]
    refs = refs[2:]
    if last:
        mean_out, *mix = refs[:4]
        refs = refs[4:]
    q_s, k_s, kt_s, v_s, g_s, sc, dp, pb, db, dk_acc, dv_acc, dq_s, prod_s, sums = refs
    s = lax.axis_index("seq")
    step = pl.program_id(0)
    head = s * LOCAL_HEADS + base + step
    owner = []
    for k in range(GROUPS):
        owner.append(flags[0, k] + (owner[-1] if k else 0))
        at = slice(k * FRAME_TOK, (k + 1) * FRAME_TOK)
        q_s[at, :] = packs[k, 0]
        key = packs[k, 1]
        k_s[at, :] = key
        kt_s[:, at] = key.astype(F32).T.astype(BF)
        v_s[at, :] = packs[k, 2]
        g_s[at, :] = packs[k, 3]
    factor = SCALING * math.log2(math.e)
    lane = lax.broadcasted_iota(jnp.int32, (1, 256), 1)
    for t in range(4):
        b = t % 2
        tile = slice(t * 256, (t + 1) * 256)
        q_t, g_t = q_s[tile, :], g_s[tile, :]
        limit = jnp.where(lane < FRAME_TOK, owner[2 * t], owner[2 * t + 1])
        bias = [jnp.where(owner[j] <= limit, 0.0, HIDDEN) for j in range(GROUPS)]
        sc[b] = nt(k_s[...], q_t)
        dp[b] = nt(v_s[...], g_t)
        top = jnp.full((8, 256), 2.0 * HIDDEN, F32)
        for j in range(GROUPS):
            part = sc[b, j * FRAME_TOK : (j + 1) * FRAME_TOK, :]
            top = jnp.maximum(top, jnp.max(part.reshape(16, 8, 256), axis=0) + bias[j])
        top = jnp.max(top, axis=0, keepdims=True)
        total = jnp.zeros((8, 256), F32)
        cross = jnp.zeros((8, 256), F32)
        for j in range(GROUPS):
            at = slice(j * FRAME_TOK, (j + 1) * FRAME_TOK)
            weight = jnp.exp2((sc[b, at, :] - (top - bias[j])) * factor)
            sc[b, at, :] = weight
            total = total + jnp.sum(weight.reshape(16, 8, 256), axis=0)
            cross = cross + jnp.sum((weight * dp[b, at, :]).reshape(16, 8, 256), axis=0)
        inverse = 1.0 / jnp.sum(total, axis=0, keepdims=True)
        delta = jnp.sum(cross, axis=0, keepdims=True) * inverse
        for j in range(GROUPS):
            at = slice(j * FRAME_TOK, (j + 1) * FRAME_TOK)
            prob = sc[b, at, :] * inverse
            pb[b, at, :] = prob.astype(BF)
            db[b, at, :] = (prob * (dp[b, at, :] - delta)).astype(BF)
        dv, dk = nn(pb[b], g_t), nn(db[b], q_t)
        if t == 0:
            dv_acc[...] = dv
            dk_acc[...] = dk
        else:
            dv_acc[...] += dv
            dk_acc[...] += dk
        dq_s[tile, :] = nn(kt_s[...], db[b]).T
    if not last:
        up_at = pl.ds(pl.multiple_of(head * HEAD_DIM, HEAD_DIM), HEAD_DIM)
        ups = [ups_all[n, :, up_at] for n in range(3)]
    gains = [gain[pl.ds(head, 1), :] for gain in (gain_q, gain_k)]
    for k in range(GROUPS):
        at = slice(k * FRAME_TOK, (k + 1) * FRAME_TOK)
        angle = angles(by_frame, within, k)
        for n, (acc, rot) in enumerate(((dq_s, q_s), (dk_acc, k_s))):
            grad = (acc[at, :] * SCALING).astype(BF).astype(F32)
            wide = gains[n] * turn(grad, angle, -1)
            wide_out[0, n, at, :] = wide.astype(BF)
            prod_s[n, at, :] = (grad * rot[at, :].astype(F32)).astype(BF)
        wide_out[0, 2, at, :] = dv_acc[at, :].astype(BF)
    ones = jnp.ones((16, HEAD_DIM), BF)
    parts = [nt(ups[n], wide_out[0, n]) for n in range(3)]
    parts += [nt(ones, prod_s[n])[0:8] for n in range(2)]
    full = jnp.concatenate(parts, 0)
    for k in range(GROUPS):
        part = full[:, k * FRAME_TOK : (k + 1) * FRAME_TOK]
        at = slice(k * 112, (k + 1) * 112)
        if last:
            sums[k] = part + before[at, :]
        else:
            summed[at, :] = part + jnp.where(step > 0, summed[at, :], 0.0)
    if not last:
        later = pl.ds(pl.multiple_of((s * LOCAL_HEADS + 2) * HEAD_DIM, HEAD_DIM), HEAD_DIM)
        for n in range(3):
            summed[HELD + n * FRAME_TOK : HELD + (n + 1) * FRAME_TOK, :] = within[n]
            first = HELD + 3 * FRAME_TOK + n * RANK
            summed[first : first + RANK, :] = ups_all[n, :, later].astype(F32)
        return
    at_row = lax.broadcasted_iota(jnp.int32, (8, FRAME_TOK), 0)
    for n in range(2):
        gathered = jnp.zeros((8, FRAME_TOK), F32)
        for k in range(GROUPS):
            row = sums[jnp.bitwise_xor(s, k), 96 + 8 * n : 104 + 8 * n]
            gathered = jnp.where(at_row == k, row, gathered)
        mean_out[8 * n : 8 * n + 8, :] = gathered
    tail = halves(mean_out[...])
    for b in range(2):
        summed[b] = sums[jnp.bitwise_xor(s, b), 0:96]
        for a in range(1, 4):
            away = jnp.bitwise_xor(s, 2 * a + b)
            mix[a - 1][b * 96 : (b + 1) * 96, :] = sums[away, 0:96].astype(BF)
    for a in range(1, 4):
        mix[a - 1][192:224, :] = tail


def halves(means):
    high = means.astype(BF).astype(F32)
    return jnp.concatenate([high, means - high], 0).astype(BF)


def add_means(got, first, bit):
    tail = got[first : first + 32, :].astype(F32)
    tail = tail[0:16] + tail[16:32]
    moved = [tail[8 * n + (p ^ bit) : 8 * n + (p ^ bit) + 1] for n in range(2) for p in range(8)]
    return jnp.concatenate(moved, 0)


def mix_kernel(keep, means, r1, r2, r3, keep_out, means_out, send):
    total = (means[...] + add_means(r1, 192, 2)) + (add_means(r2, 192, 4) + add_means(r3, 192, 6))
    means_out[...] = total
    for i in range(2):
        at = slice(i * 96, (i + 1) * 96)
        value = keep[i] + r1[at, :].astype(F32)
        value = value + (r2[at, :].astype(F32) + r3[at, :].astype(F32))
        if i == 0:
            keep_out[...] = value
        else:
            send[0:96, :] = value.astype(BF)
    send[96:128, :] = halves(total)


def owner_kernel(kept, means, got, local, tokens, keep, send, means_out, rows_s, mixed_s):
    _, y, x, c = position()
    total = kept[...] + got[0:96, :].astype(F32)
    full = means[...] + add_means(got, 96, 1)
    means_out[...] = full
    for n in range(2):
        at = slice(n * RANK, (n + 1) * RANK)
        rho = local[64 + 8 * n : 65 + 8 * n, :]
        mean = full[8 * n : 8 * n + 1] * (1.0 / CHANNELS)
        rows_s[at, :] = rho * (total[at] - mean * local[at, :])
    rows_s[64:96, :] = total[64:96]
    for k in range(4):
        first = pl.multiple_of(jnp.bitwise_xor(y, k) * 24, 8)
        mixed_s[k * 24 : (k + 1) * 24, :] = rows_s[pl.ds(first, 24), :]
    mixed = mixed_s[...].astype(BF)
    for a in range(2):
        for b in range(4):
            block = jnp.bitwise_xor(c, a) * 4 + jnp.bitwise_xor(x, b)
            at = pl.ds(pl.multiple_of(block * COLS, HEAD_DIM), COLS)
            out = nn(mixed, tokens[:, at])
            for k in range(4):
                part = out[k * 24 : (k + 1) * 24]
                if a == 0:
                    keep[b, k] = part
                else:
                    send[b, k] = part.astype(BF)


def up_kernel(means, firsts, lasts, wide01, wide2, *refs):
    gain_q, gain_k, by_frame, within, keep, send, turned_s, up_s = refs
    wides = [wide01.at[0], wide01.at[1], wide2.at[0]]
    s, _, x, c = position()
    xl = jnp.bitwise_and(x, 1)
    for h in range(LOCAL_HEADS):
        lanes = slice(h * HEAD_DIM, (h + 1) * HEAD_DIM)
        for k in range(GROUPS):
            at = slice(k * FRAME_TOK, (k + 1) * FRAME_TOK)
            angle = angles(by_frame, within, k)
            for n in range(2):
                rot = (lasts if h == 2 else firsts)[k, 4 * (h % 2) + n].astype(F32)
                turned_s[n, at, lanes] = turn(rot, angle, -1).astype(BF)
    for n in range(3):
        plain_hi, plain_lo, along = [], [], []
        for p in range(GROUPS):
            aux = lasts[p, 4].astype(F32)
            down = aux[n * RANK : (n + 1) * RANK]
            if n == 2:
                plain_hi.append(down.astype(BF))
                continue
            rho = aux[96 + 2 * n : 97 + 2 * n] + aux[97 + 2 * n : 98 + 2 * n]
            mean = means[pl.ds(8 * n + jnp.bitwise_xor(s, p), 1), :]
            scaled = down * rho
            high = scaled.astype(BF)
            plain_hi.append(high)
            plain_lo.append((scaled - high.astype(F32)).astype(BF))
            along.append((scaled * (mean * (1.0 / CHANNELS))).astype(BF))
        high = jnp.concatenate(plain_hi, 1)
        for h in range(LOCAL_HEADS):
            lanes = slice(h * HEAD_DIM, (h + 1) * HEAD_DIM)
            out = nn(high, wides[h][n])
            if n < 2:
                gain = (gain_q, gain_k)[n][pl.ds(s * LOCAL_HEADS + h, 1), :]
                out = out + nn(jnp.concatenate(plain_lo, 1), wides[h][n])
                out = out - nn(jnp.concatenate(along, 1), turned_s[n, :, lanes]) / gain
            up_s[n * RANK : (n + 1) * RANK, lanes] = out
    for a in range(2):
        for b in range(2):
            block = jnp.bitwise_xor(c, a) * 2 + jnp.bitwise_xor(xl, b)
            part = up_s[pl.ds(pl.multiple_of(block * 24, 8), 24), :]
            if a == 0:
                keep[b] = part
            else:
                send[b] = part.astype(BF)


def core_sum_kernel(keep, got, own, *sends):
    for b in range(4):
        value = keep[b] + got[b].astype(F32)
        if b == 0:
            own[...] = value
        else:
            sends[b - 1][...] = value.astype(BF)


def up_core_kernel(keep, got, own, send):
    own[...] = keep[0] + got[0].astype(F32)
    send[...] = (keep[1] + got[1].astype(F32)).astype(BF)


def x_sum_kernel(own, r1, r2, r3, keep, *sends):
    for b in range(4):
        value = (own[b] + r1[b].astype(F32)) + (r2[b].astype(F32) + r3[b].astype(F32))
        if b == 0:
            keep[...] = value
        else:
            sends[b - 1][...] = value.astype(BF)


def y_sum_kernel(own, r1, r2, r3, up_own, up_got, out):
    value = (own[...] + r1[...].astype(F32)) + (r2[...].astype(F32) + r3[...].astype(F32))
    out[:, :COLS] = value.astype(BF)
    out[:, COLS:] = (up_own[...] + up_got[...].astype(F32)).astype(BF)


def z_four_kernel(own, r1, r2, r3, out):
    value = (own[...].astype(F32) + r1[...].astype(F32)) + (r2[...].astype(F32) + r3[...].astype(F32))
    out[...] = value.astype(BF)


def z_sum_kernel(own, got, out):
    out[...] = (own[...].astype(F32) + got[...].astype(F32)).astype(BF)


def stack_kernel(*refs):
    out = refs[-1]
    for n, ref in enumerate(refs[:-1]):
        out[n] = ref[...]


def final_kernel(own, got, down_out, up_out):
    _, y, x, c = position()

    def piece(ca, xa, ya, lanes):
        xr, yr = jnp.bitwise_xor(x, xa), jnp.bitwise_xor(y, ya)
        mine = own[xr, yr, :, lanes].astype(F32)
        other = got[xr, yr, :, lanes].astype(F32)
        return jnp.where(c == ca, mine, other)

    for ca in range(2):
        for xa in range(4):
            block = [piece(ca, xa, ya, slice(0, COLS)) for ya in range(4)]
            first = (ca * 4 + xa) * COLS
            down_out[:, first : first + COLS] = jnp.concatenate(block, 0).astype(BF)
    for ya in range(4):
        for xh in range(2):
            block = [
                piece(ca, xh * 2 + xl, ya, slice(COLS, BOTH)) for ca in range(2) for xl in range(2)
            ]
            first = (ya * 2 + xh) * GCOLS
            up_out[:, first : first + GCOLS] = jnp.concatenate(block, 0).astype(BF)


def shape(dims, dtype=BF):
    return jax.ShapeDtypeStruct(dims, dtype)


def call(kernel, ins, outs, scratch=(), smem=0, mib=16):
    single = not isinstance(outs, (list, tuple))
    return pl.pallas_call(
        kernel,
        out_shape=outs,
        in_specs=[SMEM] * smem + [VMEM] * (len(ins) - smem),
        out_specs=VMEM if single else [VMEM] * len(outs),
        scratch_shapes=list(scratch),
        compiler_params=params(mib),
    )(*ins)


def place(x, y, z, c):
    return (y * 2 + x // 2) * 32 + z * 4 + (x % 2) * 2 + c


def swap(array, dx=0, dy=0, dz=0, dc=0):
    pairs = [
        (place(x, y, z, c), place(x ^ dx, y ^ dy, z ^ dz, c ^ dc))
        for x in range(4)
        for y in range(4)
        for z in range(8)
        for c in range(2)
    ]
    return lax.ppermute(array, ("seq", "dp"), pairs)


def seq_swap(array, k):
    return swap(array, dx=2 * (k & 1), dy=k >> 1)


def whole(array):
    zeros = (0,) * len(array.shape)
    return pl.BlockSpec(array.shape, lambda i: zeros)


def pack(ins, heads, outs, steps):
    count = FRAME_TOK // steps
    specs = [pl.BlockSpec((count, CHANNELS), lambda i: (i, 0))] * 4 + [whole(a) for a in ins[4:]]
    specs[8] = pl.BlockSpec((3, count, HEAD_DIM), lambda i: (0, i, 0))
    slots = outs[0].shape[1]
    out_specs = [pl.BlockSpec((GROUPS, slots, count, HEAD_DIM), lambda i: (0, 0, i, 0))]
    return pl.pallas_call(
        functools.partial(pack_kernel, heads),
        grid=(steps,),
        out_shape=outs,
        in_specs=specs,
        out_specs=out_specs + [whole(a) for a in outs[1:]],
        scratch_shapes=[pltpu.VMEM((FRAME_TOK, FRAME_TOK), F32)],
        compiler_params=params(BIG),
    )(*ins)


def attend(base, heads, ins, before):
    last = before is not None
    seq_len = FRAMES * FRAME_TOK
    rows = (seq_len, HEAD_DIM)
    piece = pl.BlockSpec((GROUPS, 4, FRAME_TOK, HEAD_DIM), lambda i: (0, i, 0, 0))
    specs = [SMEM, piece] + [whole(a) for a in ins[2:]]
    outs = [shape((heads, 3, *rows))]
    out_specs = [pl.BlockSpec((1, 3, *rows), lambda i: (i, 0, 0, 0))]
    if last:
        ins = [*ins, before]
        specs.append(whole(before))
        extra = [shape((2, 96, FRAME_TOK), F32), shape((16, FRAME_TOK), F32)]
        extra += [shape((224, FRAME_TOK))] * 3
        out_specs += [VMEM] * 5
    else:
        extra = [shape((HELD + 3 * FRAME_TOK + 96, FRAME_TOK), F32)]
        out_specs += [whole(a) for a in extra]
    return pl.pallas_call(
        functools.partial(attend_kernel, base, last),
        grid=(heads,),
        out_shape=outs + extra,
        in_specs=specs,
        out_specs=out_specs,
        scratch_shapes=[
            pltpu.VMEM(rows, BF),
            pltpu.VMEM(rows, BF),
            pltpu.VMEM((HEAD_DIM, seq_len), BF),
            pltpu.VMEM(rows, BF),
            pltpu.VMEM(rows, BF),
            pltpu.VMEM((2, seq_len, 256), F32),
            pltpu.VMEM((2, seq_len, 256), F32),
            pltpu.VMEM((2, seq_len, 256), BF),
            pltpu.VMEM((2, seq_len, 256), BF),
            pltpu.VMEM(rows, F32),
            pltpu.VMEM(rows, F32),
            pltpu.VMEM(rows, F32),
            pltpu.VMEM((2, *rows), BF),
            pltpu.VMEM((GROUPS, 112, FRAME_TOK), F32),
        ],
        compiler_params=params(32),
        cost_estimate=pl.CostEstimate(
            flops=10 * heads * seq_len * seq_len * HEAD_DIM,
            bytes_accessed=heads * (4 << 20),
            transcendentals=heads * seq_len * seq_len,
        ),
    )(*ins)


def shards(
    input_tokens,
    query_unnormed,
    key_unnormed,
    value_projected,
    cotangent,
    query_norm_gain,
    key_norm_gain,
    adapter_down_maps,
    adapter_up_maps,
    generated_mask,
    block_begin_flags,
):
    by_frame, within = (jnp.asarray(t) for t in rope_tables())
    gain_q = query_norm_gain.reshape(HEADS, HEAD_DIM)
    gain_k = key_norm_gain.reshape(HEADS, HEAD_DIM)
    norms = [gain_q, gain_k, by_frame, within]
    tokens = input_tokens[0]
    downs = adapter_down_maps.reshape(96, WIDTH)

    raws = [query_unnormed[0], key_unnormed[0], value_projected[0], cotangent[0]]
    first = [*raws, generated_mask[0], *norms]
    (firsts,) = pack(first, (0, 1), [shape((GROUPS, 8, FRAME_TOK, HEAD_DIM))], 4)
    lasts, local = pack(
        first + [adapter_up_maps, downs, tokens],
        (2,),
        [shape((GROUPS, 5, FRAME_TOK, HEAD_DIM)), shape((80, FRAME_TOK), F32)],
        1,
    )
    firsts = lax.all_to_all(firsts, "seq", 0, 0, tiled=True)
    lasts = lax.all_to_all(lasts, "seq", 0, 0, tiled=True)
    wide01, before = attend(0, 2, [block_begin_flags, firsts, *norms, adapter_up_maps], None)
    wide2, kept, means, *mix = attend(2, 1, [block_begin_flags, lasts, *norms[:3]], before)
    mix = [swap(mix[a - 1], dy=a) for a in range(1, 4)]
    kept, means, mix = call(
        mix_kernel,
        [kept, means, *mix],
        [shape((96, FRAME_TOK), F32), shape((16, FRAME_TOK), F32), shape((128, FRAME_TOK))],
    )
    mix = seq_swap(mix, 1)

    keep, send, means = call(
        owner_kernel,
        [kept, means, mix, local, tokens],
        [shape((4, 4, 24, COLS), F32), shape((4, 4, 24, COLS)), shape((16, FRAME_TOK), F32)],
        [pltpu.VMEM((96, FRAME_TOK), F32), pltpu.VMEM((96, FRAME_TOK), F32)],
    )
    up_keep, up_send = call(
        up_kernel,
        [means, firsts, lasts, wide01, wide2, *norms],
        [shape((2, 24, GCOLS), F32), shape((2, 24, GCOLS))],
        [pltpu.VMEM((2, 1024, GCOLS), BF), pltpu.VMEM((96, GCOLS), F32)],
        mib=24,
    )
    got = swap(send, dc=1)
    up_got = swap(up_send, dc=1)
    slab = (4, 24, COLS)
    own, *parts = call(
        core_sum_kernel, [keep, got], [shape(slab, F32)] + [shape(slab)] * 3
    )
    up_own, up_part = call(
        up_core_kernel, [up_keep, up_got], [shape((24, GCOLS), F32), shape((24, GCOLS))]
    )
    parts = [swap(parts[n], dx=n + 1) for n in range(3)]
    up_part = swap(up_part, dx=1)
    own, *parts = call(
        x_sum_kernel, [own, *parts], [shape(slab[1:], F32)] + [shape(slab[1:])] * 3
    )
    parts = [swap(parts[n], dy=n + 1) for n in range(3)]
    part = call(y_sum_kernel, [own, *parts, up_own, up_part], shape((24, BOTH)))
    four = [swap(part, dz=k) for k in range(1, 4)]
    part = call(z_four_kernel, [part, *four], shape((24, BOTH)))
    part = call(z_sum_kernel, [part, swap(part, dz=7)], shape((24, BOTH)))
    over_y = call(
        stack_kernel, [part] + [swap(part, dy=k) for k in range(1, 4)], shape((4, 24, BOTH))
    )
    over_x = call(
        stack_kernel,
        [over_y] + [swap(over_y, dx=k) for k in range(1, 4)],
        shape((4, 4, 24, BOTH)),
    )
    other = swap(over_x, dc=1)
    grad_down, grad_up = call(
        final_kernel,
        [over_x, other],
        [shape((96, WIDTH)), shape((96, CHANNELS))],
    )
    return grad_down.reshape(3, RANK, WIDTH), grad_up.reshape(3, RANK, CHANNELS)


def solution(mesh):
    rows = P("dp", "seq", None)
    placed = (rows,) * 5 + (P(),) * 4 + (rows, P("dp", None))
    return jax.shard_map(shards, mesh=mesh, in_specs=placed, out_specs=(P(), P()), check_vma=False)
```

```python
import functools
import math

import jax
import jax.numpy as jnp
import numpy as np
from jax import lax
from jax.experimental import pallas as pl
from jax.experimental.pallas import tpu as pltpu
from jax.sharding import PartitionSpec as P

HEADS = 24
HEAD_DIM = 128
GRID_W = 16
FRAME_TOK = 128
FRAMES = 8
RANK = 32
WIDTH = 5120
CHANNELS = 3072
GROUPS = 8
LOCAL_HEADS = 3
NORM_EPS = 1e-06
SCALING = 1.0 / math.sqrt(HEAD_DIM)
BF = jnp.bfloat16
F32 = jnp.float32
HIDDEN = -1e30
BIG = 58
HELD = FRAMES * 112
COLS = WIDTH // 8
GCOLS = CHANNELS // 8
BOTH = COLS + GCOLS

VMEM = pl.BlockSpec(memory_space=pltpu.VMEM)
SMEM = pl.BlockSpec(memory_space=pltpu.SMEM)


def params(mib):
    return pltpu.CompilerParams(vmem_limit_bytes=mib * 1024 * 1024)


def rope_tables():
    time_dims = HEAD_DIM - 4 * (HEAD_DIM // 6)
    space_dims = 2 * (HEAD_DIM // 6)
    tp, sp = time_dims // 2, space_dims // 2
    tok = np.arange(FRAMES * FRAME_TOK)
    frame, within = tok // FRAME_TOK, tok % FRAME_TOK
    row, col = within // GRID_W, within % GRID_W
    pairs = np.arange(HEAD_DIM) // 2
    in_time = pairs < tp
    in_rows = (pairs >= tp) & (pairs < tp + sp)
    offset = np.where(in_time, pairs, np.where(in_rows, pairs - tp, pairs - tp - sp))
    extent = np.where(in_time, time_dims, space_dims)
    rates = np.exp(-math.log(10000.0) * (2 * offset) / extent)
    pos = np.where(
        in_time[None], frame[:, None], np.where(in_rows[None], row[:, None], col[:, None])
    )
    angle = pos * rates[None]
    even = (np.arange(HEAD_DIM) % 2 == 0)[None]
    sine = np.sin(angle)
    table = np.stack([np.cos(angle), np.where(even, -sine, 0.0), np.where(even, 0.0, sine)], 0)
    table = table.reshape(3, FRAMES, FRAME_TOK, HEAD_DIM)
    by_frame = np.where(in_time[None, None], table[:, :, 0], 0.0).transpose(1, 0, 2)
    within = np.where(in_time[None, None], 0.0, table[:, 0])
    return by_frame.reshape(3 * FRAMES, HEAD_DIM).astype(np.float32), within.astype(np.float32)


def angles(by_frame, within, frame):
    return [within[n] + by_frame[pl.ds(3 * frame + n, 1), :] for n in range(3)]


def turn(z, angle, sign):
    cosine, left, right = angle
    mixed = pltpu.roll(z, HEAD_DIM - 1, 1) * left + pltpu.roll(z, 1, 1) * right
    base = z * cosine
    return base + mixed if sign > 0 else base - mixed


def position():
    s, d = lax.axis_index("seq"), lax.axis_index("dp")
    x = lax.rem(s, 2) * 2 + lax.rem(lax.div(d, 2), 2)
    return s, lax.div(s, 2), x, lax.rem(d, 2)


def nt(a, b, **kw):
    return lax.dot_general(
        a, b, (((1,), (1,)), ((), ())), preferred_element_type=F32, **kw
    )


def nn(a, b):
    return lax.dot_general(a, b, (((1,), (0,)), ((), ())), preferred_element_type=F32)


def rho_of(raw):
    total = jnp.zeros((raw.shape[0], HEAD_DIM), F32)
    for n in range(HEADS):
        part = raw[:, n * HEAD_DIM : (n + 1) * HEAD_DIM].astype(F32)
        total = total + part * part
    mean = jnp.sum(total, axis=1, keepdims=True) * (1.0 / CHANNELS)
    return lax.rsqrt(mean + NORM_EPS)


def pack_kernel(heads, query, key, value, cot, mask, gain_q, gain_k, by_frame, within, *refs):
    s = lax.axis_index("seq")
    if len(refs) > 2:
        ups, downs, tokens, *outs, local, keep_s = refs
    else:
        ups, (outs, keep_s) = None, refs
    count = query.shape[0]
    keep_s[...] = jnp.broadcast_to(mask[...].astype(F32), (FRAME_TOK, FRAME_TOK)).T
    keep = keep_s[pl.ds(pl.multiple_of(pl.program_id(0) * count, count), count), :] > 0.0
    rhos = [rho_of(raw) for raw in (query, key)]
    angle = angles(by_frame, within, s)
    for k in range(GROUPS):
        for i, h in enumerate(heads):
            head = (k if ups is None else jnp.bitwise_xor(s, k)) * LOCAL_HEADS + h
            at = pl.ds(pl.multiple_of(head * HEAD_DIM, HEAD_DIM), HEAD_DIM)
            out = outs.at[k] if ups is None else outs[k]
            for n, (raw, gain) in enumerate(((query, gain_q), (key, gain_k))):
                normed = raw[:, at].astype(F32) * rhos[n] * gain[pl.ds(head, 1), :]
                out[4 * i + n] = turn(normed, angle, 1).astype(BF)
            out[4 * i + 2] = value[:, at]
            out[4 * i + 3] = jnp.where(keep, cot[:, at].astype(F32), 0.0).astype(BF)
    if ups is None:
        return
    rows = []
    for n, raw in ((0, query), (1, key)):
        rows.append(jnp.broadcast_to(rhos[n], (FRAME_TOK, FRAME_TOK)).T[0:8])
        carried = jnp.zeros((RANK, FRAME_TOK), F32)
        for head in range(HEADS):
            at = slice(head * HEAD_DIM, (head + 1) * HEAD_DIM)
            normed = (raw[:, at].astype(F32) * rhos[n]).astype(BF)
            carried = carried + nt(ups[n, :, at], normed)
        local[n * RANK : (n + 1) * RANK, :] = carried
        local[64 + 8 * n : 72 + 8 * n, :] = rows[n]
    down = nt(downs[...], tokens[...])
    at_row = lax.broadcasted_iota(jnp.int32, (RANK, FRAME_TOK), 0)
    extra = jnp.zeros((RANK, FRAME_TOK), F32)
    for n in range(2):
        wide = jnp.concatenate([rows[n]] * 4, 0)
        high = wide.astype(BF).astype(F32)
        extra = jnp.where(at_row == 2 * n, high, extra)
        extra = jnp.where(at_row == 2 * n + 1, wide - high, extra)
    aux = jnp.concatenate([down, extra], 0).astype(BF)
    for k in range(GROUPS):
        outs[k][4] = aux


def attend_kernel(base, flags, *refs):
    last = base == LOCAL_HEADS - 1
    s = lax.axis_index("seq")
    if last:
        packs, refs = refs[:GROUPS], refs[GROUPS:]
        frames = [jnp.bitwise_xor(s, k) for k in range(GROUPS)]
    else:
        packs, refs = [refs[0].at[k] for k in range(GROUPS)], refs[1:]
        frames = list(range(GROUPS))
    gain_q, gain_k, by_frame, *refs = refs
    if base == 0:
        within, ups_all, *refs = refs
    else:
        state, *refs = refs
        before = state
        if last:
            before, *refs = refs
        within = [state[HELD + n * FRAME_TOK : HELD + (n + 1) * FRAME_TOK, :] for n in range(3)]
        first = HELD + 3 * FRAME_TOK + (base - 1) * 96
        ups = [state[first + n * RANK : first + (n + 1) * RANK, :].astype(BF) for n in range(3)]
    wide_out, summed = refs[:2]
    refs = refs[2:]
    if last:
        mean_out, *mix = refs[:4]
        refs = refs[4:]
    q_s, k_s, kt_s, v_s, g_s, sc, dp, pb, db, dk_acc, dv_acc, dq_s, prod_s, sums = refs
    head = s * LOCAL_HEADS + base
    owner = []
    for k in range(GROUPS):
        owner.append(sum(jnp.where(f <= frames[k], flags[0, f], 0) for f in range(FRAMES)))
        at = slice(k * FRAME_TOK, (k + 1) * FRAME_TOK)
        q_s[at, :] = packs[k][0]
        key = packs[k][1]
        k_s[at, :] = key
        kt_s[:, at] = key.astype(F32).T.astype(BF)
        v_s[at, :] = packs[k][2]
        g_s[at, :] = packs[k][3]
    factor = SCALING * math.log2(math.e)
    lane = lax.broadcasted_iota(jnp.int32, (1, 256), 1)
    for t in range(4):
        b = t % 2
        tile = slice(t * 256, (t + 1) * 256)
        q_t, g_t = q_s[tile, :], g_s[tile, :]
        limit = jnp.where(lane < FRAME_TOK, owner[2 * t], owner[2 * t + 1])
        bias = [jnp.where(owner[j] <= limit, 0.0, HIDDEN) for j in range(GROUPS)]
        sc[b] = nt(k_s[...], q_t)
        dp[b] = nt(v_s[...], g_t)
        top = jnp.full((8, 256), 2.0 * HIDDEN, F32)
        for j in range(GROUPS):
            part = sc[b, j * FRAME_TOK : (j + 1) * FRAME_TOK, :]
            top = jnp.maximum(top, jnp.max(part.reshape(16, 8, 256), axis=0) + bias[j])
        top = jnp.max(top, axis=0, keepdims=True)
        total = jnp.zeros((8, 256), F32)
        cross = jnp.zeros((8, 256), F32)
        for j in range(GROUPS):
            at = slice(j * FRAME_TOK, (j + 1) * FRAME_TOK)
            weight = jnp.exp2((sc[b, at, :] - (top - bias[j])) * factor)
            sc[b, at, :] = weight
            total = total + jnp.sum(weight.reshape(16, 8, 256), axis=0)
            cross = cross + jnp.sum((weight * dp[b, at, :]).reshape(16, 8, 256), axis=0)
        inverse = 1.0 / jnp.sum(total, axis=0, keepdims=True)
        delta = jnp.sum(cross, axis=0, keepdims=True) * inverse
        for j in range(GROUPS):
            at = slice(j * FRAME_TOK, (j + 1) * FRAME_TOK)
            prob = sc[b, at, :] * inverse
            pb[b, at, :] = prob.astype(BF)
            db[b, at, :] = (prob * (dp[b, at, :] - delta)).astype(BF)
        dv, dk = nn(pb[b], g_t), nn(db[b], q_t)
        if t == 0:
            dv_acc[...] = dv
            dk_acc[...] = dk
        else:
            dv_acc[...] += dv
            dk_acc[...] += dk
        dq_s[tile, :] = nn(kt_s[...], db[b]).T
    if base == 0:
        up_at = pl.ds(pl.multiple_of(head * HEAD_DIM, HEAD_DIM), HEAD_DIM)
        ups = [ups_all[n, :, up_at] for n in range(3)]
    gains = [gain[pl.ds(head, 1), :] for gain in (gain_q, gain_k)]
    for k in range(GROUPS):
        at = slice(k * FRAME_TOK, (k + 1) * FRAME_TOK)
        angle = angles(by_frame, within, frames[k])
        for n, (acc, rot) in enumerate(((dq_s, q_s), (dk_acc, k_s))):
            grad = (acc[at, :] * SCALING).astype(BF).astype(F32)
            wide = gains[n] * turn(grad, angle, -1)
            wide_out[0, n, at, :] = wide.astype(BF)
            prod_s[n, at, :] = (grad * rot[at, :].astype(F32)).astype(BF)
        wide_out[0, 2, at, :] = dv_acc[at, :].astype(BF)
    ones = jnp.ones((16, HEAD_DIM), BF)
    parts = [nt(ups[n], wide_out[0, n]) for n in range(3)]
    parts += [nt(ones, prod_s[n])[0:8] for n in range(2)]
    full = jnp.concatenate(parts, 0)
    for k in range(GROUPS):
        part = full[:, k * FRAME_TOK : (k + 1) * FRAME_TOK]
        at = slice(k * 112, (k + 1) * 112)
        if last:
            at = pl.ds(pl.multiple_of(frames[k] * 112, 8), 112)
            sums[k] = part + before[at, :]
        elif base == 0:
            summed[at, :] = part
        else:
            summed[at, :] = part + before[at, :]
    if base == 0:
        for n in range(3):
            summed[HELD + n * FRAME_TOK : HELD + (n + 1) * FRAME_TOK, :] = within[n]
            for h in range(1, LOCAL_HEADS):
                at = pl.ds(pl.multiple_of((head + h) * HEAD_DIM, HEAD_DIM), HEAD_DIM)
                first = HELD + 3 * FRAME_TOK + (h - 1) * 96 + n * RANK
                summed[first : first + RANK, :] = ups_all[n, :, at].astype(F32)
    if not last:
        return
    at_row = lax.broadcasted_iota(jnp.int32, (8, FRAME_TOK), 0)
    for n in range(2):
        gathered = jnp.zeros((8, FRAME_TOK), F32)
        for k in range(GROUPS):
            row = sums[k, 96 + 8 * n : 104 + 8 * n]
            gathered = jnp.where(at_row == k, row, gathered)
        mean_out[8 * n : 8 * n + 8, :] = gathered
    tail = halves(mean_out[...])
    for b in range(2):
        summed[b] = sums[b, 0:96]
        for a in range(1, 4):
            mix[a - 1][b * 96 : (b + 1) * 96, :] = sums[2 * a + b, 0:96].astype(BF)
    for a in range(1, 4):
        mix[a - 1][192:224, :] = tail


def halves(means):
    high = means.astype(BF).astype(F32)
    return jnp.concatenate([high, means - high], 0).astype(BF)


def add_means(got, first, bit):
    tail = got[first : first + 32, :].astype(F32)
    tail = tail[0:16] + tail[16:32]
    moved = [tail[8 * n + (p ^ bit) : 8 * n + (p ^ bit) + 1] for n in range(2) for p in range(8)]
    return jnp.concatenate(moved, 0)


def mix_kernel(keep, means, r1, r2, r3, keep_out, means_out, send):
    total = (means[...] + add_means(r1, 192, 2)) + (add_means(r2, 192, 4) + add_means(r3, 192, 6))
    means_out[...] = total
    for i in range(2):
        at = slice(i * 96, (i + 1) * 96)
        value = keep[i] + r1[at, :].astype(F32)
        value = value + (r2[at, :].astype(F32) + r3[at, :].astype(F32))
        if i == 0:
            keep_out[...] = value
        else:
            send[0:96, :] = value.astype(BF)
    send[96:128, :] = halves(total)


def owner_kernel(kept, means, got, local, tokens, keep, send, means_out, rows_s, mixed_s):
    _, y, x, c = position()
    total = kept[...] + got[0:96, :].astype(F32)
    full = means[...] + add_means(got, 96, 1)
    means_out[...] = full
    for n in range(2):
        at = slice(n * RANK, (n + 1) * RANK)
        rho = local[64 + 8 * n : 65 + 8 * n, :]
        mean = full[8 * n : 8 * n + 1] * (1.0 / CHANNELS)
        rows_s[at, :] = rho * (total[at] - mean * local[at, :])
    rows_s[64:96, :] = total[64:96]
    for k in range(4):
        first = pl.multiple_of(jnp.bitwise_xor(y, k) * 24, 8)
        mixed_s[k * 24 : (k + 1) * 24, :] = rows_s[pl.ds(first, 24), :]
    mixed = mixed_s[...].astype(BF)
    for a in range(2):
        for b in range(4):
            block = jnp.bitwise_xor(c, a) * 4 + jnp.bitwise_xor(x, b)
            at = pl.ds(pl.multiple_of(block * COLS, HEAD_DIM), COLS)
            out = nn(mixed, tokens[:, at])
            for k in range(4):
                part = out[k * 24 : (k + 1) * 24]
                if a == 0:
                    keep[b, k] = part
                else:
                    send[b, k] = part.astype(BF)


def up_kernel(means, firsts, *refs):
    lasts, wides = refs[:GROUPS], [ref.at[0] for ref in refs[GROUPS : GROUPS + 3]]
    gain_q, gain_k, by_frame, within, keep, send, turned_s, up_s, scaled_s = refs[GROUPS + 3 :]
    s, _, x, c = position()
    xl = jnp.bitwise_and(x, 1)
    order = [jnp.bitwise_xor(s, k) for k in range(GROUPS)]
    for k in range(GROUPS):
        at = slice(k * FRAME_TOK, (k + 1) * FRAME_TOK)
        for h in range(LOCAL_HEADS):
            lanes = slice(h * HEAD_DIM, (h + 1) * HEAD_DIM)
            if h != 1:
                angle = angles(by_frame, within, order[k] if h == 2 else k)
            for n in range(2):
                rot = lasts[k][n] if h == 2 else firsts[k, 4 * h + n]
                turned_s[n, at, lanes] = turn(rot.astype(F32), angle, -1).astype(BF)
    for p in range(GROUPS):
        aux = lasts[p][4].astype(F32)
        for n in range(3):
            down = aux[n * RANK : (n + 1) * RANK]
            if n == 2:
                scaled_s[p, n, 0] = down.astype(BF)
                continue
            rho = aux[96 + 2 * n : 97 + 2 * n] + aux[97 + 2 * n : 98 + 2 * n]
            scaled = down * rho
            high = scaled.astype(BF)
            mean = means[8 * n + p : 8 * n + p + 1, :] * (1.0 / CHANNELS)
            scaled_s[p, n, 0] = high
            scaled_s[p, n, 1] = (scaled - high.astype(F32)).astype(BF)
            scaled_s[p, n, 2] = (scaled * mean).astype(BF)

    def rows(n, kind, h):
        places = range(GROUPS) if h == 2 else order
        return jnp.concatenate([scaled_s[p, n, kind] for p in places], 1)

    for n in range(3):
        for h in range(LOCAL_HEADS):
            lanes = slice(h * HEAD_DIM, (h + 1) * HEAD_DIM)
            out = nn(rows(n, 0, h), wides[h][n])
            if n < 2:
                gain = (gain_q, gain_k)[n][pl.ds(s * LOCAL_HEADS + h, 1), :]
                out = out + nn(rows(n, 1, h), wides[h][n])
                out = out - nn(rows(n, 2, h), turned_s[n, :, lanes]) / gain
            up_s[n * RANK : (n + 1) * RANK, lanes] = out
    for a in range(2):
        for b in range(2):
            block = jnp.bitwise_xor(c, a) * 2 + jnp.bitwise_xor(xl, b)
            part = up_s[pl.ds(pl.multiple_of(block * 24, 8), 24), :]
            if a == 0:
                keep[b] = part
            else:
                send[b] = part.astype(BF)


def core_sum_kernel(keep, got, own, *sends):
    for b in range(4):
        value = keep[b] + got[b].astype(F32)
        if b == 0:
            own[...] = value
        else:
            sends[b - 1][...] = value.astype(BF)


def up_core_kernel(keep, got, own, send):
    own[...] = keep[0] + got[0].astype(F32)
    send[...] = (keep[1] + got[1].astype(F32)).astype(BF)


def x_sum_kernel(own, r1, r2, r3, keep, *sends):
    for b in range(4):
        value = (own[b] + r1[b].astype(F32)) + (r2[b].astype(F32) + r3[b].astype(F32))
        if b == 0:
            keep[...] = value
        else:
            sends[b - 1][...] = value.astype(BF)


def y_sum_kernel(own, r1, r2, r3, up_own, up_got, out):
    value = (own[...] + r1[...].astype(F32)) + (r2[...].astype(F32) + r3[...].astype(F32))
    out[:, :COLS] = value.astype(BF)
    out[:, COLS:] = (up_own[...] + up_got[...].astype(F32)).astype(BF)


def z_four_kernel(own, r1, r2, r3, out):
    value = (own[...].astype(F32) + r1[...].astype(F32)) + (r2[...].astype(F32) + r3[...].astype(F32))
    out[...] = value.astype(BF)


def z_sum_kernel(own, got, out):
    out[...] = (own[...].astype(F32) + got[...].astype(F32)).astype(BF)


def stack_kernel(*refs):
    out = refs[-1]
    for n, ref in enumerate(refs[:-1]):
        out[n] = ref[...]


def final_kernel(own, got, down_out, up_out):
    _, y, x, c = position()

    def piece(ca, xa, ya, lanes):
        xr, yr = jnp.bitwise_xor(x, xa), jnp.bitwise_xor(y, ya)
        mine = own[xr, yr, :, lanes].astype(F32)
        other = got[xr, yr, :, lanes].astype(F32)
        return jnp.where(c == ca, mine, other)

    for ca in range(2):
        for xa in range(4):
            block = [piece(ca, xa, ya, slice(0, COLS)) for ya in range(4)]
            first = (ca * 4 + xa) * COLS
            down_out[:, first : first + COLS] = jnp.concatenate(block, 0).astype(BF)
    for ya in range(4):
        for xh in range(2):
            block = [
                piece(ca, xh * 2 + xl, ya, slice(COLS, BOTH)) for ca in range(2) for xl in range(2)
            ]
            first = (ya * 2 + xh) * GCOLS
            up_out[:, first : first + GCOLS] = jnp.concatenate(block, 0).astype(BF)


def shape(dims, dtype=BF):
    return jax.ShapeDtypeStruct(dims, dtype)


def call(kernel, ins, outs, scratch=(), smem=0, mib=16):
    single = not isinstance(outs, (list, tuple))
    return pl.pallas_call(
        kernel,
        out_shape=outs,
        in_specs=[SMEM] * smem + [VMEM] * (len(ins) - smem),
        out_specs=VMEM if single else [VMEM] * len(outs),
        scratch_shapes=list(scratch),
        compiler_params=params(mib),
    )(*ins)


def place(x, y, z, c):
    return (y * 2 + x // 2) * 32 + z * 4 + (x % 2) * 2 + c


def swap(array, dx=0, dy=0, dz=0, dc=0):
    pairs = [
        (place(x, y, z, c), place(x ^ dx, y ^ dy, z ^ dz, c ^ dc))
        for x in range(4)
        for y in range(4)
        for z in range(8)
        for c in range(2)
    ]
    return lax.ppermute(array, ("seq", "dp"), pairs)


def seq_swap(array, k):
    return swap(array, dx=2 * (k & 1), dy=k >> 1)


def whole(array):
    zeros = (0,) * len(array.shape)
    return pl.BlockSpec(array.shape, lambda i: zeros)


def pack(ins, heads, outs, steps):
    count = FRAME_TOK // steps
    specs = [pl.BlockSpec((count, CHANNELS), lambda i: (i, 0))] * 4 + [whole(a) for a in ins[4:]]
    specs[8] = pl.BlockSpec((3, count, HEAD_DIM), lambda i: (0, i, 0))
    out_specs = [whole(a) for a in outs]
    if len(outs) == 1:
        out_specs = [pl.BlockSpec((GROUPS, 8, count, HEAD_DIM), lambda i: (0, 0, i, 0))]
    return pl.pallas_call(
        functools.partial(pack_kernel, heads),
        grid=(steps,),
        out_shape=outs,
        in_specs=specs,
        out_specs=out_specs,
        scratch_shapes=[pltpu.VMEM((FRAME_TOK, FRAME_TOK), F32)],
        compiler_params=params(BIG),
    )(*ins)


def attend(base, ins):
    seq_len = FRAMES * FRAME_TOK
    rows = (seq_len, HEAD_DIM)
    outs = [shape((1, 3, *rows))]
    out_specs = [whole(outs[0])]
    if base == LOCAL_HEADS - 1:
        specs = [SMEM] + [pl.BlockSpec((4, FRAME_TOK, HEAD_DIM), lambda i: (0, 0, 0))] * GROUPS
        extra = [shape((2, 96, FRAME_TOK), F32), shape((16, FRAME_TOK), F32)]
        extra += [shape((224, FRAME_TOK))] * 3
        out_specs += [VMEM] * 5
    else:
        specs = [SMEM, pl.BlockSpec((GROUPS, 4, FRAME_TOK, HEAD_DIM), lambda i: (0, base, 0, 0))]
        extra = [shape((HELD + (1 - base) * (3 * FRAME_TOK + 192), FRAME_TOK), F32)]
        out_specs += [whole(a) for a in extra]
    specs += [whole(a) for a in ins[len(specs) :]]
    return pl.pallas_call(
        functools.partial(attend_kernel, base),
        grid=(1,),
        out_shape=outs + extra,
        in_specs=specs,
        out_specs=out_specs,
        scratch_shapes=[
            pltpu.VMEM(rows, BF),
            pltpu.VMEM(rows, BF),
            pltpu.VMEM((HEAD_DIM, seq_len), BF),
            pltpu.VMEM(rows, BF),
            pltpu.VMEM(rows, BF),
            pltpu.VMEM((2, seq_len, 256), F32),
            pltpu.VMEM((2, seq_len, 256), F32),
            pltpu.VMEM((2, seq_len, 256), BF),
            pltpu.VMEM((2, seq_len, 256), BF),
            pltpu.VMEM(rows, F32),
            pltpu.VMEM(rows, F32),
            pltpu.VMEM(rows, F32),
            pltpu.VMEM((2, *rows), BF),
            pltpu.VMEM((GROUPS, 112, FRAME_TOK), F32),
        ],
        compiler_params=params(32),
        cost_estimate=pl.CostEstimate(
            flops=10 * seq_len * seq_len * HEAD_DIM,
            bytes_accessed=4 << 20,
            transcendentals=seq_len * seq_len,
        ),
    )(*ins)


def shards(
    input_tokens,
    query_unnormed,
    key_unnormed,
    value_projected,
    cotangent,
    query_norm_gain,
    key_norm_gain,
    adapter_down_maps,
    adapter_up_maps,
    generated_mask,
    block_begin_flags,
):
    by_frame, within = (jnp.asarray(t) for t in rope_tables())
    gain_q = query_norm_gain.reshape(HEADS, HEAD_DIM)
    gain_k = key_norm_gain.reshape(HEADS, HEAD_DIM)
    norms = [gain_q, gain_k, by_frame, within]
    tokens = input_tokens[0]
    downs = adapter_down_maps.reshape(96, WIDTH)

    raws = [query_unnormed[0], key_unnormed[0], value_projected[0], cotangent[0]]
    first = [*raws, generated_mask[0], *norms]
    (firsts,) = pack(first, (0, 1), [shape((GROUPS, 8, FRAME_TOK, HEAD_DIM))], 4)
    *lasts, local = pack(
        first + [adapter_up_maps, downs, tokens],
        (2,),
        [shape((5, FRAME_TOK, HEAD_DIM))] * GROUPS + [shape((80, FRAME_TOK), F32)],
        1,
    )
    firsts = lax.all_to_all(firsts, "seq", 0, 0, tiled=True)
    wide0, state = attend(0, [block_begin_flags, firsts, *norms, adapter_up_maps])
    state, lasts[2], lasts[6] = lax.optimization_barrier((state, lasts[2], lasts[6]))
    lasts = lasts[:1] + [seq_swap(lasts[k], k) for k in range(1, GROUPS)]
    wide1, summed = attend(1, [block_begin_flags, firsts, *norms[:3], state])
    wide2, kept, means, *mix = attend(
        2, [block_begin_flags, *lasts, *norms[:3], state, summed]
    )
    mix = [swap(mix[a - 1], dy=a) for a in range(1, 4)]
    kept, means, mix = call(
        mix_kernel,
        [kept, means, *mix],
        [shape((96, FRAME_TOK), F32), shape((16, FRAME_TOK), F32), shape((128, FRAME_TOK))],
    )
    mix = seq_swap(mix, 1)

    keep, send, means = call(
        owner_kernel,
        [kept, means, mix, local, tokens],
        [shape((4, 4, 24, COLS), F32), shape((4, 4, 24, COLS)), shape((16, FRAME_TOK), F32)],
        [pltpu.VMEM((96, FRAME_TOK), F32), pltpu.VMEM((96, FRAME_TOK), F32)],
    )
    up_keep, up_send = call(
        up_kernel,
        [means, firsts, *lasts, wide0, wide1, wide2, *norms],
        [shape((2, 24, GCOLS), F32), shape((2, 24, GCOLS))],
        [
            pltpu.VMEM((2, 1024, GCOLS), BF),
            pltpu.VMEM((96, GCOLS), F32),
            pltpu.VMEM((GROUPS, 3, 3, RANK, FRAME_TOK), BF),
        ],
        mib=24,
    )
    got = swap(send, dc=1)
    up_got = swap(up_send, dc=1)
    slab = (4, 24, COLS)
    own, *parts = call(
        core_sum_kernel, [keep, got], [shape(slab, F32)] + [shape(slab)] * 3
    )
    up_own, up_part = call(
        up_core_kernel, [up_keep, up_got], [shape((24, GCOLS), F32), shape((24, GCOLS))]
    )
    parts = [swap(parts[n], dx=n + 1) for n in range(3)]
    up_part = swap(up_part, dx=1)
    own, *parts = call(
        x_sum_kernel, [own, *parts], [shape(slab[1:], F32)] + [shape(slab[1:])] * 3
    )
    parts = [swap(parts[n], dy=n + 1) for n in range(3)]
    part = call(y_sum_kernel, [own, *parts, up_own, up_part], shape((24, BOTH)))
    four = [swap(part, dz=k) for k in range(1, 4)]
    part = call(z_four_kernel, [part, *four], shape((24, BOTH)))
    part = call(z_sum_kernel, [part, swap(part, dz=7)], shape((24, BOTH)))
    over_y = call(
        stack_kernel, [part] + [swap(part, dy=k) for k in range(1, 4)], shape((4, 24, BOTH))
    )
    over_x = call(
        stack_kernel,
        [over_y] + [swap(over_y, dx=k) for k in range(1, 4)],
        shape((4, 4, 24, BOTH)),
    )
    other = swap(over_x, dc=1)
    grad_down, grad_up = call(
        final_kernel,
        [over_x, other],
        [shape((96, WIDTH)), shape((96, CHANNELS))],
    )
    return grad_down.reshape(3, RANK, WIDTH), grad_up.reshape(3, RANK, CHANNELS)


def solution(mesh):
    rows = P("dp", "seq", None)
    placed = (rows,) * 5 + (P(),) * 4 + (rows, P("dp", None))
    return jax.shard_map(shards, mesh=mesh, in_specs=placed, out_specs=(P(), P()), check_vma=False)
```

```python
import functools
import math

import jax
import jax.numpy as jnp
import numpy as np
from jax import lax
from jax.experimental import pallas as pl
from jax.experimental.pallas import tpu as pltpu
from jax.sharding import PartitionSpec as P

HEADS = 24
HEAD_DIM = 128
GRID_W = 16
FRAME_TOK = 128
FRAMES = 8
RANK = 32
WIDTH = 5120
CHANNELS = 3072
GROUPS = 8
LOCAL_HEADS = 3
NORM_EPS = 1e-06
SCALING = 1.0 / math.sqrt(HEAD_DIM)
BF = jnp.bfloat16
F32 = jnp.float32
HIDDEN = -1e30
BIG = 58
HELD = FRAMES * 112
COLS = WIDTH // 8
GCOLS = CHANNELS // 8
BOTH = COLS + GCOLS

VMEM = pl.BlockSpec(memory_space=pltpu.VMEM)
SMEM = pl.BlockSpec(memory_space=pltpu.SMEM)


def params(mib):
    return pltpu.CompilerParams(vmem_limit_bytes=mib * 1024 * 1024)


def rope_tables():
    time_dims = HEAD_DIM - 4 * (HEAD_DIM // 6)
    space_dims = 2 * (HEAD_DIM // 6)
    tp, sp = time_dims // 2, space_dims // 2
    tok = np.arange(FRAMES * FRAME_TOK)
    frame, within = tok // FRAME_TOK, tok % FRAME_TOK
    row, col = within // GRID_W, within % GRID_W
    pairs = np.arange(HEAD_DIM) // 2
    in_time = pairs < tp
    in_rows = (pairs >= tp) & (pairs < tp + sp)
    offset = np.where(in_time, pairs, np.where(in_rows, pairs - tp, pairs - tp - sp))
    extent = np.where(in_time, time_dims, space_dims)
    rates = np.exp(-math.log(10000.0) * (2 * offset) / extent)
    pos = np.where(
        in_time[None], frame[:, None], np.where(in_rows[None], row[:, None], col[:, None])
    )
    angle = pos * rates[None]
    even = (np.arange(HEAD_DIM) % 2 == 0)[None]
    sine = np.sin(angle)
    table = np.stack([np.cos(angle), np.where(even, -sine, 0.0), np.where(even, 0.0, sine)], 0)
    table = table.reshape(3, FRAMES, FRAME_TOK, HEAD_DIM)
    by_frame = np.where(in_time[None, None], table[:, :, 0], 0.0).transpose(1, 0, 2)
    within = np.where(in_time[None, None], 0.0, table[:, 0])
    return by_frame.reshape(3 * FRAMES, HEAD_DIM).astype(np.float32), within.astype(np.float32)


def angles(by_frame, within, frame):
    return [within[n] + by_frame[pl.ds(3 * frame + n, 1), :] for n in range(3)]


def turn(z, angle, sign):
    cosine, left, right = angle
    mixed = pltpu.roll(z, HEAD_DIM - 1, 1) * left + pltpu.roll(z, 1, 1) * right
    base = z * cosine
    return base + mixed if sign > 0 else base - mixed


def position():
    s, d = lax.axis_index("seq"), lax.axis_index("dp")
    x = lax.rem(s, 2) * 2 + lax.rem(lax.div(d, 2), 2)
    return s, lax.div(s, 2), x, lax.rem(d, 2)


def nt(a, b, **kw):
    return lax.dot_general(
        a, b, (((1,), (1,)), ((), ())), preferred_element_type=F32, **kw
    )


def nn(a, b):
    return lax.dot_general(a, b, (((1,), (0,)), ((), ())), preferred_element_type=F32)


def rho_of(raw):
    total = jnp.zeros((raw.shape[0], HEAD_DIM), F32)
    for n in range(HEADS):
        part = raw[:, n * HEAD_DIM : (n + 1) * HEAD_DIM].astype(F32)
        total = total + part * part
    mean = jnp.sum(total, axis=1, keepdims=True) * (1.0 / CHANNELS)
    return lax.rsqrt(mean + NORM_EPS)


def pack_kernel(heads, query, key, value, cot, mask, gain_q, gain_k, by_frame, within, *refs):
    s = lax.axis_index("seq")
    if len(refs) > 2:
        ups, downs, tokens, *outs, local, keep_s = refs
    else:
        ups, (outs, keep_s) = None, refs
    count = query.shape[0]
    keep_s[...] = jnp.broadcast_to(mask[...].astype(F32), (FRAME_TOK, FRAME_TOK)).T
    keep = keep_s[pl.ds(pl.multiple_of(pl.program_id(0) * count, count), count), :] > 0.0
    rhos = [jnp.broadcast_to(rho_of(raw), (count, HEAD_DIM)) for raw in (query, key)]
    angle = angles(by_frame, within, s)
    for k in range(GROUPS):
        for i, h in enumerate(heads):
            head = (k if ups is None else jnp.bitwise_xor(s, k)) * LOCAL_HEADS + h
            at = pl.ds(pl.multiple_of(head * HEAD_DIM, HEAD_DIM), HEAD_DIM)
            out = outs.at[k] if ups is None else outs[k]
            for n, (raw, gain) in enumerate(((query, gain_q), (key, gain_k))):
                normed = raw[:, at].astype(F32) * rhos[n] * gain[pl.ds(head, 1), :]
                out[4 * i + n] = turn(normed, angle, 1).astype(BF)
            out[4 * i + 2] = value[:, at]
            out[4 * i + 3] = jnp.where(keep, cot[:, at].astype(F32), 0.0).astype(BF)
    if ups is None:
        return
    rows = []
    for n, raw in ((0, query), (1, key)):
        rows.append(rhos[n].T[0:8])
        carried = jnp.zeros((RANK, FRAME_TOK), F32)
        for head in range(HEADS):
            at = slice(head * HEAD_DIM, (head + 1) * HEAD_DIM)
            normed = (raw[:, at].astype(F32) * rhos[n]).astype(BF)
            carried = carried + nt(ups[n, :, at], normed)
        local[n * RANK : (n + 1) * RANK, :] = carried
        local[64 + 8 * n : 72 + 8 * n, :] = rows[n]
    down = nt(downs[...], tokens[...])
    at_row = lax.broadcasted_iota(jnp.int32, (RANK, FRAME_TOK), 0)
    extra = jnp.zeros((RANK, FRAME_TOK), F32)
    for n in range(2):
        wide = jnp.concatenate([rows[n]] * 4, 0)
        high = wide.astype(BF).astype(F32)
        extra = jnp.where(at_row == 2 * n, high, extra)
        extra = jnp.where(at_row == 2 * n + 1, wide - high, extra)
    aux = jnp.concatenate([down, extra], 0).astype(BF)
    for k in range(GROUPS):
        outs[k][4] = aux


def attend_kernel(base, flags, *refs):
    last = base == LOCAL_HEADS - 1
    s = lax.axis_index("seq")
    if last:
        packs, refs = refs[:GROUPS], refs[GROUPS:]
        frames = [jnp.bitwise_xor(s, k) for k in range(GROUPS)]
    else:
        packs, refs = [refs[0].at[k] for k in range(GROUPS)], refs[1:]
        frames = list(range(GROUPS))
    gain_q, gain_k, by_frame, *refs = refs
    if base == 0:
        within, ups_all, *refs = refs
    else:
        state, *refs = refs
        before = state
        if last:
            before, *refs = refs
        within = [state[HELD + n * FRAME_TOK : HELD + (n + 1) * FRAME_TOK, :] for n in range(3)]
        first = HELD + 3 * FRAME_TOK + (base - 1) * 96
        ups = [state[first + n * RANK : first + (n + 1) * RANK, :].astype(BF) for n in range(3)]
    wide_out, summed = refs[:2]
    refs = refs[2:]
    if last:
        mean_out, *mix = refs[:4]
        refs = refs[4:]
    q_s, k_s, kt_s, v_s, g_s, sc, dp, pb, db, dk_acc, dv_acc, dq_s, prod_s, sums = refs
    head = s * LOCAL_HEADS + base
    owner = []
    for k in range(GROUPS):
        owner.append(sum(jnp.where(f <= frames[k], flags[0, f], 0) for f in range(FRAMES)))
        at = slice(k * FRAME_TOK, (k + 1) * FRAME_TOK)
        q_s[at, :] = packs[k][0]
        key = packs[k][1]
        k_s[at, :] = key
        kt_s[:, at] = key.astype(F32).T.astype(BF)
        v_s[at, :] = packs[k][2]
        g_s[at, :] = packs[k][3]
    factor = SCALING * math.log2(math.e)
    lane = lax.broadcasted_iota(jnp.int32, (1, 256), 1)
    for t in range(4):
        b = t % 2
        tile = slice(t * 256, (t + 1) * 256)
        q_t, g_t = q_s[tile, :], g_s[tile, :]
        limit = jnp.where(lane < FRAME_TOK, owner[2 * t], owner[2 * t + 1])
        bias = [jnp.where(owner[j] <= limit, 0.0, HIDDEN) for j in range(GROUPS)]
        sc[b] = nt(k_s[...], q_t)
        dp[b] = nt(v_s[...], g_t)
        top = jnp.full((8, 256), 2.0 * HIDDEN, F32)
        for j in range(GROUPS):
            part = sc[b, j * FRAME_TOK : (j + 1) * FRAME_TOK, :]
            top = jnp.maximum(top, jnp.max(part.reshape(16, 8, 256), axis=0) + bias[j])
        top = jnp.max(top, axis=0, keepdims=True)
        total = jnp.zeros((8, 256), F32)
        cross = jnp.zeros((8, 256), F32)
        for j in range(GROUPS):
            at = slice(j * FRAME_TOK, (j + 1) * FRAME_TOK)
            weight = jnp.exp2((sc[b, at, :] - (top - bias[j])) * factor)
            sc[b, at, :] = weight
            total = total + jnp.sum(weight.reshape(16, 8, 256), axis=0)
            cross = cross + jnp.sum((weight * dp[b, at, :]).reshape(16, 8, 256), axis=0)
        inverse = 1.0 / jnp.sum(total, axis=0, keepdims=True)
        delta = jnp.sum(cross, axis=0, keepdims=True) * inverse
        for j in range(GROUPS):
            at = slice(j * FRAME_TOK, (j + 1) * FRAME_TOK)
            prob = sc[b, at, :] * inverse
            pb[b, at, :] = prob.astype(BF)
            db[b, at, :] = (prob * (dp[b, at, :] - delta)).astype(BF)
        dv, dk = nn(pb[b], g_t), nn(db[b], q_t)
        if t == 0:
            dv_acc[...] = dv
            dk_acc[...] = dk
        else:
            dv_acc[...] += dv
            dk_acc[...] += dk
        dq_s[tile, :] = nn(kt_s[...], db[b]).T
    if base == 0:
        up_at = pl.ds(pl.multiple_of(head * HEAD_DIM, HEAD_DIM), HEAD_DIM)
        ups = [ups_all[n, :, up_at] for n in range(3)]
    gains = [gain[pl.ds(head, 1), :] for gain in (gain_q, gain_k)]
    for k in range(GROUPS):
        at = slice(k * FRAME_TOK, (k + 1) * FRAME_TOK)
        angle = angles(by_frame, within, frames[k])
        for n, (acc, rot) in enumerate(((dq_s, q_s), (dk_acc, k_s))):
            grad = (acc[at, :] * SCALING).astype(BF).astype(F32)
            wide = gains[n] * turn(grad, angle, -1)
            wide_out[0, n, at, :] = wide.astype(BF)
            prod_s[n, at, :] = (grad * rot[at, :].astype(F32)).astype(BF)
        wide_out[0, 2, at, :] = dv_acc[at, :].astype(BF)
    ones = jnp.ones((16, HEAD_DIM), BF)
    parts = [nt(ups[n], wide_out[0, n]) for n in range(3)]
    parts += [nt(ones, prod_s[n])[0:8] for n in range(2)]
    full = jnp.concatenate(parts, 0)
    for k in range(GROUPS):
        part = full[:, k * FRAME_TOK : (k + 1) * FRAME_TOK]
        at = slice(k * 112, (k + 1) * 112)
        if last:
            at = pl.ds(pl.multiple_of(frames[k] * 112, 8), 112)
            sums[k] = part + before[at, :]
        elif base == 0:
            summed[at, :] = part
        else:
            summed[at, :] = part + before[at, :]
    if base == 0:
        for n in range(3):
            summed[HELD + n * FRAME_TOK : HELD + (n + 1) * FRAME_TOK, :] = within[n]
            for h in range(1, LOCAL_HEADS):
                at = pl.ds(pl.multiple_of((head + h) * HEAD_DIM, HEAD_DIM), HEAD_DIM)
                first = HELD + 3 * FRAME_TOK + (h - 1) * 96 + n * RANK
                summed[first : first + RANK, :] = ups_all[n, :, at].astype(F32)
    if not last:
        return
    at_row = lax.broadcasted_iota(jnp.int32, (8, FRAME_TOK), 0)
    for n in range(2):
        gathered = jnp.zeros((8, FRAME_TOK), F32)
        for k in range(GROUPS):
            row = sums[k, 96 + 8 * n : 104 + 8 * n]
            gathered = jnp.where(at_row == k, row, gathered)
        mean_out[8 * n : 8 * n + 8, :] = gathered
    tail = halves(mean_out[...])
    for b in range(2):
        summed[b] = sums[b, 0:96]
        for a in range(1, 4):
            mix[a - 1][b * 96 : (b + 1) * 96, :] = sums[2 * a + b, 0:96].astype(BF)
    for a in range(1, 4):
        mix[a - 1][192:224, :] = tail


def halves(means):
    high = means.astype(BF).astype(F32)
    return jnp.concatenate([high, means - high], 0).astype(BF)


def add_means(got, first, bit):
    tail = got[first : first + 32, :].astype(F32)
    tail = tail[0:16] + tail[16:32]
    moved = [tail[8 * n + (p ^ bit) : 8 * n + (p ^ bit) + 1] for n in range(2) for p in range(8)]
    return jnp.concatenate(moved, 0)


def mix_kernel(keep, means, r1, r2, r3, keep_out, means_out, send):
    total = (means[...] + add_means(r1, 192, 2)) + (add_means(r2, 192, 4) + add_means(r3, 192, 6))
    means_out[...] = total
    for i in range(2):
        at = slice(i * 96, (i + 1) * 96)
        value = keep[i] + r1[at, :].astype(F32)
        value = value + (r2[at, :].astype(F32) + r3[at, :].astype(F32))
        if i == 0:
            keep_out[...] = value
        else:
            send[0:96, :] = value.astype(BF)
    send[96:128, :] = halves(total)


def owner_kernel(kept, means, got, local, tokens, keep, send, means_out, rows_s, mixed_s):
    _, y, x, c = position()
    total = kept[...] + got[0:96, :].astype(F32)
    full = means[...] + add_means(got, 96, 1)
    means_out[...] = full
    for n in range(2):
        at = slice(n * RANK, (n + 1) * RANK)
        rho = local[64 + 8 * n : 65 + 8 * n, :]
        mean = full[8 * n : 8 * n + 1] * (1.0 / CHANNELS)
        rows_s[at, :] = rho * (total[at] - mean * local[at, :])
    rows_s[64:96, :] = total[64:96]
    for k in range(4):
        first = pl.multiple_of(jnp.bitwise_xor(y, k) * 24, 8)
        mixed_s[k * 24 : (k + 1) * 24, :] = rows_s[pl.ds(first, 24), :]
    mixed = mixed_s[...].astype(BF)
    for a in range(2):
        for b in range(4):
            block = jnp.bitwise_xor(c, a) * 4 + jnp.bitwise_xor(x, b)
            at = pl.ds(pl.multiple_of(block * COLS, HEAD_DIM), COLS)
            out = nn(mixed, tokens[:, at])
            for k in range(4):
                part = out[k * 24 : (k + 1) * 24]
                if a == 0:
                    keep[b, k] = part
                else:
                    send[b, k] = part.astype(BF)


def up_kernel(means, firsts, *refs):
    lasts, wides = refs[:GROUPS], [ref.at[0] for ref in refs[GROUPS : GROUPS + 3]]
    gain_q, gain_k, by_frame, within, keep, send, turned_s, up_s, scaled_s = refs[GROUPS + 3 :]
    s, _, x, c = position()
    xl = jnp.bitwise_and(x, 1)
    order = [jnp.bitwise_xor(s, k) for k in range(GROUPS)]
    for k in range(GROUPS):
        at = slice(k * FRAME_TOK, (k + 1) * FRAME_TOK)
        for h in range(LOCAL_HEADS):
            lanes = slice(h * HEAD_DIM, (h + 1) * HEAD_DIM)
            if h != 1:
                angle = angles(by_frame, within, order[k] if h == 2 else k)
            for n in range(2):
                rot = lasts[k][n] if h == 2 else firsts[k, 4 * h + n]
                turned_s[n, at, lanes] = turn(rot.astype(F32), angle, -1).astype(BF)
    for p in range(GROUPS):
        aux = lasts[p][4].astype(F32)
        for n in range(3):
            down = aux[n * RANK : (n + 1) * RANK]
            if n == 2:
                scaled_s[p, n, 0] = down.astype(BF)
                continue
            rho = aux[96 + 2 * n : 97 + 2 * n] + aux[97 + 2 * n : 98 + 2 * n]
            scaled = down * rho
            high = scaled.astype(BF)
            mean = means[8 * n + p : 8 * n + p + 1, :] * (1.0 / CHANNELS)
            scaled_s[p, n, 0] = high
            scaled_s[p, n, 1] = (scaled - high.astype(F32)).astype(BF)
            scaled_s[p, n, 2] = (scaled * mean).astype(BF)

    def rows(n, kind, h):
        places = range(GROUPS) if h == 2 else order
        return jnp.concatenate([scaled_s[p, n, kind] for p in places], 1)

    for n in range(3):
        for h in range(LOCAL_HEADS):
            lanes = slice(h * HEAD_DIM, (h + 1) * HEAD_DIM)
            out = nn(rows(n, 0, h), wides[h][n])
            if n < 2:
                gain = (gain_q, gain_k)[n][pl.ds(s * LOCAL_HEADS + h, 1), :]
                out = out + nn(rows(n, 1, h), wides[h][n])
                out = out - nn(rows(n, 2, h), turned_s[n, :, lanes]) / gain
            up_s[n * RANK : (n + 1) * RANK, lanes] = out
    for a in range(2):
        for b in range(2):
            block = jnp.bitwise_xor(c, a) * 2 + jnp.bitwise_xor(xl, b)
            part = up_s[pl.ds(pl.multiple_of(block * 24, 8), 24), :]
            if a == 0:
                keep[b] = part
            else:
                send[b] = part.astype(BF)


def core_sum_kernel(keep, got, own, *sends):
    for b in range(4):
        value = keep[b] + got[b].astype(F32)
        if b == 0:
            own[...] = value
        else:
            sends[b - 1][...] = value.astype(BF)


def up_core_kernel(keep, got, own, send):
    own[...] = keep[0] + got[0].astype(F32)
    send[...] = (keep[1] + got[1].astype(F32)).astype(BF)


def x_sum_kernel(own, r1, r2, r3, keep, *sends):
    for b in range(4):
        value = (own[b] + r1[b].astype(F32)) + (r2[b].astype(F32) + r3[b].astype(F32))
        if b == 0:
            keep[...] = value
        else:
            sends[b - 1][...] = value.astype(BF)


def y_sum_kernel(up_own, up_got, own, r1, r2, r3, out):
    value = (own[...] + r1[...].astype(F32)) + (r2[...].astype(F32) + r3[...].astype(F32))
    out[:, :COLS] = value.astype(BF)
    out[:, COLS:] = (up_own[...] + up_got[...].astype(F32)).astype(BF)


def z_four_kernel(own, r1, r2, r3, out):
    value = (own[...].astype(F32) + r1[...].astype(F32)) + (r2[...].astype(F32) + r3[...].astype(F32))
    out[...] = value.astype(BF)


def z_sum_kernel(own, got, out):
    out[...] = (own[...].astype(F32) + got[...].astype(F32)).astype(BF)


def stack_kernel(*refs):
    out = refs[-1]
    for n, ref in enumerate(refs[:-1]):
        out[n] = ref[...]


def final_kernel(own, got, down_out, up_out):
    _, y, x, c = position()

    def piece(ca, xa, ya, lanes):
        xr, yr = jnp.bitwise_xor(x, xa), jnp.bitwise_xor(y, ya)
        mine = own[xr, yr, :, lanes].astype(F32)
        other = got[xr, yr, :, lanes].astype(F32)
        return jnp.where(c == ca, mine, other)

    for ca in range(2):
        for xa in range(4):
            block = [piece(ca, xa, ya, slice(0, COLS)) for ya in range(4)]
            first = (ca * 4 + xa) * COLS
            down_out[:, first : first + COLS] = jnp.concatenate(block, 0).astype(BF)
    for ya in range(4):
        for xh in range(2):
            block = [
                piece(ca, xh * 2 + xl, ya, slice(COLS, BOTH)) for ca in range(2) for xl in range(2)
            ]
            first = (ya * 2 + xh) * GCOLS
            up_out[:, first : first + GCOLS] = jnp.concatenate(block, 0).astype(BF)


def shape(dims, dtype=BF):
    return jax.ShapeDtypeStruct(dims, dtype)


def call(kernel, ins, outs, scratch=(), smem=0, mib=16):
    single = not isinstance(outs, (list, tuple))
    return pl.pallas_call(
        kernel,
        out_shape=outs,
        in_specs=[SMEM] * smem + [VMEM] * (len(ins) - smem),
        out_specs=VMEM if single else [VMEM] * len(outs),
        scratch_shapes=list(scratch),
        compiler_params=params(mib),
    )(*ins)


def place(x, y, z, c):
    return (y * 2 + x // 2) * 32 + z * 4 + (x % 2) * 2 + c


def swap(array, dx=0, dy=0, dz=0, dc=0):
    pairs = [
        (place(x, y, z, c), place(x ^ dx, y ^ dy, z ^ dz, c ^ dc))
        for x in range(4)
        for y in range(4)
        for z in range(8)
        for c in range(2)
    ]
    return lax.ppermute(array, ("seq", "dp"), pairs)


def seq_swap(array, k):
    return swap(array, dx=2 * (k & 1), dy=k >> 1)


def whole(array):
    zeros = (0,) * len(array.shape)
    return pl.BlockSpec(array.shape, lambda i: zeros)


def pack(ins, heads, outs, steps):
    count = FRAME_TOK // steps
    specs = [pl.BlockSpec((count, CHANNELS), lambda i: (i, 0))] * 4 + [whole(a) for a in ins[4:]]
    specs[8] = pl.BlockSpec((3, count, HEAD_DIM), lambda i: (0, i, 0))
    out_specs = [whole(a) for a in outs]
    if len(outs) == 1:
        out_specs = [pl.BlockSpec((GROUPS, 8, count, HEAD_DIM), lambda i: (0, 0, i, 0))]
    return pl.pallas_call(
        functools.partial(pack_kernel, heads),
        grid=(steps,),
        out_shape=outs,
        in_specs=specs,
        out_specs=out_specs,
        scratch_shapes=[pltpu.VMEM((FRAME_TOK, FRAME_TOK), F32)],
        compiler_params=params(BIG),
    )(*ins)


def attend(base, ins):
    seq_len = FRAMES * FRAME_TOK
    rows = (seq_len, HEAD_DIM)
    outs = [shape((1, 3, *rows))]
    out_specs = [whole(outs[0])]
    if base == LOCAL_HEADS - 1:
        specs = [SMEM] + [pl.BlockSpec((4, FRAME_TOK, HEAD_DIM), lambda i: (0, 0, 0))] * GROUPS
        extra = [shape((2, 96, FRAME_TOK), F32), shape((16, FRAME_TOK), F32)]
        extra += [shape((224, FRAME_TOK))] * 3
        out_specs += [VMEM] * 5
    else:
        specs = [SMEM, pl.BlockSpec((GROUPS, 4, FRAME_TOK, HEAD_DIM), lambda i: (0, base, 0, 0))]
        extra = [shape((HELD + (1 - base) * (3 * FRAME_TOK + 192), FRAME_TOK), F32)]
        out_specs += [whole(a) for a in extra]
    specs += [whole(a) for a in ins[len(specs) :]]
    return pl.pallas_call(
        functools.partial(attend_kernel, base),
        grid=(1,),
        out_shape=outs + extra,
        in_specs=specs,
        out_specs=out_specs,
        scratch_shapes=[
            pltpu.VMEM(rows, BF),
            pltpu.VMEM(rows, BF),
            pltpu.VMEM((HEAD_DIM, seq_len), BF),
            pltpu.VMEM(rows, BF),
            pltpu.VMEM(rows, BF),
            pltpu.VMEM((2, seq_len, 256), F32),
            pltpu.VMEM((2, seq_len, 256), F32),
            pltpu.VMEM((2, seq_len, 256), BF),
            pltpu.VMEM((2, seq_len, 256), BF),
            pltpu.VMEM(rows, F32),
            pltpu.VMEM(rows, F32),
            pltpu.VMEM(rows, F32),
            pltpu.VMEM((2, *rows), BF),
            pltpu.VMEM((GROUPS, 112, FRAME_TOK), F32),
        ],
        compiler_params=params(32),
        cost_estimate=pl.CostEstimate(
            flops=10 * seq_len * seq_len * HEAD_DIM,
            bytes_accessed=4 << 20,
            transcendentals=seq_len * seq_len,
        ),
    )(*ins)


def shards(
    input_tokens,
    query_unnormed,
    key_unnormed,
    value_projected,
    cotangent,
    query_norm_gain,
    key_norm_gain,
    adapter_down_maps,
    adapter_up_maps,
    generated_mask,
    block_begin_flags,
):
    by_frame, within = (jnp.asarray(t) for t in rope_tables())
    gain_q = query_norm_gain.reshape(HEADS, HEAD_DIM)
    gain_k = key_norm_gain.reshape(HEADS, HEAD_DIM)
    norms = [gain_q, gain_k, by_frame, within]
    tokens = input_tokens[0]
    downs = adapter_down_maps.reshape(96, WIDTH)

    raws = [query_unnormed[0], key_unnormed[0], value_projected[0], cotangent[0]]
    first = [*raws, generated_mask[0], *norms]
    (firsts,) = pack(first, (0, 1), [shape((GROUPS, 8, FRAME_TOK, HEAD_DIM))], 2)
    *lasts, local = pack(
        first + [adapter_up_maps, downs, tokens],
        (2,),
        [shape((5, FRAME_TOK, HEAD_DIM))] * GROUPS + [shape((80, FRAME_TOK), F32)],
        1,
    )
    firsts = lax.all_to_all(firsts, "seq", 0, 0, tiled=True)
    wide0, state = attend(0, [block_begin_flags, firsts, *norms, adapter_up_maps])
    state, lasts[2], lasts[6] = lax.optimization_barrier((state, lasts[2], lasts[6]))
    lasts = lasts[:1] + [seq_swap(lasts[k], k) for k in range(1, GROUPS)]
    wide1, summed = attend(1, [block_begin_flags, firsts, *norms[:3], state])
    wide2, kept, means, *mix = attend(
        2, [block_begin_flags, *lasts, *norms[:3], state, summed]
    )
    mix = [swap(mix[a - 1], dy=a) for a in range(1, 4)]
    kept, means, mix = call(
        mix_kernel,
        [kept, means, *mix],
        [shape((96, FRAME_TOK), F32), shape((16, FRAME_TOK), F32), shape((128, FRAME_TOK))],
    )
    mix = seq_swap(mix, 1)

    keep, send, means = call(
        owner_kernel,
        [kept, means, mix, local, tokens],
        [shape((4, 4, 24, COLS), F32), shape((4, 4, 24, COLS)), shape((16, FRAME_TOK), F32)],
        [pltpu.VMEM((96, FRAME_TOK), F32), pltpu.VMEM((96, FRAME_TOK), F32)],
    )
    up_keep, up_send = call(
        up_kernel,
        [means, firsts, *lasts, wide0, wide1, wide2, *norms],
        [shape((2, 24, GCOLS), F32), shape((2, 24, GCOLS))],
        [
            pltpu.VMEM((2, 1024, GCOLS), BF),
            pltpu.VMEM((96, GCOLS), F32),
            pltpu.VMEM((GROUPS, 3, 3, RANK, FRAME_TOK), BF),
        ],
        mib=24,
    )
    got = swap(send, dc=1)
    up_got = swap(up_send, dc=1)
    slab = (4, 24, COLS)
    own, *parts = call(
        core_sum_kernel, [keep, got], [shape(slab, F32)] + [shape(slab)] * 3
    )
    up_own, up_part = call(
        up_core_kernel, [up_keep, up_got], [shape((24, GCOLS), F32), shape((24, GCOLS))]
    )
    parts = [swap(parts[n], dx=n + 1) for n in range(3)]
    own, *parts = call(
        x_sum_kernel, [own, *parts], [shape(slab[1:], F32)] + [shape(slab[1:])] * 3
    )
    up_part, *parts = lax.optimization_barrier((up_part, *parts))
    up_part = swap(up_part, dx=1)
    parts = [swap(parts[n], dy=n + 1) for n in range(3)]
    part = call(y_sum_kernel, [up_own, up_part, own, *parts], shape((24, BOTH)))
    four = [swap(part, dz=k) for k in range(1, 4)]
    part = call(z_four_kernel, [part, *four], shape((24, BOTH)))
    part = call(z_sum_kernel, [part, swap(part, dz=7)], shape((24, BOTH)))
    over_y = call(
        stack_kernel, [part] + [swap(part, dy=k) for k in range(1, 4)], shape((4, 24, BOTH))
    )
    over_x = call(
        stack_kernel,
        [over_y] + [swap(over_y, dx=k) for k in range(1, 4)],
        shape((4, 4, 24, BOTH)),
    )
    other = swap(over_x, dc=1)
    grad_down, grad_up = call(
        final_kernel,
        [over_x, other],
        [shape((96, WIDTH)), shape((96, CHANNELS))],
    )
    return grad_down.reshape(3, RANK, WIDTH), grad_up.reshape(3, RANK, CHANNELS)


def solution(mesh):
    rows = P("dp", "seq", None)
    placed = (rows,) * 5 + (P(),) * 4 + (rows, P("dp", None))
    return jax.shard_map(shards, mesh=mesh, in_specs=placed, out_specs=(P(), P()), check_vma=False)
```
